32 devices in a mesh: pipe: 4 (over y, core), seq: 4 (over z), tp: 2 (over x).
Axes of the slice: x: 2, y: 2, z: 4, core: 2. Of those that a mesh axis runs over, the one named last changes fastest.
Arguments:
- upstream: bfloat16 [4, 2, 384, 2048], P('pipe', 'tp', 'seq'), may hold values from -6 to 6
- queries: bfloat16 [4, 2, 384, 2048], P('pipe', 'tp', 'seq'), may hold values from -6 to 6
- attention_out: bfloat16 [4, 2, 384, 2048], P('pipe', 'tp', 'seq'), may hold values from -6 to 6
- keys_values: bfloat16 [4, 2, 32, 384, 128], P('pipe', 'tp', 'seq'), may hold values from -6 to 6
- log_totals: float32 [4, 2, 32, 384], P('pipe', 'tp', 'seq'), may hold values from 3.5 to 5.5
- neighbours: int32 [12, 7], replicated, may hold values from -1 to 11, as said below
Outputs:
- query_grad: bfloat16 [4, 2, 32, 384, 64], P('pipe', 'tp', 'seq')
- cache_grad: bfloat16 [4, 2, 32, 384, 128], P('pipe', 'tp', 'seq')
The draws below stay inside these ranges and needn't reach their ends.
Inputs may be any that keep to these rules, and one draw needn't show every extreme that they name: `neighbours`: in each row the used entries come first and are distinct; the first is the row's own block; every used entry lies within 4 blocks of the row's block; unused entries are -1. Some aligned run of 6 rows has every row listing as many blocks as lie within reach, up to 7; elsewhere rows list 1 to 3 blocks.
All inputs are finite; a program needn't handle non-finite values.
Results may differ from the reference program's by a relative error of at most 0.0055.
Values may be sent and summed in bfloat16 or wider, within the bound.
A program may use at most 128 MiB of HBM per device.

```python
import jax
import jax.numpy as jnp
from jax import lax

H = 32
HD = 64
BLK = 64
REACH = 4
NBR = 7
D = 2048
QUART = 384
QBD = 6
NB = 12
N_PIPE = 4
N_TP = 2


def draw_neighbours(key, part):
    width = 2 * REACH + 1
    key_score, key_count, key_dense = jax.random.split(key, 3)
    offsets = jnp.arange(width, dtype=jnp.int32) - REACH
    rows = jnp.arange(NB, dtype=jnp.int32)
    target = rows[:, None] + offsets[None, :]
    inside = (target >= 0) & (target < NB)
    score = jax.random.randint(key_score, (NB, width), 0, 1 << 20) * width + jnp.arange(width, dtype=jnp.int32)[None, :]
    score = jnp.where(offsets[None, :] == 0, (1 << 20) * width + width, score)
    score = jnp.where(inside, score, -1)
    top_score, order = lax.top_k(score, NBR)
    picked = jnp.take_along_axis(target, order, axis=1)
    reach_count = jnp.sum(inside.astype(jnp.int32), axis=1)
    sparse_count = jax.random.randint(key_count, (NB,), 1, 4)
    dense_quarter = jax.random.randint(key_dense, (), 0, NB // QBD)
    wanted = jnp.where(rows // QBD == dense_quarter, NBR, sparse_count)
    count = jnp.minimum(wanted, reach_count)
    slot = jnp.arange(NBR, dtype=jnp.int32)
    return jnp.where(slot[None, :] < count[:, None], picked, -1).astype(jnp.int32)


def level_of(stream_key, dims, cuts, smallest, top_value):
    gain, own = 1.0, jax.random.fold_in(stream_key, 6)
    for dim, shards_of in cuts:
        heights = jnp.exp(jax.random.uniform(jax.random.fold_in(own, dim), (shards_of,), jnp.float32, smallest / len(cuts), top_value / len(cuts)))
        gain = gain * jnp.repeat(heights, dims[dim] // shards_of).reshape([-1 if axis == dim else 1 for axis in range(len(dims))])
    return gain


def noise(key, dims, spread, limit, shards=(), held_as=jnp.bfloat16):
    factor_of = level_of(key, dims, shards, -0.22, 0.18) if shards else 1.0
    array = jax.random.normal(key, dims, jnp.float32) * spread * factor_of
    return jnp.minimum(jnp.maximum(array, -limit), limit).astype(held_as)


def setup_inputs(seed: int = 0) -> dict:
    arg_keys = jax.random.split(jax.random.key(seed), 7)
    return {
        "upstream": noise(arg_keys[0], (N_PIPE, N_TP, QUART, D), 1.0, 6.0, ((0, 4), (1, 2), (2, 4))),
        "queries": noise(arg_keys[1], (N_PIPE, N_TP, QUART, D), 1.0, 6.0, ((0, 4), (1, 2), (2, 4))),
        "attention_out": noise(arg_keys[2], (N_PIPE, N_TP, QUART, D), 1.0, 6.0, ((0, 4), (1, 2), (2, 4))),
        "keys_values": noise(arg_keys[3], (N_PIPE, N_TP, H, QUART, 2 * HD), 1.0, 6.0, ((0, 4), (1, 2), (2, 4))),
        "log_totals": jnp.clip(3.5 + 2.0 * jax.random.uniform(arg_keys[4], (N_PIPE, N_TP, H, QUART), jnp.float32) ** level_of(arg_keys[4], (N_PIPE, N_TP, H, QUART), ((0, 4), (1, 2), (2, 4)), -0.2, 0.2), 3.5, 5.5),
        "neighbours": draw_neighbours(jax.random.fold_in(arg_keys[6], 71), 0),
    }


def head_grads(query_rows, grad_rows, key_rows, value_rows, norm_rows, delta_rows, neighbours):
    block_total = neighbours.shape[0]
    inv_root = HD ** -0.5
    listed = neighbours >= 0
    key_index = jnp.where(listed, neighbours, 0).astype(jnp.int32)
    query_blocks = query_rows.reshape(block_total, BLK, HD).astype(jnp.float32)
    grad_blocks = grad_rows.reshape(block_total, BLK, HD).astype(jnp.float32)
    key_blocks = key_rows.reshape(block_total, BLK, HD).astype(jnp.float32)
    value_blocks = value_rows.reshape(block_total, BLK, HD).astype(jnp.float32)
    norm_blocks = norm_rows.reshape(block_total, BLK)
    delta_blocks = delta_rows.reshape(block_total, BLK)
    key_taken = key_blocks[key_index]
    value_taken = value_blocks[key_index]
    live_mask = listed.astype(jnp.float32)[:, :, None, None]
    scores = jnp.einsum("aqd,ajkd->ajqk", query_blocks, key_taken) * inv_root
    weights = jnp.exp(scores - norm_blocks[:, None, :, None]) * live_mask
    weights_half = lax.optimization_barrier(weights.astype(jnp.bfloat16)).astype(jnp.float32)
    grad_weights = jnp.einsum("aqd,ajkd->ajqk", grad_blocks, value_taken)
    grad_scores = lax.optimization_barrier((weights * (grad_weights - delta_blocks[:, None, :, None])).astype(jnp.bfloat16)).astype(jnp.float32)
    grad_query = jnp.einsum("ajqk,ajkd->aqd", grad_scores, key_taken) * inv_root
    key_terms = jnp.einsum("ajqk,aqd->ajkd", grad_scores, query_blocks) * inv_root
    value_terms = jnp.einsum("ajqk,aqd->ajkd", weights_half, grad_blocks)
    all_terms = jnp.concatenate([key_terms, value_terms], axis=-1).reshape(-1, BLK, 2 * HD)
    grad_cache = jnp.zeros((block_total, BLK, 2 * HD), jnp.float32).at[key_index.reshape(-1)].add(all_terms)
    return grad_query.reshape(block_total * BLK, HD).astype(jnp.bfloat16), grad_cache.reshape(block_total * BLK, 2 * HD).astype(jnp.bfloat16)


def reference(upstream, queries, attention_out, keys_values, log_totals, neighbours):
    incoming = jnp.roll(upstream, -1, axis=0)
    seq_total = N_TP * QUART

    def section_grads(section_number):
        query_all = queries[section_number].reshape(seq_total, H, HD)
        grad_all = incoming[section_number].reshape(seq_total, H, HD)
        out_all = attention_out[section_number].reshape(seq_total, H, HD)
        row_delta = jnp.sum(grad_all.astype(jnp.float32) * out_all.astype(jnp.float32), axis=2)
        cache_all = jnp.transpose(keys_values[section_number], (1, 0, 2, 3)).reshape(H, seq_total, 2 * HD)
        norm_all = jnp.transpose(log_totals[section_number], (1, 0, 2)).reshape(H, seq_total)

        def one_head(head_number):
            cache_rows = cache_all[head_number]
            return head_grads(query_all[:, head_number, :], grad_all[:, head_number, :], cache_rows[:, :HD], cache_rows[:, HD:], norm_all[head_number], row_delta[:, head_number], neighbours)

        grad_query, grad_cache = lax.map(one_head, jnp.arange(H, dtype=jnp.int32))
        grad_query = jnp.transpose(grad_query.reshape(H, N_TP, QUART, HD), (1, 0, 2, 3))
        grad_cache = jnp.transpose(grad_cache.reshape(H, N_TP, QUART, 2 * HD), (1, 0, 2, 3))
        return grad_query, grad_cache

    query_grad, cache_grad = lax.map(section_grads, jnp.arange(N_PIPE, dtype=jnp.int32))
    return (query_grad, cache_grad)
```

```python
import jax
import jax.numpy as jnp
from jax import lax
from jax.experimental import pallas as pl
from jax.experimental.pallas import tpu as pltpu
from jax.sharding import PartitionSpec as P

H = 32
HD = 64
BLK = 64
REACH = 4
NBR = 7


pair_group = 32


def passed_along(value, axis, steps):
    count = lax.axis_size(axis)
    pairs = [(source, (source + steps) % count) for source in range(count)]
    return lax.ppermute(value, axis, pairs)


def padded_2(cells, sides, width):
    for axis, dim in sides:
        count = lax.axis_size(axis)
        ends = count - 1
        head = lax.slice_in_dim(cells, 0, width, axis=dim)
        tail = lax.slice_in_dim(cells, cells.shape[dim] - width, cells.shape[dim], axis=dim)
        cells = jnp.concatenate(
            [
                lax.ppermute(tail, axis, [(i, (i + 1) % count) for i in range(ends)]),
                cells,
                lax.ppermute(head, axis, [((i + 1) % count, i) for i in range(ends)]),
            ],
            axis=dim,
        )
    return cells


def block_layout(values, blocks_here):
    heads_here = values.shape[1]
    turned = jnp.transpose(values, (1, 0, 2))
    return turned.reshape(heads_here, blocks_here, BLK, values.shape[2])


def general_body(upstream, queries, attention_out, keys_values, log_totals, neighbours):
    tokens_here = queries.shape[2]
    inv_root = HD ** (-0.5)
    incoming = passed_along(upstream, "pipe", -1)
    query_tok = queries.reshape(tokens_here, H, HD)
    grad_tok = incoming.reshape(tokens_here, H, HD)
    out_tok = attention_out.reshape(tokens_here, H, HD)
    packed = jnp.concatenate([query_tok, grad_tok, out_tok], axis=2)
    regrouped = lax.all_to_all(packed, "seq", split_axis=1, concat_axis=0, tiled=True)
    query_heads = regrouped[:, :, :HD]
    grad_heads = regrouped[:, :, HD : 2 * HD]
    out_heads = regrouped[:, :, 2 * HD :]
    row_delta = jnp.sum(grad_heads.astype(jnp.float32) * out_heads.astype(jnp.float32), axis=2)
    rows_here = query_heads.shape[0]
    heads_here = query_heads.shape[1]
    blocks_here = rows_here // BLK
    query_blocks = block_layout(query_heads, blocks_here)
    grad_blocks = block_layout(grad_heads, blocks_here)
    delta_blocks = jnp.transpose(row_delta).reshape(heads_here, blocks_here, BLK)
    norm_blocks = log_totals.reshape(heads_here, blocks_here, BLK)
    cache_blocks = keys_values.reshape(heads_here, blocks_here, BLK, 2 * HD)
    padded = padded_2(cache_blocks, (("tp", 1),), REACH)
    first_block = lax.axis_index("tp") * blocks_here
    listed = lax.dynamic_slice_in_dim(neighbours, first_block, blocks_here, 0)
    present = (listed >= 0).reshape(-1)
    slot_count = blocks_here * NBR
    group_total = (slot_count + pair_group - 1) // pair_group
    capacity = group_total * pair_group
    running = jnp.cumsum(present.astype(jnp.int32)) - 1
    pair_count = jnp.sum(present.astype(jnp.int32))
    target = jnp.where(present, running, capacity)
    query_source = jnp.repeat(jnp.arange(blocks_here, dtype=jnp.int32), NBR)
    key_source = (listed - first_block + REACH).reshape(-1)
    pair_query = jnp.zeros((capacity,), jnp.int32).at[target].set(query_source, mode="drop")
    pair_key = jnp.zeros((capacity,), jnp.int32).at[target].set(key_source, mode="drop")

    def one_group(group_step, totals):
        query_acc, cache_acc = totals
        first_pair = group_step * pair_group
        query_pick = lax.dynamic_slice_in_dim(pair_query, first_pair, pair_group)
        key_pick = lax.dynamic_slice_in_dim(pair_key, first_pair, pair_group)
        live_mask = (first_pair + jnp.arange(pair_group) < pair_count).astype(jnp.float32)
        query_rows = query_blocks[:, query_pick]
        grad_rows = grad_blocks[:, query_pick]
        norm_rows = norm_blocks[:, query_pick]
        delta_rows = delta_blocks[:, query_pick]
        cache_rows = padded[:, key_pick]
        key_rows = cache_rows[..., :HD]
        value_rows = cache_rows[..., HD:]
        scores = (
            jnp.einsum("hgqd,hgkd->hgqk", query_rows, key_rows, preferred_element_type=jnp.float32)
            * inv_root
        )
        weights = jnp.exp(scores - norm_rows[..., None]) * live_mask[None, :, None, None]
        weights_half = weights.astype(jnp.bfloat16)
        grad_weights = jnp.einsum(
            "hgqd,hgkd->hgqk", grad_rows, value_rows, preferred_element_type=jnp.float32
        )
        grad_scores = (weights * (grad_weights - delta_rows[..., None])).astype(jnp.bfloat16)
        query_part = (
            jnp.einsum("hgqk,hgkd->hgqd", grad_scores, key_rows, preferred_element_type=jnp.float32)
            * inv_root
        )
        key_part = (
            jnp.einsum(
                "hgqk,hgqd->hgkd", grad_scores, query_rows, preferred_element_type=jnp.float32
            )
            * inv_root
        )
        value_part = jnp.einsum(
            "hgqk,hgqd->hgkd", weights_half, grad_rows, preferred_element_type=jnp.float32
        )
        query_acc = query_acc.at[:, query_pick].add(query_part)
        cache_acc = cache_acc.at[:, key_pick].add(jnp.concatenate([key_part, value_part], axis=-1))
        return (query_acc, cache_acc)

    group_live = (pair_count + pair_group - 1) // pair_group
    query_start = jnp.zeros((heads_here, blocks_here, BLK, HD), jnp.float32)
    cache_start = jnp.zeros((heads_here, blocks_here + 2 * REACH, BLK, 2 * HD), jnp.float32)
    query_acc, cache_acc = lax.fori_loop(0, group_live, one_group, (query_start, cache_start))
    rim_terms = jnp.concatenate([cache_acc[:, :REACH], cache_acc[:, REACH + blocks_here :]], axis=1)
    arrived = padded_2(rim_terms.astype(jnp.bfloat16), (("tp", 1),), REACH).astype(rim_terms.dtype)
    own_part = cache_acc[:, REACH : REACH + blocks_here]
    own_part = own_part.at[:, :REACH].add(arrived[:, :REACH])
    own_part = own_part.at[:, blocks_here - REACH :].add(arrived[:, 3 * REACH :])
    query_grad = query_acc.reshape(1, 1, heads_here, rows_here, HD).astype(jnp.bfloat16)
    cache_grad = own_part.reshape(1, 1, heads_here, rows_here, 2 * HD).astype(jnp.bfloat16)
    return (query_grad, cache_grad)


MESH = pl.DeviceIdType.MESH
LANES = 128
PER_TILE = LANES // HD
LOG2E = 1.4426950408889634
ABSENT = -1e30
NT = (((1,), (1,)), ((), ()))
TN = (((0,), (0,)), ((), ()))


def dot_f32(left, right, dims=(((1,), (0,)), ((), ()))):
    return lax.dot_general(left, right, dims, preferred_element_type=jnp.float32)


def listed_bias(neigh_ref, first_row, first_key, key_rows, blocks_here):
    lane = lax.broadcasted_iota(jnp.int32, (key_rows, LANES), 1)
    key = lax.broadcasted_iota(jnp.int32, (key_rows, LANES), 0) + first_key
    tiles = []
    for pair in range(blocks_here // 2):
        found = None
        for slot in range(NBR):
            here = jnp.where(
                lane < BLK,
                neigh_ref[slot, first_row + 2 * pair],
                neigh_ref[slot, first_row + 2 * pair + 1],
            )
            hit = (key == here).astype(jnp.float32)
            found = hit if found is None else jnp.maximum(found, hit)
        tiles.append((found - 1.0) * -ABSENT)
    return jnp.concatenate(tiles, axis=1)


def fused_kernel(
    neigh_ref, norm_ref, up_ref, query_ref, out_ref, cache_ref, dq_ref, dkv_ref,
    inc, outs, kv, halo, qbuf, gbuf, dsend, dgot, acc, acc_kv, back_out, back_in, bias_own, bias_halo, rows_aux,
    up_send, up_recv, q_send, q_recv, g_send, g_recv, d_send, d_recv, h_send, h_recv, b_send, b_recv, local_sem,
):
    n_pipe, n_seq = lax.axis_size("pipe"), lax.axis_size("seq")
    pipe, seq, tp = lax.axis_index("pipe"), lax.axis_index("seq"), lax.axis_index("tp")
    tokens, width = inc.shape
    heads, rows, _ = kv.shape
    tiles = heads // PER_TILE
    span = REACH * BLK
    blocks_here = rows // BLK
    share = heads * HD
    below, above = lax.rem(pipe + n_pipe - 1, n_pipe), lax.rem(pipe + 1, n_pipe)
    mate = 1 - tp
    window = pl.multiple_of(mate * (rows - span), LANES)
    mine = pl.multiple_of(seq * tokens, 16)

    def peer(step):
        return lax.rem(seq + step, n_seq)

    def tile_cols(dest, tile):
        return pl.ds(pl.multiple_of(dest * share + tile * LANES, LANES), LANES)

    def up_copy(tile, dest):
        cols = pl.ds(dest * share + tile * LANES, LANES)
        return pltpu.make_async_remote_copy(
            src_ref=up_ref.at[:, cols], dst_ref=inc.at[:, cols],
            send_sem=up_send.at[tile, dest], recv_sem=up_recv.at[tile, dest],
            device_id={"pipe": below}, device_id_type=MESH,
        )

    def q_copy(tile, step):
        return pltpu.make_async_remote_copy(
            src_ref=query_ref.at[:, tile_cols(peer(step), tile)],
            dst_ref=qbuf.at[tile, pl.ds(mine, tokens), :],
            send_sem=q_send.at[tile, step - 1], recv_sem=q_recv.at[tile, step - 1],
            device_id={"seq": peer(step)}, device_id_type=MESH,
        )

    def g_copy(tile, step):
        return pltpu.make_async_remote_copy(
            src_ref=inc.at[:, tile_cols(peer(step), tile)],
            dst_ref=gbuf.at[tile, pl.ds(mine, tokens), :],
            send_sem=g_send.at[tile, step - 1], recv_sem=g_recv.at[tile, step - 1],
            device_id={"seq": peer(step)}, device_id_type=MESH,
        )

    def d_copy(step):
        return pltpu.make_async_remote_copy(
            src_ref=dsend.at[peer(step)], dst_ref=dgot.at[seq],
            send_sem=d_send.at[step - 1], recv_sem=d_recv.at[step - 1],
            device_id={"seq": peer(step)}, device_id_type=MESH,
        )

    def h_copy(tile):
        pair = pl.ds(tile * PER_TILE, PER_TILE)
        return pltpu.make_async_remote_copy(
            src_ref=cache_ref.at[pair, pl.ds(window, span), :], dst_ref=halo.at[pair],
            send_sem=h_send.at[tile], recv_sem=h_recv.at[tile],
            device_id={"tp": mate}, device_id_type=MESH,
        )

    def b_copy(tile):
        pair = pl.ds(tile * PER_TILE, PER_TILE)
        return pltpu.make_async_remote_copy(
            src_ref=back_out.at[pair], dst_ref=back_in.at[pair],
            send_sem=b_send.at[tile], recv_sem=b_recv.at[tile],
            device_id={"tp": mate}, device_id_type=MESH,
        )

    out_local = pltpu.make_async_copy(out_ref, outs, local_sem.at[0])
    kv_local = pltpu.make_async_copy(cache_ref, kv, local_sem.at[1])
    q_local = [
        pltpu.make_async_copy(
            query_ref.at[:, tile_cols(seq, tile)], qbuf.at[tile, pl.ds(mine, tokens), :], local_sem.at[2 + tile]
        )
        for tile in range(tiles)
    ]
    out_local.start()
    kv_local.start()
    for copy in q_local:
        copy.start()

    barrier = pltpu.get_barrier_semaphore()
    pl.semaphore_signal(barrier, inc=1, device_id={"pipe": above}, device_id_type=MESH)
    pl.semaphore_signal(barrier, inc=1, device_id={"tp": mate}, device_id_type=MESH)
    for step in range(1, n_seq):
        pl.semaphore_signal(barrier, inc=1, device_id={"seq": peer(step)}, device_id_type=MESH)
    pl.semaphore_wait(barrier, n_seq + 1)

    for tile in range(tiles):
        for dest in range(n_seq):
            up_copy(tile, dest).start()
        h_copy(tile).start()
        if tile < 2:
            for step in range(1, n_seq):
                q_copy(tile, step).start()

    first_row = tp * blocks_here
    halo_key = mate * blocks_here + tp * (blocks_here - REACH)
    bias_own[...] = listed_bias(neigh_ref, first_row, first_row, bias_own.shape[0], blocks_here)
    bias_halo[...] = listed_bias(neigh_ref, first_row, halo_key, bias_halo.shape[0], blocks_here)

    for tile in range(tiles):
        for dest in range(n_seq):
            up_copy(tile, dest).wait_recv()
        for step in range(1, n_seq):
            g_copy(tile, step).start()
        if tile + 2 < tiles:
            for step in range(1, n_seq):
                q_copy(tile + 2, step).start()

    out_local.wait()
    picks = (
        lax.broadcasted_iota(jnp.int32, (heads, share), 1) // HD
        == lax.broadcasted_iota(jnp.int32, (heads, share), 0)
    ).astype(jnp.bfloat16)
    dsend[...] = jnp.zeros_like(dsend)
    for dest in range(n_seq):
        cols = pl.ds(dest * share, share)
        terms = inc[:, cols].astype(jnp.float32) * outs[:, cols].astype(jnp.float32)
        high = terms.astype(jnp.bfloat16)
        low = (terms - high.astype(jnp.float32)).astype(jnp.bfloat16)
        dsend[dest, :, :tokens] = dot_f32(picks, high, NT) + dot_f32(picks, low, NT)
    for step in range(1, n_seq):
        d_copy(step).start()
    dgot[seq] = dsend[seq]
    for tile in range(tiles):
        gbuf[tile, pl.ds(mine, tokens), :] = inc[:, tile_cols(seq, tile)]
    kv_local.wait()
    for copy in q_local:
        copy.wait()
    for step in range(1, n_seq):
        d_copy(step).wait_recv()
    delta = None
    for source in range(n_seq):
        part = jnp.concatenate([dgot[source], jnp.zeros((heads, rows - LANES), jnp.float32)], axis=1)
        if source:
            part = pltpu.roll(part, source * tokens, 1)
        delta = part if delta is None else delta + part
    norm = norm_ref[...] * LOG2E
    for head in range(heads):
        rows_aux[head, 0:1, :] = norm[head : head + 1]
        rows_aux[head, 1:2, :] = delta[head : head + 1]

    inv_root = HD ** (-0.5)

    def block_terms(keys, values, q_rows, g_rows, bias, norm_row, delta_row):
        count = keys.shape[0] // BLK
        scores = dot_f32(keys, q_rows, NT) * (inv_root * LOG2E)
        shift = bias[:count] - norm_row
        scores = scores.reshape(count, BLK, scores.shape[1]) + shift[:, None, :]
        weights = jnp.exp2(scores).reshape(keys.shape[0], scores.shape[2])
        grad_weights = dot_f32(values, g_rows, NT)
        grad_scores = (weights * (grad_weights - delta_row)).astype(jnp.bfloat16)
        key_part = dot_f32(grad_scores, q_rows) * inv_root
        value_part = dot_f32(weights.astype(jnp.bfloat16), g_rows)
        query_part = dot_f32(keys, grad_scores, TN) * inv_root
        return query_part, jnp.concatenate([key_part, value_part], axis=1)

    def one_tile(tile, carry):
        for step in range(1, n_seq):
            q_copy(tile, step).wait_recv()
            g_copy(tile, step).wait_recv()
        h_copy(tile).wait_recv()
        for inner in range(PER_TILE):
            head = tile * PER_TILE + inner
            lanes = slice(inner * HD, (inner + 1) * HD)
            query_part, cache_part = block_terms(
                halo[head, :, :HD],
                halo[head, :, HD:],
                qbuf[tile, pl.ds(window, span), lanes],
                gbuf[tile, pl.ds(window, span), lanes],
                bias_halo[:, pl.ds(window, span)],
                rows_aux[head, 0:1, pl.ds(window, span)],
                rows_aux[head, 1:2, pl.ds(window, span)],
            )
            back_out[head] = cache_part.astype(jnp.bfloat16)
            acc[head, :, pl.ds(window, span)] = query_part
            acc[head, :, pl.ds(pl.multiple_of(tp * span, LANES), rows - span)] = jnp.zeros(
                (HD, rows - span), jnp.float32
            )
        b_copy(tile).start()
        for inner in range(PER_TILE):
            head = tile * PER_TILE + inner
            lanes = slice(inner * HD, (inner + 1) * HD)
            query_part, cache_part = block_terms(
                kv[head, :, :HD],
                kv[head, :, HD:],
                qbuf[tile, :, lanes],
                gbuf[tile, :, lanes],
                bias_own[...],
                rows_aux[head, 0:1, :],
                rows_aux[head, 1:2, :],
            )
            dq_ref[head] = (acc[head] + query_part).astype(jnp.bfloat16)
            acc_kv[head] = cache_part
        return carry

    lax.fori_loop(0, tiles, one_tile, 0)

    def finish(tile, carry):
        b_copy(tile).wait_recv()
        for inner in range(PER_TILE):
            head = tile * PER_TILE + inner
            acc_kv[head, pl.ds(window, span), :] += back_in[head].astype(jnp.float32)
            dkv_ref[head] = acc_kv[head].astype(jnp.bfloat16)
        return carry

    lax.fori_loop(0, tiles, finish, 0)

    for tile in range(tiles):
        for dest in range(n_seq):
            up_copy(tile, dest).wait_send()
        for step in range(1, n_seq):
            q_copy(tile, step).wait_send()
            g_copy(tile, step).wait_send()
        h_copy(tile).wait_send()
        b_copy(tile).wait_send()
    for step in range(1, n_seq):
        d_copy(step).wait_send()


def fused_body(upstream, queries, attention_out, keys_values, log_totals, neighbours):
    tokens, width = queries.shape[2:]
    heads, rows = keys_values.shape[2:4]
    tiles = heads // PER_TILE
    n_seq = lax.axis_size("seq")
    span = REACH * BLK
    blocks_pad = 8 * -(-(rows // BLK) // 8)
    bf16, f32 = jnp.bfloat16, jnp.float32
    vmem = pl.BlockSpec(memory_space=pltpu.VMEM)
    anywhere = pl.BlockSpec(memory_space=pl.ANY)
    dma = pltpu.SemaphoreType.DMA
    query_turned, cache_grad = pl.pallas_call(
        fused_kernel,
        out_shape=(
            jax.ShapeDtypeStruct((heads, HD, rows), bf16),
            jax.ShapeDtypeStruct((heads, rows, 2 * HD), bf16),
        ),
        in_specs=[pl.BlockSpec(memory_space=pltpu.SMEM), vmem] + [anywhere] * 4,
        out_specs=(vmem, vmem),
        scratch_shapes=[
            pltpu.VMEM((tokens, width), bf16),
            pltpu.VMEM((tokens, width), bf16),
            pltpu.VMEM((heads, rows, 2 * HD), bf16),
            pltpu.VMEM((heads, span, 2 * HD), bf16),
            pltpu.VMEM((tiles, rows, LANES), bf16),
            pltpu.VMEM((tiles, rows, LANES), bf16),
            pltpu.VMEM((n_seq, heads, LANES), f32),
            pltpu.VMEM((n_seq, heads, LANES), f32),
            pltpu.VMEM((heads, HD, rows), f32),
            pltpu.VMEM((heads, rows, 2 * HD), f32),
            pltpu.VMEM((heads, span, 2 * HD), bf16),
            pltpu.VMEM((heads, span, 2 * HD), bf16),
            pltpu.VMEM((blocks_pad, rows), f32),
            pltpu.VMEM((8, rows), f32),
            pltpu.VMEM((heads, 8, rows), f32),
            dma((tiles, n_seq)),
            dma((tiles, n_seq)),
            dma((tiles, n_seq - 1)),
            dma((tiles, n_seq - 1)),
            dma((tiles, n_seq - 1)),
            dma((tiles, n_seq - 1)),
            dma((n_seq - 1,)),
            dma((n_seq - 1,)),
            dma((tiles,)),
            dma((tiles,)),
            dma((tiles,)),
            dma((tiles,)),
            dma((2 + tiles,)),
        ],
        compiler_params=pltpu.CompilerParams(
            collective_id=0, has_side_effects=True, vmem_limit_bytes=48 * 1024 * 1024
        ),
    )(
        jnp.transpose(neighbours),
        log_totals.reshape(heads, rows),
        upstream.reshape(tokens, width),
        queries.reshape(tokens, width),
        attention_out.reshape(tokens, width),
        keys_values.reshape(heads, rows, 2 * HD),
    )
    query_grad = jnp.transpose(query_turned, (0, 2, 1)).reshape(1, 1, heads, rows, HD)
    return query_grad, cache_grad.reshape(1, 1, heads, rows, 2 * HD)


def body(upstream, queries, attention_out, keys_values, log_totals, neighbours):
    tokens = queries.shape[2]
    heads, rows = keys_values.shape[2:4]
    fits = (
        lax.axis_size("tp") == 2
        and lax.axis_size("pipe") > 1
        and lax.axis_size("seq") > 1
        and heads == 8
        and tokens % 16 == 0
        and tokens <= LANES
        and rows % LANES == 0
        and REACH * BLK < rows <= 512
    )
    chosen = fused_body if fits else general_body
    return chosen(upstream, queries, attention_out, keys_values, log_totals, neighbours)


def solution(mesh):
    placed = (
        P("pipe", "tp", "seq", None),
        P("pipe", "tp", "seq", None),
        P("pipe", "tp", "seq", None),
        P("pipe", "tp", "seq", None, None),
        P("pipe", "tp", "seq", None),
        P(),
    )
    return jax.shard_map(
        body,
        mesh=mesh,
        in_specs=placed,
        out_specs=(P("pipe", "tp", "seq", None, None), P("pipe", "tp", "seq", None, None)),
        check_vma=False,
    )
```

```python
import jax
import jax.numpy as jnp
from jax import lax
from jax.experimental import pallas as pl
from jax.experimental.pallas import tpu as pltpu
from jax.sharding import PartitionSpec as P

H = 32
HD = 64
BLK = 64
REACH = 4
NBR = 7


pair_group = 32


def passed_along(value, axis, steps):
    count = lax.axis_size(axis)
    pairs = [(source, (source + steps) % count) for source in range(count)]
    return lax.ppermute(value, axis, pairs)


def padded_2(cells, sides, width):
    for axis, dim in sides:
        count = lax.axis_size(axis)
        ends = count - 1
        head = lax.slice_in_dim(cells, 0, width, axis=dim)
        tail = lax.slice_in_dim(cells, cells.shape[dim] - width, cells.shape[dim], axis=dim)
        cells = jnp.concatenate(
            [
                lax.ppermute(tail, axis, [(i, (i + 1) % count) for i in range(ends)]),
                cells,
                lax.ppermute(head, axis, [((i + 1) % count, i) for i in range(ends)]),
            ],
            axis=dim,
        )
    return cells


def block_layout(values, blocks_here):
    heads_here = values.shape[1]
    turned = jnp.transpose(values, (1, 0, 2))
    return turned.reshape(heads_here, blocks_here, BLK, values.shape[2])


def general_body(upstream, queries, attention_out, keys_values, log_totals, neighbours):
    tokens_here = queries.shape[2]
    inv_root = HD ** (-0.5)
    incoming = passed_along(upstream, "pipe", -1)
    query_tok = queries.reshape(tokens_here, H, HD)
    grad_tok = incoming.reshape(tokens_here, H, HD)
    out_tok = attention_out.reshape(tokens_here, H, HD)
    packed = jnp.concatenate([query_tok, grad_tok, out_tok], axis=2)
    regrouped = lax.all_to_all(packed, "seq", split_axis=1, concat_axis=0, tiled=True)
    query_heads = regrouped[:, :, :HD]
    grad_heads = regrouped[:, :, HD : 2 * HD]
    out_heads = regrouped[:, :, 2 * HD :]
    row_delta = jnp.sum(grad_heads.astype(jnp.float32) * out_heads.astype(jnp.float32), axis=2)
    rows_here = query_heads.shape[0]
    heads_here = query_heads.shape[1]
    blocks_here = rows_here // BLK
    query_blocks = block_layout(query_heads, blocks_here)
    grad_blocks = block_layout(grad_heads, blocks_here)
    delta_blocks = jnp.transpose(row_delta).reshape(heads_here, blocks_here, BLK)
    norm_blocks = log_totals.reshape(heads_here, blocks_here, BLK)
    cache_blocks = keys_values.reshape(heads_here, blocks_here, BLK, 2 * HD)
    padded = padded_2(cache_blocks, (("tp", 1),), REACH)
    first_block = lax.axis_index("tp") * blocks_here
    listed = lax.dynamic_slice_in_dim(neighbours, first_block, blocks_here, 0)
    present = (listed >= 0).reshape(-1)
    slot_count = blocks_here * NBR
    group_total = (slot_count + pair_group - 1) // pair_group
    capacity = group_total * pair_group
    running = jnp.cumsum(present.astype(jnp.int32)) - 1
    pair_count = jnp.sum(present.astype(jnp.int32))
    target = jnp.where(present, running, capacity)
    query_source = jnp.repeat(jnp.arange(blocks_here, dtype=jnp.int32), NBR)
    key_source = (listed - first_block + REACH).reshape(-1)
    pair_query = jnp.zeros((capacity,), jnp.int32).at[target].set(query_source, mode="drop")
    pair_key = jnp.zeros((capacity,), jnp.int32).at[target].set(key_source, mode="drop")

    def one_group(group_step, totals):
        query_acc, cache_acc = totals
        first_pair = group_step * pair_group
        query_pick = lax.dynamic_slice_in_dim(pair_query, first_pair, pair_group)
        key_pick = lax.dynamic_slice_in_dim(pair_key, first_pair, pair_group)
        live_mask = (first_pair + jnp.arange(pair_group) < pair_count).astype(jnp.float32)
        query_rows = query_blocks[:, query_pick]
        grad_rows = grad_blocks[:, query_pick]
        norm_rows = norm_blocks[:, query_pick]
        delta_rows = delta_blocks[:, query_pick]
        cache_rows = padded[:, key_pick]
        key_rows = cache_rows[..., :HD]
        value_rows = cache_rows[..., HD:]
        scores = (
            jnp.einsum("hgqd,hgkd->hgqk", query_rows, key_rows, preferred_element_type=jnp.float32)
            * inv_root
        )
        weights = jnp.exp(scores - norm_rows[..., None]) * live_mask[None, :, None, None]
        weights_half = weights.astype(jnp.bfloat16)
        grad_weights = jnp.einsum(
            "hgqd,hgkd->hgqk", grad_rows, value_rows, preferred_element_type=jnp.float32
        )
        grad_scores = (weights * (grad_weights - delta_rows[..., None])).astype(jnp.bfloat16)
        query_part = (
            jnp.einsum("hgqk,hgkd->hgqd", grad_scores, key_rows, preferred_element_type=jnp.float32)
            * inv_root
        )
        key_part = (
            jnp.einsum(
                "hgqk,hgqd->hgkd", grad_scores, query_rows, preferred_element_type=jnp.float32
            )
            * inv_root
        )
        value_part = jnp.einsum(
            "hgqk,hgqd->hgkd", weights_half, grad_rows, preferred_element_type=jnp.float32
        )
        query_acc = query_acc.at[:, query_pick].add(query_part)
        cache_acc = cache_acc.at[:, key_pick].add(jnp.concatenate([key_part, value_part], axis=-1))
        return (query_acc, cache_acc)

    group_live = (pair_count + pair_group - 1) // pair_group
    query_start = jnp.zeros((heads_here, blocks_here, BLK, HD), jnp.float32)
    cache_start = jnp.zeros((heads_here, blocks_here + 2 * REACH, BLK, 2 * HD), jnp.float32)
    query_acc, cache_acc = lax.fori_loop(0, group_live, one_group, (query_start, cache_start))
    rim_terms = jnp.concatenate([cache_acc[:, :REACH], cache_acc[:, REACH + blocks_here :]], axis=1)
    arrived = padded_2(rim_terms.astype(jnp.bfloat16), (("tp", 1),), REACH).astype(rim_terms.dtype)
    own_part = cache_acc[:, REACH : REACH + blocks_here]
    own_part = own_part.at[:, :REACH].add(arrived[:, :REACH])
    own_part = own_part.at[:, blocks_here - REACH :].add(arrived[:, 3 * REACH :])
    query_grad = query_acc.reshape(1, 1, heads_here, rows_here, HD).astype(jnp.bfloat16)
    cache_grad = own_part.reshape(1, 1, heads_here, rows_here, 2 * HD).astype(jnp.bfloat16)
    return (query_grad, cache_grad)


MESH = pl.DeviceIdType.MESH
LANES = 128
PER_TILE = LANES // HD
ABSENT = -1e30
NT = (((1,), (1,)), ((), ()))
TN = (((0,), (0,)), ((), ()))


def dot_f32(left, right, dims=(((1,), (0,)), ((), ()))):
    return lax.dot_general(left, right, dims, preferred_element_type=jnp.float32)


def listed_bias(neigh_ref, first_row, first_key, key_rows, blocks_here):
    lane = lax.broadcasted_iota(jnp.int32, (key_rows, LANES), 1)
    key = lax.broadcasted_iota(jnp.int32, (key_rows, LANES), 0) + first_key
    tiles = []
    for pair in range(blocks_here // 2):
        found = None
        for slot in range(NBR):
            here = jnp.where(
                lane < BLK,
                neigh_ref[slot, first_row + 2 * pair],
                neigh_ref[slot, first_row + 2 * pair + 1],
            )
            hit = (key == here).astype(jnp.float32)
            found = hit if found is None else jnp.maximum(found, hit)
        tiles.append((found - 1.0) * -ABSENT)
    return jnp.concatenate(tiles, axis=1)


def fused_kernel(
    neigh_hbm, norm_hbm, up_ref, query_ref, out_ref, cache_ref, dq_ref, dkv_ref,
    neigh_ref, norm_ref, inc, outs, kv, halo, qbuf, gbuf, dsend, dgot, acc, acc_kv, back_out, back_in, bias_own, bias_halo, rows_aux,
    up_send, up_recv, q_send, q_recv, g_send, g_recv, d_send, d_recv, h_send, h_recv, b_send, b_recv, local_sem,
):
    n_pipe, n_seq = lax.axis_size("pipe"), lax.axis_size("seq")
    pipe, seq, tp = lax.axis_index("pipe"), lax.axis_index("seq"), lax.axis_index("tp")
    tokens, width = inc.shape
    heads, rows, _ = kv.shape
    tiles = heads // PER_TILE
    span = REACH * BLK
    blocks_here = rows // BLK
    share = heads * HD
    below, above = lax.rem(pipe + n_pipe - 1, n_pipe), lax.rem(pipe + 1, n_pipe)
    mate = 1 - tp
    window = pl.multiple_of(mate * (rows - span), LANES)
    mine = pl.multiple_of(seq * tokens, 16)

    def peer(step):
        return lax.rem(seq + step, n_seq)

    def tile_cols(dest, tile):
        return pl.ds(pl.multiple_of(dest * share + tile * LANES, LANES), LANES)

    def up_copy(tile, dest):
        cols = pl.ds(dest * share + tile * LANES, LANES)
        return pltpu.make_async_remote_copy(
            src_ref=up_ref.at[:, cols], dst_ref=inc.at[:, cols],
            send_sem=up_send.at[tile, dest], recv_sem=up_recv.at[tile, dest],
            device_id={"pipe": below}, device_id_type=MESH,
        )

    def q_copy(tile, step):
        return pltpu.make_async_remote_copy(
            src_ref=query_ref.at[:, tile_cols(peer(step), tile)],
            dst_ref=qbuf.at[tile, pl.ds(mine, tokens), :],
            send_sem=q_send.at[tile, step - 1], recv_sem=q_recv.at[tile, step - 1],
            device_id={"seq": peer(step)}, device_id_type=MESH,
        )

    def g_copy(tile, step):
        return pltpu.make_async_remote_copy(
            src_ref=inc.at[:, tile_cols(peer(step), tile)],
            dst_ref=gbuf.at[tile, pl.ds(mine, tokens), :],
            send_sem=g_send.at[tile, step - 1], recv_sem=g_recv.at[tile, step - 1],
            device_id={"seq": peer(step)}, device_id_type=MESH,
        )

    def d_copy(step):
        return pltpu.make_async_remote_copy(
            src_ref=dsend.at[peer(step)], dst_ref=dgot.at[seq],
            send_sem=d_send.at[step - 1], recv_sem=d_recv.at[step - 1],
            device_id={"seq": peer(step)}, device_id_type=MESH,
        )

    def h_copy(tile):
        pair = pl.ds(tile * PER_TILE, PER_TILE)
        return pltpu.make_async_remote_copy(
            src_ref=cache_ref.at[pair, pl.ds(window, span), :], dst_ref=halo.at[pair],
            send_sem=h_send.at[tile], recv_sem=h_recv.at[tile],
            device_id={"tp": mate}, device_id_type=MESH,
        )

    def b_copy(tile):
        pair = pl.ds(tile * PER_TILE, PER_TILE)
        return pltpu.make_async_remote_copy(
            src_ref=back_out.at[pair], dst_ref=back_in.at[pair],
            send_sem=b_send.at[tile], recv_sem=b_recv.at[tile],
            device_id={"tp": mate}, device_id_type=MESH,
        )

    out_local = pltpu.make_async_copy(out_ref, outs, local_sem.at[0])
    kv_local = pltpu.make_async_copy(cache_ref, kv, local_sem.at[1])
    q_local = [
        pltpu.make_async_copy(
            query_ref.at[:, tile_cols(seq, tile)], qbuf.at[tile, pl.ds(mine, tokens), :], local_sem.at[2 + tile]
        )
        for tile in range(tiles)
    ]
    neigh_local = pltpu.make_async_copy(neigh_hbm, neigh_ref, local_sem.at[2 + tiles])
    norm_local = pltpu.make_async_copy(norm_hbm, norm_ref, local_sem.at[3 + tiles])
    neigh_local.start()
    norm_local.start()
    out_local.start()
    kv_local.start()
    for copy in q_local:
        copy.start()

    barrier = pltpu.get_barrier_semaphore()
    pl.semaphore_signal(barrier, inc=1, device_id={"pipe": above}, device_id_type=MESH)
    pl.semaphore_signal(barrier, inc=1, device_id={"tp": mate}, device_id_type=MESH)
    for step in range(1, n_seq):
        pl.semaphore_signal(barrier, inc=1, device_id={"seq": peer(step)}, device_id_type=MESH)
    pl.semaphore_wait(barrier, n_seq + 1)

    for tile in range(tiles):
        for dest in range(n_seq):
            up_copy(tile, dest).start()
        h_copy(tile).start()
        if tile < 2:
            for step in range(1, n_seq):
                q_copy(tile, step).start()

    neigh_local.wait()
    first_row = tp * blocks_here
    halo_key = mate * blocks_here + tp * (blocks_here - REACH)
    bias_own[...] = listed_bias(neigh_ref, first_row, first_row, bias_own.shape[0], blocks_here)
    bias_halo[...] = listed_bias(neigh_ref, first_row, halo_key, bias_halo.shape[0], blocks_here)

    for tile in range(tiles):
        for dest in range(n_seq):
            up_copy(tile, dest).wait_recv()
        for step in range(1, n_seq):
            g_copy(tile, step).start()
        if tile + 2 < tiles:
            for step in range(1, n_seq):
                q_copy(tile + 2, step).start()

    out_local.wait()
    picks = (
        lax.broadcasted_iota(jnp.int32, (heads, share), 1) // HD
        == lax.broadcasted_iota(jnp.int32, (heads, share), 0)
    ).astype(jnp.bfloat16)
    dsend[...] = jnp.zeros_like(dsend)
    for dest in range(n_seq):
        cols = pl.ds(dest * share, share)
        terms = inc[:, cols].astype(jnp.float32) * outs[:, cols].astype(jnp.float32)
        high = terms.astype(jnp.bfloat16)
        low = (terms - high.astype(jnp.float32)).astype(jnp.bfloat16)
        dsend[dest, :, :tokens] = dot_f32(picks, high, NT) + dot_f32(picks, low, NT)
    for step in range(1, n_seq):
        d_copy(step).start()
    dgot[seq] = dsend[seq]
    for tile in range(tiles):
        gbuf[tile, pl.ds(mine, tokens), :] = inc[:, tile_cols(seq, tile)]
    kv_local.wait()
    for copy in q_local:
        copy.wait()
    for step in range(1, n_seq):
        d_copy(step).wait_recv()
    delta = None
    for source in range(n_seq):
        part = jnp.concatenate([dgot[source], jnp.zeros((heads, rows - LANES), jnp.float32)], axis=1)
        if source:
            part = pltpu.roll(part, source * tokens, 1)
        delta = part if delta is None else delta + part
    norm_local.wait()
    norm = norm_ref[...]
    for head in range(heads):
        rows_aux[head, 0:1, :] = norm[head : head + 1]
        rows_aux[head, 1:2, :] = delta[head : head + 1]

    inv_root = HD ** (-0.5)

    def block_terms(keys, values, q_rows, g_rows, bias, norm_row, delta_row):
        count = keys.shape[0] // BLK
        keys = keys * jnp.bfloat16(inv_root)
        scores = dot_f32(keys, q_rows, NT)
        shift = bias[:count] - norm_row
        scores = scores.reshape(count, BLK, scores.shape[1]) + shift[:, None, :]
        weights = jnp.exp(scores).reshape(keys.shape[0], scores.shape[2])
        grad_weights = dot_f32(values, g_rows, NT)
        grad_scores = (weights * (grad_weights - delta_row)).astype(jnp.bfloat16)
        key_part = dot_f32(grad_scores, q_rows) * inv_root
        value_part = dot_f32(weights.astype(jnp.bfloat16), g_rows)
        query_part = dot_f32(keys, grad_scores, TN)
        return query_part, jnp.concatenate([key_part, value_part], axis=1)

    def one_tile(tile, carry):
        for step in range(1, n_seq):
            q_copy(tile, step).wait_recv()
            g_copy(tile, step).wait_recv()
        h_copy(tile).wait_recv()
        for inner in range(PER_TILE):
            head = tile * PER_TILE + inner
            lanes = slice(inner * HD, (inner + 1) * HD)
            query_part, cache_part = block_terms(
                halo[head, :, :HD],
                halo[head, :, HD:],
                qbuf[tile, pl.ds(window, span), lanes],
                gbuf[tile, pl.ds(window, span), lanes],
                bias_halo[:, pl.ds(window, span)],
                rows_aux[head, 0:1, pl.ds(window, span)],
                rows_aux[head, 1:2, pl.ds(window, span)],
            )
            back_out[head] = cache_part.astype(jnp.bfloat16)
            acc[head, :, pl.ds(window, span)] = query_part
            acc[head, :, pl.ds(pl.multiple_of(tp * span, LANES), rows - span)] = jnp.zeros(
                (HD, rows - span), jnp.float32
            )
        b_copy(tile).start()
        for inner in range(PER_TILE):
            head = tile * PER_TILE + inner
            lanes = slice(inner * HD, (inner + 1) * HD)
            query_part, cache_part = block_terms(
                kv[head, :, :HD],
                kv[head, :, HD:],
                qbuf[tile, :, lanes],
                gbuf[tile, :, lanes],
                bias_own[...],
                rows_aux[head, 0:1, :],
                rows_aux[head, 1:2, :],
            )
            dq_ref[head] = (acc[head] + query_part).astype(jnp.bfloat16)
            acc_kv[head] = cache_part
        return carry

    lax.fori_loop(0, tiles, one_tile, 0)

    def finish(tile, carry):
        b_copy(tile).wait_recv()
        for inner in range(PER_TILE):
            head = tile * PER_TILE + inner
            acc_kv[head, pl.ds(window, span), :] += back_in[head].astype(jnp.float32)
            dkv_ref[head] = acc_kv[head].astype(jnp.bfloat16)
        return carry

    lax.fori_loop(0, tiles, finish, 0)

    for tile in range(tiles):
        for dest in range(n_seq):
            up_copy(tile, dest).wait_send()
        for step in range(1, n_seq):
            q_copy(tile, step).wait_send()
            g_copy(tile, step).wait_send()
        h_copy(tile).wait_send()
        b_copy(tile).wait_send()
    for step in range(1, n_seq):
        d_copy(step).wait_send()


def fused_body(upstream, queries, attention_out, keys_values, log_totals, neighbours):
    tokens, width = queries.shape[2:]
    heads, rows = keys_values.shape[2:4]
    tiles = heads // PER_TILE
    n_seq = lax.axis_size("seq")
    span = REACH * BLK
    blocks_pad = 8 * -(-(rows // BLK) // 8)
    bf16, f32 = jnp.bfloat16, jnp.float32
    vmem = pl.BlockSpec(memory_space=pltpu.VMEM)
    pinned = pl.BlockSpec(memory_space=pltpu.HBM)
    dma = pltpu.SemaphoreType.DMA
    query_turned, cache_grad = pl.pallas_call(
        fused_kernel,
        out_shape=(
            jax.ShapeDtypeStruct((heads, HD, rows), bf16),
            jax.ShapeDtypeStruct((heads, rows, 2 * HD), bf16),
        ),
        in_specs=[pinned] * 6,
        out_specs=(vmem, vmem),
        scratch_shapes=[
            pltpu.SMEM((NBR, neighbours.shape[0]), jnp.int32),
            pltpu.VMEM((heads, rows), f32),
            pltpu.VMEM((tokens, width), bf16),
            pltpu.VMEM((tokens, width), bf16),
            pltpu.VMEM((heads, rows, 2 * HD), bf16),
            pltpu.VMEM((heads, span, 2 * HD), bf16),
            pltpu.VMEM((tiles, rows, LANES), bf16),
            pltpu.VMEM((tiles, rows, LANES), bf16),
            pltpu.VMEM((n_seq, heads, LANES), f32),
            pltpu.VMEM((n_seq, heads, LANES), f32),
            pltpu.VMEM((heads, HD, rows), f32),
            pltpu.VMEM((heads, rows, 2 * HD), f32),
            pltpu.VMEM((heads, span, 2 * HD), bf16),
            pltpu.VMEM((heads, span, 2 * HD), bf16),
            pltpu.VMEM((blocks_pad, rows), f32),
            pltpu.VMEM((8, rows), f32),
            pltpu.VMEM((heads, 8, rows), f32),
            dma((tiles, n_seq)),
            dma((tiles, n_seq)),
            dma((tiles, n_seq - 1)),
            dma((tiles, n_seq - 1)),
            dma((tiles, n_seq - 1)),
            dma((tiles, n_seq - 1)),
            dma((n_seq - 1,)),
            dma((n_seq - 1,)),
            dma((tiles,)),
            dma((tiles,)),
            dma((tiles,)),
            dma((tiles,)),
            dma((4 + tiles,)),
        ],
        compiler_params=pltpu.CompilerParams(
            collective_id=0, has_side_effects=True, vmem_limit_bytes=48 * 1024 * 1024
        ),
    )(
        *[
            pltpu.with_memory_space_constraint(operand, pltpu.HBM)
            for operand in (
                jnp.transpose(neighbours),
                log_totals.reshape(heads, rows),
                upstream.reshape(tokens, width),
                queries.reshape(tokens, width),
                attention_out.reshape(tokens, width),
                keys_values.reshape(heads, rows, 2 * HD),
            )
        ]
    )
    query_grad = jnp.transpose(query_turned, (0, 2, 1)).reshape(1, 1, heads, rows, HD)
    return query_grad, cache_grad.reshape(1, 1, heads, rows, 2 * HD)


def body(upstream, queries, attention_out, keys_values, log_totals, neighbours):
    tokens = queries.shape[2]
    heads, rows = keys_values.shape[2:4]
    fits = (
        lax.axis_size("tp") == 2
        and lax.axis_size("pipe") > 1
        and lax.axis_size("seq") > 1
        and heads == 8
        and tokens % 16 == 0
        and tokens <= LANES
        and rows % LANES == 0
        and REACH * BLK < rows <= 512
    )
    chosen = fused_body if fits else general_body
    return chosen(upstream, queries, attention_out, keys_values, log_totals, neighbours)


def solution(mesh):
    placed = (
        P("pipe", "tp", "seq", None),
        P("pipe", "tp", "seq", None),
        P("pipe", "tp", "seq", None),
        P("pipe", "tp", "seq", None, None),
        P("pipe", "tp", "seq", None),
        P(),
    )
    return jax.shard_map(
        body,
        mesh=mesh,
        in_specs=placed,
        out_specs=(P("pipe", "tp", "seq", None, None), P("pipe", "tp", "seq", None, None)),
        check_vma=False,
    )
```

```python
import jax
import jax.numpy as jnp
from jax import lax
from jax.experimental import pallas as pl
from jax.experimental.pallas import tpu as pltpu
from jax.sharding import PartitionSpec as P

H = 32
HD = 64
BLK = 64
REACH = 4
NBR = 7


pair_group = 32


def passed_along(value, axis, steps):
    count = lax.axis_size(axis)
    pairs = [(source, (source + steps) % count) for source in range(count)]
    return lax.ppermute(value, axis, pairs)


def padded_2(cells, sides, width):
    for axis, dim in sides:
        count = lax.axis_size(axis)
        ends = count - 1
        head = lax.slice_in_dim(cells, 0, width, axis=dim)
        tail = lax.slice_in_dim(cells, cells.shape[dim] - width, cells.shape[dim], axis=dim)
        cells = jnp.concatenate(
            [
                lax.ppermute(tail, axis, [(i, (i + 1) % count) for i in range(ends)]),
                cells,
                lax.ppermute(head, axis, [((i + 1) % count, i) for i in range(ends)]),
            ],
            axis=dim,
        )
    return cells


def block_layout(values, blocks_here):
    heads_here = values.shape[1]
    turned = jnp.transpose(values, (1, 0, 2))
    return turned.reshape(heads_here, blocks_here, BLK, values.shape[2])


def general_body(upstream, queries, attention_out, keys_values, log_totals, neighbours):
    tokens_here = queries.shape[2]
    inv_root = HD ** (-0.5)
    incoming = passed_along(upstream, "pipe", -1)
    query_tok = queries.reshape(tokens_here, H, HD)
    grad_tok = incoming.reshape(tokens_here, H, HD)
    out_tok = attention_out.reshape(tokens_here, H, HD)
    packed = jnp.concatenate([query_tok, grad_tok, out_tok], axis=2)
    regrouped = lax.all_to_all(packed, "seq", split_axis=1, concat_axis=0, tiled=True)
    query_heads = regrouped[:, :, :HD]
    grad_heads = regrouped[:, :, HD : 2 * HD]
    out_heads = regrouped[:, :, 2 * HD :]
    row_delta = jnp.sum(grad_heads.astype(jnp.float32) * out_heads.astype(jnp.float32), axis=2)
    rows_here = query_heads.shape[0]
    heads_here = query_heads.shape[1]
    blocks_here = rows_here // BLK
    query_blocks = block_layout(query_heads, blocks_here)
    grad_blocks = block_layout(grad_heads, blocks_here)
    delta_blocks = jnp.transpose(row_delta).reshape(heads_here, blocks_here, BLK)
    norm_blocks = log_totals.reshape(heads_here, blocks_here, BLK)
    cache_blocks = keys_values.reshape(heads_here, blocks_here, BLK, 2 * HD)
    padded = padded_2(cache_blocks, (("tp", 1),), REACH)
    first_block = lax.axis_index("tp") * blocks_here
    listed = lax.dynamic_slice_in_dim(neighbours, first_block, blocks_here, 0)
    present = (listed >= 0).reshape(-1)
    slot_count = blocks_here * NBR
    group_total = (slot_count + pair_group - 1) // pair_group
    capacity = group_total * pair_group
    running = jnp.cumsum(present.astype(jnp.int32)) - 1
    pair_count = jnp.sum(present.astype(jnp.int32))
    target = jnp.where(present, running, capacity)
    query_source = jnp.repeat(jnp.arange(blocks_here, dtype=jnp.int32), NBR)
    key_source = (listed - first_block + REACH).reshape(-1)
    pair_query = jnp.zeros((capacity,), jnp.int32).at[target].set(query_source, mode="drop")
    pair_key = jnp.zeros((capacity,), jnp.int32).at[target].set(key_source, mode="drop")

    def one_group(group_step, totals):
        query_acc, cache_acc = totals
        first_pair = group_step * pair_group
        query_pick = lax.dynamic_slice_in_dim(pair_query, first_pair, pair_group)
        key_pick = lax.dynamic_slice_in_dim(pair_key, first_pair, pair_group)
        live_mask = (first_pair + jnp.arange(pair_group) < pair_count).astype(jnp.float32)
        query_rows = query_blocks[:, query_pick]
        grad_rows = grad_blocks[:, query_pick]
        norm_rows = norm_blocks[:, query_pick]
        delta_rows = delta_blocks[:, query_pick]
        cache_rows = padded[:, key_pick]
        key_rows = cache_rows[..., :HD]
        value_rows = cache_rows[..., HD:]
        scores = (
            jnp.einsum("hgqd,hgkd->hgqk", query_rows, key_rows, preferred_element_type=jnp.float32)
            * inv_root
        )
        weights = jnp.exp(scores - norm_rows[..., None]) * live_mask[None, :, None, None]
        weights_half = weights.astype(jnp.bfloat16)
        grad_weights = jnp.einsum(
            "hgqd,hgkd->hgqk", grad_rows, value_rows, preferred_element_type=jnp.float32
        )
        grad_scores = (weights * (grad_weights - delta_rows[..., None])).astype(jnp.bfloat16)
        query_part = (
            jnp.einsum("hgqk,hgkd->hgqd", grad_scores, key_rows, preferred_element_type=jnp.float32)
            * inv_root
        )
        key_part = (
            jnp.einsum(
                "hgqk,hgqd->hgkd", grad_scores, query_rows, preferred_element_type=jnp.float32
            )
            * inv_root
        )
        value_part = jnp.einsum(
            "hgqk,hgqd->hgkd", weights_half, grad_rows, preferred_element_type=jnp.float32
        )
        query_acc = query_acc.at[:, query_pick].add(query_part)
        cache_acc = cache_acc.at[:, key_pick].add(jnp.concatenate([key_part, value_part], axis=-1))
        return (query_acc, cache_acc)

    group_live = (pair_count + pair_group - 1) // pair_group
    query_start = jnp.zeros((heads_here, blocks_here, BLK, HD), jnp.float32)
    cache_start = jnp.zeros((heads_here, blocks_here + 2 * REACH, BLK, 2 * HD), jnp.float32)
    query_acc, cache_acc = lax.fori_loop(0, group_live, one_group, (query_start, cache_start))
    rim_terms = jnp.concatenate([cache_acc[:, :REACH], cache_acc[:, REACH + blocks_here :]], axis=1)
    arrived = padded_2(rim_terms.astype(jnp.bfloat16), (("tp", 1),), REACH).astype(rim_terms.dtype)
    own_part = cache_acc[:, REACH : REACH + blocks_here]
    own_part = own_part.at[:, :REACH].add(arrived[:, :REACH])
    own_part = own_part.at[:, blocks_here - REACH :].add(arrived[:, 3 * REACH :])
    query_grad = query_acc.reshape(1, 1, heads_here, rows_here, HD).astype(jnp.bfloat16)
    cache_grad = own_part.reshape(1, 1, heads_here, rows_here, 2 * HD).astype(jnp.bfloat16)
    return (query_grad, cache_grad)


MESH = pl.DeviceIdType.MESH
LANES = 128
PER_TILE = LANES // HD
ABSENT = -1e30
NT = (((1,), (1,)), ((), ()))
TN = (((0,), (0,)), ((), ()))


def dot_f32(left, right, dims=(((1,), (0,)), ((), ()))):
    return lax.dot_general(left, right, dims, preferred_element_type=jnp.float32)


def listed_bias(neigh_ref, first_row, first_key, key_rows, blocks_here):
    lane = lax.broadcasted_iota(jnp.int32, (key_rows, LANES), 1)
    key = lax.broadcasted_iota(jnp.int32, (key_rows, LANES), 0) + first_key
    tiles = []
    for pair in range(blocks_here // 2):
        found = None
        for slot in range(NBR):
            here = jnp.where(
                lane < BLK,
                neigh_ref[slot, first_row + 2 * pair],
                neigh_ref[slot, first_row + 2 * pair + 1],
            )
            hit = (key == here).astype(jnp.float32)
            found = hit if found is None else jnp.maximum(found, hit)
        tiles.append((found - 1.0) * -ABSENT)
    return jnp.concatenate(tiles, axis=1)


def fused_kernel(
    neigh_hbm, norm_hbm, up_ref, query_ref, out_ref, cache_ref, dq_ref, dkv_ref,
    neigh_ref, norm_ref, inc, outs, kv, halo, qbuf, gbuf, dsend, dgot, acc, acc_kv, back_out, back_in, bias_own, bias_halo, rows_aux, joint,
    up_send, up_recv, q_send, q_recv, g_send, g_recv, d_send, d_recv, h_send, h_recv, b_send, b_recv, local_sem,
):
    n_pipe, n_seq = lax.axis_size("pipe"), lax.axis_size("seq")
    pipe, seq, tp = lax.axis_index("pipe"), lax.axis_index("seq"), lax.axis_index("tp")
    tokens, width = inc.shape
    heads, rows, _ = kv.shape
    tiles = heads // PER_TILE
    span = REACH * BLK
    blocks_here = rows // BLK
    share = heads * HD
    below, above = lax.rem(pipe + n_pipe - 1, n_pipe), lax.rem(pipe + 1, n_pipe)
    mate = 1 - tp
    window = pl.multiple_of(mate * (rows - span), LANES)
    mine = pl.multiple_of(seq * tokens, 16)

    def peer(step):
        return lax.rem(seq + step, n_seq)

    def tile_cols(dest, tile):
        return pl.ds(pl.multiple_of(dest * share + tile * LANES, LANES), LANES)

    def up_copy(tile, dest):
        cols = pl.ds(dest * share + tile * LANES, LANES)
        return pltpu.make_async_remote_copy(
            src_ref=up_ref.at[:, cols], dst_ref=inc.at[:, cols],
            send_sem=up_send.at[tile, dest], recv_sem=up_recv.at[tile, dest],
            device_id={"pipe": below}, device_id_type=MESH,
        )

    def q_copy(tile, step):
        return pltpu.make_async_remote_copy(
            src_ref=query_ref.at[:, tile_cols(peer(step), tile)],
            dst_ref=qbuf.at[tile, pl.ds(mine, tokens), :],
            send_sem=q_send.at[tile, step - 1], recv_sem=q_recv.at[tile, step - 1],
            device_id={"seq": peer(step)}, device_id_type=MESH,
        )

    def g_copy(tile, step):
        return pltpu.make_async_remote_copy(
            src_ref=inc.at[:, tile_cols(peer(step), tile)],
            dst_ref=gbuf.at[tile, pl.ds(mine, tokens), :],
            send_sem=g_send.at[tile, step - 1], recv_sem=g_recv.at[tile, step - 1],
            device_id={"seq": peer(step)}, device_id_type=MESH,
        )

    def d_copy(step):
        return pltpu.make_async_remote_copy(
            src_ref=dsend.at[peer(step)], dst_ref=dgot.at[seq],
            send_sem=d_send.at[step - 1], recv_sem=d_recv.at[step - 1],
            device_id={"seq": peer(step)}, device_id_type=MESH,
        )

    def h_copy(tile):
        pair = pl.ds(tile * PER_TILE, PER_TILE)
        return pltpu.make_async_remote_copy(
            src_ref=cache_ref.at[pair, pl.ds(window, span), :], dst_ref=halo.at[pair],
            send_sem=h_send.at[tile], recv_sem=h_recv.at[tile],
            device_id={"tp": mate}, device_id_type=MESH,
        )

    def b_copy(tile):
        pair = pl.ds(tile * PER_TILE, PER_TILE)
        return pltpu.make_async_remote_copy(
            src_ref=back_out.at[pair], dst_ref=back_in.at[pair],
            send_sem=b_send.at[tile], recv_sem=b_recv.at[tile],
            device_id={"tp": mate}, device_id_type=MESH,
        )

    out_local = pltpu.make_async_copy(out_ref, outs, local_sem.at[0])
    kv_local = pltpu.make_async_copy(cache_ref, kv, local_sem.at[1])
    q_local = [
        pltpu.make_async_copy(
            query_ref.at[:, tile_cols(seq, tile)], qbuf.at[tile, pl.ds(mine, tokens), :], local_sem.at[2 + tile]
        )
        for tile in range(tiles)
    ]
    neigh_local = pltpu.make_async_copy(neigh_hbm, neigh_ref, local_sem.at[2 + tiles])
    norm_local = pltpu.make_async_copy(norm_hbm, norm_ref, local_sem.at[3 + tiles])
    neigh_local.start()
    norm_local.start()
    out_local.start()
    kv_local.start()
    for copy in q_local:
        copy.start()

    barrier = pltpu.get_barrier_semaphore()
    pl.semaphore_signal(barrier, inc=1, device_id={"pipe": above}, device_id_type=MESH)
    pl.semaphore_signal(barrier, inc=1, device_id={"tp": mate}, device_id_type=MESH)
    for step in range(1, n_seq):
        pl.semaphore_signal(barrier, inc=1, device_id={"seq": peer(step)}, device_id_type=MESH)
    pl.semaphore_wait(barrier, n_seq + 1)

    for tile in range(tiles):
        for dest in range(n_seq):
            up_copy(tile, dest).start()
        if tile == 0:
            h_copy(tile).start()
        if tile < 2:
            for step in range(1, n_seq):
                q_copy(tile, step).start()

    neigh_local.wait()
    first_row = tp * blocks_here
    halo_key = mate * blocks_here + tp * (blocks_here - REACH)
    bias_own[...] = listed_bias(neigh_ref, first_row, first_row, bias_own.shape[0], blocks_here)
    bias_halo[...] = listed_bias(neigh_ref, first_row, halo_key, bias_halo.shape[0], blocks_here)

    for tile in range(tiles):
        for dest in range(n_seq):
            up_copy(tile, dest).wait_recv()
        for step in range(1, n_seq):
            g_copy(tile, step).start()
        if tile + 1 < tiles:
            h_copy(tile + 1).start()
        if tile + 2 < tiles:
            for step in range(1, n_seq):
                q_copy(tile + 2, step).start()

    out_local.wait()
    picks = (
        lax.broadcasted_iota(jnp.int32, (heads, share), 1) // HD
        == lax.broadcasted_iota(jnp.int32, (heads, share), 0)
    ).astype(jnp.bfloat16)
    dsend[...] = jnp.zeros_like(dsend)
    for dest in range(n_seq):
        cols = pl.ds(dest * share, share)
        terms = inc[:, cols].astype(jnp.float32) * outs[:, cols].astype(jnp.float32)
        high = terms.astype(jnp.bfloat16)
        low = (terms - high.astype(jnp.float32)).astype(jnp.bfloat16)
        dsend[dest, :, :tokens] = dot_f32(picks, high, NT) + dot_f32(picks, low, NT)
    for step in range(1, n_seq):
        d_copy(step).start()
    dgot[seq] = dsend[seq]
    for tile in range(tiles):
        gbuf[tile, pl.ds(mine, tokens), :] = inc[:, tile_cols(seq, tile)]
    kv_local.wait()
    for copy in q_local:
        copy.wait()
    for step in range(1, n_seq):
        d_copy(step).wait_recv()
    delta = None
    for source in range(n_seq):
        part = jnp.concatenate([dgot[source], jnp.zeros((heads, rows - LANES), jnp.float32)], axis=1)
        if source:
            part = pltpu.roll(part, source * tokens, 1)
        delta = part if delta is None else delta + part
    norm_local.wait()
    norm = norm_ref[...]
    for head in range(heads):
        rows_aux[head, 0:1, :] = norm[head : head + 1]
        rows_aux[head, 1:2, :] = delta[head : head + 1]

    inv_root = HD ** (-0.5)
    key_lane = lax.broadcasted_iota(jnp.int32, (1, 2 * HD), 1) < HD
    lane_scale = jnp.where(key_lane, inv_root, 1.0)
    lane_scale_half = lane_scale.astype(jnp.bfloat16)

    def block_terms(cache_rows, both_rows, bias, norm_row, delta_row):
        count, width_here = cache_rows.shape[0] // BLK, delta_row.shape[1]
        scaled = cache_rows * lane_scale_half
        products = dot_f32(scaled, both_rows, NT)
        scores = products[:, :width_here].reshape(count, BLK, width_here)
        shift = bias[:count] - norm_row
        weights = jnp.exp(scores + shift[:, None, :]).reshape(count * BLK, width_here)
        grad_scores = (weights * (products[:, width_here:] - delta_row)).astype(jnp.bfloat16)
        joined = jnp.concatenate([grad_scores, weights.astype(jnp.bfloat16)], axis=1)
        cache_part = dot_f32(joined, both_rows) * lane_scale
        query_part = dot_f32(scaled[:, :HD], grad_scores, TN)
        return query_part, cache_part

    def one_tile(tile, carry):
        for step in range(1, n_seq):
            q_copy(tile, step).wait_recv()
            g_copy(tile, step).wait_recv()
        blank = jnp.zeros((rows, HD), jnp.bfloat16)
        for inner in range(PER_TILE):
            lanes = slice(inner * HD, (inner + 1) * HD)
            joint[inner, 0] = jnp.concatenate([qbuf[tile, :, lanes], blank], axis=1)
            joint[inner, 1] = jnp.concatenate([blank, gbuf[tile, :, lanes]], axis=1)
        h_copy(tile).wait_recv()
        for inner in range(PER_TILE):
            head = tile * PER_TILE + inner
            query_part, cache_part = block_terms(
                halo[head],
                joint[inner, :, pl.ds(window, span), :].reshape(2 * span, LANES),
                bias_halo[:, pl.ds(window, span)],
                rows_aux[head, 0:1, pl.ds(window, span)],
                rows_aux[head, 1:2, pl.ds(window, span)],
            )
            back_out[head] = cache_part.astype(jnp.bfloat16)
            acc[head, :, pl.ds(window, span)] = query_part
            acc[head, :, pl.ds(pl.multiple_of(tp * span, LANES), rows - span)] = jnp.zeros(
                (HD, rows - span), jnp.float32
            )
        b_copy(tile).start()
        for inner in range(PER_TILE):
            head = tile * PER_TILE + inner
            query_part, cache_part = block_terms(
                kv[head],
                joint[inner].reshape(2 * rows, LANES),
                bias_own[...],
                rows_aux[head, 0:1, :],
                rows_aux[head, 1:2, :],
            )
            dq_ref[head] = (acc[head] + query_part).astype(jnp.bfloat16)
            acc_kv[head] = cache_part
        return carry

    lax.fori_loop(0, tiles, one_tile, 0)

    def finish(tile, carry):
        b_copy(tile).wait_recv()
        for inner in range(PER_TILE):
            head = tile * PER_TILE + inner
            acc_kv[head, pl.ds(window, span), :] += back_in[head].astype(jnp.float32)
            dkv_ref[head] = acc_kv[head].astype(jnp.bfloat16)
        return carry

    lax.fori_loop(0, tiles, finish, 0)

    for tile in range(tiles):
        for dest in range(n_seq):
            up_copy(tile, dest).wait_send()
        for step in range(1, n_seq):
            q_copy(tile, step).wait_send()
            g_copy(tile, step).wait_send()
        h_copy(tile).wait_send()
        b_copy(tile).wait_send()
    for step in range(1, n_seq):
        d_copy(step).wait_send()


def fused_body(upstream, queries, attention_out, keys_values, log_totals, neighbours):
    tokens, width = queries.shape[2:]
    heads, rows = keys_values.shape[2:4]
    tiles = heads // PER_TILE
    n_seq = lax.axis_size("seq")
    span = REACH * BLK
    blocks_pad = 8 * -(-(rows // BLK) // 8)
    bf16, f32 = jnp.bfloat16, jnp.float32
    vmem = pl.BlockSpec(memory_space=pltpu.VMEM)
    pinned = pl.BlockSpec(memory_space=pltpu.HBM)
    dma = pltpu.SemaphoreType.DMA
    query_turned, cache_grad = pl.pallas_call(
        fused_kernel,
        out_shape=(
            jax.ShapeDtypeStruct((heads, HD, rows), bf16),
            jax.ShapeDtypeStruct((heads, rows, 2 * HD), bf16),
        ),
        in_specs=[pinned] * 6,
        out_specs=(vmem, vmem),
        scratch_shapes=[
            pltpu.SMEM((NBR, neighbours.shape[0]), jnp.int32),
            pltpu.VMEM((heads, rows), f32),
            pltpu.VMEM((tokens, width), bf16),
            pltpu.VMEM((tokens, width), bf16),
            pltpu.VMEM((heads, rows, 2 * HD), bf16),
            pltpu.VMEM((heads, span, 2 * HD), bf16),
            pltpu.VMEM((tiles, rows, LANES), bf16),
            pltpu.VMEM((tiles, rows, LANES), bf16),
            pltpu.VMEM((n_seq, heads, LANES), f32),
            pltpu.VMEM((n_seq, heads, LANES), f32),
            pltpu.VMEM((heads, HD, rows), f32),
            pltpu.VMEM((heads, rows, 2 * HD), f32),
            pltpu.VMEM((heads, span, 2 * HD), bf16),
            pltpu.VMEM((heads, span, 2 * HD), bf16),
            pltpu.VMEM((blocks_pad, rows), f32),
            pltpu.VMEM((8, rows), f32),
            pltpu.VMEM((heads, 8, rows), f32),
            pltpu.VMEM((PER_TILE, 2, rows, LANES), bf16),
            dma((tiles, n_seq)),
            dma((tiles, n_seq)),
            dma((tiles, n_seq - 1)),
            dma((tiles, n_seq - 1)),
            dma((tiles, n_seq - 1)),
            dma((tiles, n_seq - 1)),
            dma((n_seq - 1,)),
            dma((n_seq - 1,)),
            dma((tiles,)),
            dma((tiles,)),
            dma((tiles,)),
            dma((tiles,)),
            dma((4 + tiles,)),
        ],
        compiler_params=pltpu.CompilerParams(
            collective_id=0, has_side_effects=True, vmem_limit_bytes=48 * 1024 * 1024
        ),
    )(
        *[
            pltpu.with_memory_space_constraint(operand, pltpu.HBM)
            for operand in (
                jnp.transpose(neighbours),
                log_totals.reshape(heads, rows),
                upstream.reshape(tokens, width),
                queries.reshape(tokens, width),
                attention_out.reshape(tokens, width),
                keys_values.reshape(heads, rows, 2 * HD),
            )
        ]
    )
    query_grad = jnp.transpose(query_turned, (0, 2, 1)).reshape(1, 1, heads, rows, HD)
    return query_grad, cache_grad.reshape(1, 1, heads, rows, 2 * HD)


def body(upstream, queries, attention_out, keys_values, log_totals, neighbours):
    tokens = queries.shape[2]
    heads, rows = keys_values.shape[2:4]
    fits = (
        lax.axis_size("tp") == 2
        and lax.axis_size("pipe") > 1
        and lax.axis_size("seq") > 1
        and heads == 8
        and tokens % 16 == 0
        and tokens <= LANES
        and rows % LANES == 0
        and REACH * BLK < rows <= 512
    )
    chosen = fused_body if fits else general_body
    return chosen(upstream, queries, attention_out, keys_values, log_totals, neighbours)


def solution(mesh):
    placed = (
        P("pipe", "tp", "seq", None),
        P("pipe", "tp", "seq", None),
        P("pipe", "tp", "seq", None),
        P("pipe", "tp", "seq", None, None),
        P("pipe", "tp", "seq", None),
        P(),
    )
    return jax.shard_map(
        body,
        mesh=mesh,
        in_specs=placed,
        out_specs=(P("pipe", "tp", "seq", None, None), P("pipe", "tp", "seq", None, None)),
        check_vma=False,
    )
```

```python
import jax
import jax.numpy as jnp
from jax import lax
from jax.experimental import pallas as pl
from jax.experimental.pallas import tpu as pltpu
from jax.sharding import PartitionSpec as P

H = 32
HD = 64
BLK = 64
REACH = 4
NBR = 7


pair_group = 32


def passed_along(value, axis, steps):
    count = lax.axis_size(axis)
    pairs = [(source, (source + steps) % count) for source in range(count)]
    return lax.ppermute(value, axis, pairs)


def padded_2(cells, sides, width):
    for axis, dim in sides:
        count = lax.axis_size(axis)
        ends = count - 1
        head = lax.slice_in_dim(cells, 0, width, axis=dim)
        tail = lax.slice_in_dim(cells, cells.shape[dim] - width, cells.shape[dim], axis=dim)
        cells = jnp.concatenate(
            [
                lax.ppermute(tail, axis, [(i, (i + 1) % count) for i in range(ends)]),
                cells,
                lax.ppermute(head, axis, [((i + 1) % count, i) for i in range(ends)]),
            ],
            axis=dim,
        )
    return cells


def block_layout(values, blocks_here):
    heads_here = values.shape[1]
    turned = jnp.transpose(values, (1, 0, 2))
    return turned.reshape(heads_here, blocks_here, BLK, values.shape[2])


def general_body(upstream, queries, attention_out, keys_values, log_totals, neighbours):
    tokens_here = queries.shape[2]
    inv_root = HD ** (-0.5)
    incoming = passed_along(upstream, "pipe", -1)
    query_tok = queries.reshape(tokens_here, H, HD)
    grad_tok = incoming.reshape(tokens_here, H, HD)
    out_tok = attention_out.reshape(tokens_here, H, HD)
    packed = jnp.concatenate([query_tok, grad_tok, out_tok], axis=2)
    regrouped = lax.all_to_all(packed, "seq", split_axis=1, concat_axis=0, tiled=True)
    query_heads = regrouped[:, :, :HD]
    grad_heads = regrouped[:, :, HD : 2 * HD]
    out_heads = regrouped[:, :, 2 * HD :]
    row_delta = jnp.sum(grad_heads.astype(jnp.float32) * out_heads.astype(jnp.float32), axis=2)
    rows_here = query_heads.shape[0]
    heads_here = query_heads.shape[1]
    blocks_here = rows_here // BLK
    query_blocks = block_layout(query_heads, blocks_here)
    grad_blocks = block_layout(grad_heads, blocks_here)
    delta_blocks = jnp.transpose(row_delta).reshape(heads_here, blocks_here, BLK)
    norm_blocks = log_totals.reshape(heads_here, blocks_here, BLK)
    cache_blocks = keys_values.reshape(heads_here, blocks_here, BLK, 2 * HD)
    padded = padded_2(cache_blocks, (("tp", 1),), REACH)
    first_block = lax.axis_index("tp") * blocks_here
    listed = lax.dynamic_slice_in_dim(neighbours, first_block, blocks_here, 0)
    present = (listed >= 0).reshape(-1)
    slot_count = blocks_here * NBR
    group_total = (slot_count + pair_group - 1) // pair_group
    capacity = group_total * pair_group
    running = jnp.cumsum(present.astype(jnp.int32)) - 1
    pair_count = jnp.sum(present.astype(jnp.int32))
    target = jnp.where(present, running, capacity)
    query_source = jnp.repeat(jnp.arange(blocks_here, dtype=jnp.int32), NBR)
    key_source = (listed - first_block + REACH).reshape(-1)
    pair_query = jnp.zeros((capacity,), jnp.int32).at[target].set(query_source, mode="drop")
    pair_key = jnp.zeros((capacity,), jnp.int32).at[target].set(key_source, mode="drop")

    def one_group(group_step, totals):
        query_acc, cache_acc = totals
        first_pair = group_step * pair_group
        query_pick = lax.dynamic_slice_in_dim(pair_query, first_pair, pair_group)
        key_pick = lax.dynamic_slice_in_dim(pair_key, first_pair, pair_group)
        live_mask = (first_pair + jnp.arange(pair_group) < pair_count).astype(jnp.float32)
        query_rows = query_blocks[:, query_pick]
        grad_rows = grad_blocks[:, query_pick]
        norm_rows = norm_blocks[:, query_pick]
        delta_rows = delta_blocks[:, query_pick]
        cache_rows = padded[:, key_pick]
        key_rows = cache_rows[..., :HD]
        value_rows = cache_rows[..., HD:]
        scores = (
            jnp.einsum("hgqd,hgkd->hgqk", query_rows, key_rows, preferred_element_type=jnp.float32)
            * inv_root
        )
        weights = jnp.exp(scores - norm_rows[..., None]) * live_mask[None, :, None, None]
        weights_half = weights.astype(jnp.bfloat16)
        grad_weights = jnp.einsum(
            "hgqd,hgkd->hgqk", grad_rows, value_rows, preferred_element_type=jnp.float32
        )
        grad_scores = (weights * (grad_weights - delta_rows[..., None])).astype(jnp.bfloat16)
        query_part = (
            jnp.einsum("hgqk,hgkd->hgqd", grad_scores, key_rows, preferred_element_type=jnp.float32)
            * inv_root
        )
        key_part = (
            jnp.einsum(
                "hgqk,hgqd->hgkd", grad_scores, query_rows, preferred_element_type=jnp.float32
            )
            * inv_root
        )
        value_part = jnp.einsum(
            "hgqk,hgqd->hgkd", weights_half, grad_rows, preferred_element_type=jnp.float32
        )
        query_acc = query_acc.at[:, query_pick].add(query_part)
        cache_acc = cache_acc.at[:, key_pick].add(jnp.concatenate([key_part, value_part], axis=-1))
        return (query_acc, cache_acc)

    group_live = (pair_count + pair_group - 1) // pair_group
    query_start = jnp.zeros((heads_here, blocks_here, BLK, HD), jnp.float32)
    cache_start = jnp.zeros((heads_here, blocks_here + 2 * REACH, BLK, 2 * HD), jnp.float32)
    query_acc, cache_acc = lax.fori_loop(0, group_live, one_group, (query_start, cache_start))
    rim_terms = jnp.concatenate([cache_acc[:, :REACH], cache_acc[:, REACH + blocks_here :]], axis=1)
    arrived = padded_2(rim_terms.astype(jnp.bfloat16), (("tp", 1),), REACH).astype(rim_terms.dtype)
    own_part = cache_acc[:, REACH : REACH + blocks_here]
    own_part = own_part.at[:, :REACH].add(arrived[:, :REACH])
    own_part = own_part.at[:, blocks_here - REACH :].add(arrived[:, 3 * REACH :])
    query_grad = query_acc.reshape(1, 1, heads_here, rows_here, HD).astype(jnp.bfloat16)
    cache_grad = own_part.reshape(1, 1, heads_here, rows_here, 2 * HD).astype(jnp.bfloat16)
    return (query_grad, cache_grad)


MESH = pl.DeviceIdType.MESH
LANES = 128
PER_TILE = LANES // HD
ABSENT = -1e30
NT = (((1,), (1,)), ((), ()))
TN = (((0,), (0,)), ((), ()))


def dot_f32(left, right, dims=(((1,), (0,)), ((), ()))):
    return lax.dot_general(left, right, dims, preferred_element_type=jnp.float32)


def listed_bias(neigh_ref, first_row, first_key, key_rows, blocks_here):
    lane = lax.broadcasted_iota(jnp.int32, (key_rows, LANES), 1)
    key = lax.broadcasted_iota(jnp.int32, (key_rows, LANES), 0) + first_key
    tiles = []
    for pair in range(blocks_here // 2):
        found = None
        for slot in range(NBR):
            here = jnp.where(
                lane < BLK,
                neigh_ref[slot, first_row + 2 * pair],
                neigh_ref[slot, first_row + 2 * pair + 1],
            )
            hit = (key == here).astype(jnp.float32)
            found = hit if found is None else jnp.maximum(found, hit)
        tiles.append((found - 1.0) * -ABSENT)
    return jnp.concatenate(tiles, axis=1)


def fused_kernel(
    neigh_hbm, norm_hbm, up_ref, query_ref, out_ref, cache_ref, dq_ref, dkv_ref,
    neigh_ref, norm_ref, inc, outs, kv, halo, qbuf, gbuf, dsend, dgot, acc, acc_kv, back_out, back_in, bias_own, bias_halo, bias_cross, aux, aux_got, joint,
    joint_cross, ahead_q, ahead_g, turned_out, turned_in,
    up_send, up_recv, q_send, q_recv, g_send, g_recv, d_send, d_recv, h_send, h_recv, b_send, b_recv, a_send, a_recv, t_send, t_recv, x_send, x_recv, local_sem,
):
    n_pipe, n_seq = lax.axis_size("pipe"), lax.axis_size("seq")
    pipe, seq, tp = lax.axis_index("pipe"), lax.axis_index("seq"), lax.axis_index("tp")
    tokens, width = inc.shape
    heads, rows, _ = kv.shape
    tiles = heads // PER_TILE
    span = REACH * BLK
    blocks_here = rows // BLK
    share = heads * HD
    below, above = lax.rem(pipe + n_pipe - 1, n_pipe), lax.rem(pipe + 1, n_pipe)
    mate = 1 - tp
    handed = ahead_q.shape[0]
    window = pl.multiple_of(mate * (rows - span), LANES)
    mine = pl.multiple_of(seq * tokens, 16)

    def peer(step):
        return lax.rem(seq + step, n_seq)

    def tile_cols(dest, tile):
        return pl.ds(pl.multiple_of(dest * share + tile * LANES, LANES), LANES)

    def up_copy(tile, dest):
        cols = pl.ds(dest * share + tile * LANES, LANES)
        return pltpu.make_async_remote_copy(
            src_ref=up_ref.at[:, cols], dst_ref=inc.at[:, cols],
            send_sem=up_send.at[tile, dest], recv_sem=up_recv.at[tile, dest],
            device_id={"pipe": below}, device_id_type=MESH,
        )

    def q_copy(tile, step):
        return pltpu.make_async_remote_copy(
            src_ref=query_ref.at[:, tile_cols(peer(step), tile)],
            dst_ref=qbuf.at[tile, pl.ds(mine, tokens), :],
            send_sem=q_send.at[tile, step - 1], recv_sem=q_recv.at[tile, step - 1],
            device_id={"seq": peer(step)}, device_id_type=MESH,
        )

    def g_copy(tile, step):
        return pltpu.make_async_remote_copy(
            src_ref=inc.at[:, tile_cols(peer(step), tile)],
            dst_ref=gbuf.at[tile, pl.ds(mine, tokens), :],
            send_sem=g_send.at[tile, step - 1], recv_sem=g_recv.at[tile, step - 1],
            device_id={"seq": peer(step)}, device_id_type=MESH,
        )

    def d_copy(step):
        return pltpu.make_async_remote_copy(
            src_ref=dsend.at[peer(step)], dst_ref=dgot.at[seq],
            send_sem=d_send.at[step - 1], recv_sem=d_recv.at[step - 1],
            device_id={"seq": peer(step)}, device_id_type=MESH,
        )

    def h_copy(tile):
        pair = pl.ds(tile * PER_TILE, PER_TILE)
        return pltpu.make_async_remote_copy(
            src_ref=cache_ref.at[pair, pl.ds(window, span), :], dst_ref=halo.at[pair],
            send_sem=h_send.at[tile], recv_sem=h_recv.at[tile],
            device_id={"tp": mate}, device_id_type=MESH,
        )

    def b_copy(tile):
        pair = pl.ds(tile * PER_TILE, PER_TILE)
        return pltpu.make_async_remote_copy(
            src_ref=back_out.at[pair], dst_ref=back_in.at[pair],
            send_sem=b_send.at[tile], recv_sem=b_recv.at[tile],
            device_id={"tp": mate}, device_id_type=MESH,
        )

    def a_copy(tile, kind):
        source, target = ((qbuf, ahead_q), (gbuf, ahead_g))[kind]
        return pltpu.make_async_remote_copy(
            src_ref=source.at[tile, pl.ds(window, span), :], dst_ref=target.at[tile],
            send_sem=a_send.at[tile, kind], recv_sem=a_recv.at[tile, kind],
            device_id={"tp": mate}, device_id_type=MESH,
        )

    def t_copy(tile):
        pair = pl.ds(tile * PER_TILE, PER_TILE)
        return pltpu.make_async_remote_copy(
            src_ref=turned_out.at[pair], dst_ref=turned_in.at[pair],
            send_sem=t_send.at[tile], recv_sem=t_recv.at[tile],
            device_id={"tp": mate}, device_id_type=MESH,
        )

    x_copy = pltpu.make_async_remote_copy(
        src_ref=aux, dst_ref=aux_got, send_sem=x_send.at[0], recv_sem=x_recv.at[0],
        device_id={"tp": mate}, device_id_type=MESH,
    )

    out_local = pltpu.make_async_copy(out_ref, outs, local_sem.at[0])
    kv_local = pltpu.make_async_copy(cache_ref, kv, local_sem.at[1])
    q_local = [
        pltpu.make_async_copy(
            query_ref.at[:, tile_cols(seq, tile)], qbuf.at[tile, pl.ds(mine, tokens), :], local_sem.at[2 + tile]
        )
        for tile in range(tiles)
    ]
    neigh_local = pltpu.make_async_copy(neigh_hbm, neigh_ref, local_sem.at[2 + tiles])
    norm_local = pltpu.make_async_copy(norm_hbm, norm_ref, local_sem.at[3 + tiles])
    neigh_local.start()
    norm_local.start()
    out_local.start()
    kv_local.start()
    for copy in q_local:
        copy.start()

    barrier = pltpu.get_barrier_semaphore()
    pl.semaphore_signal(barrier, inc=1, device_id={"pipe": above}, device_id_type=MESH)
    pl.semaphore_signal(barrier, inc=1, device_id={"tp": mate}, device_id_type=MESH)
    for step in range(1, n_seq):
        pl.semaphore_signal(barrier, inc=1, device_id={"seq": peer(step)}, device_id_type=MESH)
    pl.semaphore_wait(barrier, n_seq + 1)

    for tile in range(tiles):
        for dest in range(n_seq):
            up_copy(tile, dest).start()
        if tile == 0:
            h_copy(handed).start()
        if tile < 2:
            for step in range(1, n_seq):
                q_copy(tile, step).start()

    neigh_local.wait()
    first_row = tp * blocks_here
    halo_key = mate * blocks_here + tp * (blocks_here - REACH)
    bias_own[...] = listed_bias(neigh_ref, first_row, first_row, bias_own.shape[0], blocks_here)
    bias_halo[...] = listed_bias(neigh_ref, first_row, halo_key, bias_halo.shape[0], blocks_here)
    cross_key = first_row + mate * (blocks_here - REACH)
    bias_cross[...] = listed_bias(neigh_ref, mate * blocks_here, cross_key, bias_cross.shape[0], blocks_here)
    mate_window = pl.multiple_of(tp * (rows - span), LANES)

    for tile in range(tiles):
        for dest in range(n_seq):
            up_copy(tile, dest).wait_recv()
        for step in range(1, n_seq):
            g_copy(tile, step).start()
        if handed + tile + 1 < tiles:
            h_copy(handed + tile + 1).start()
        if tile + 2 < tiles:
            for step in range(1, n_seq):
                q_copy(tile + 2, step).start()

    out_local.wait()
    picks = (
        lax.broadcasted_iota(jnp.int32, (heads, share), 1) // HD
        == lax.broadcasted_iota(jnp.int32, (heads, share), 0)
    ).astype(jnp.bfloat16)
    dsend[...] = jnp.zeros_like(dsend)
    for dest in range(n_seq):
        cols = pl.ds(dest * share, share)
        terms = inc[:, cols].astype(jnp.float32) * outs[:, cols].astype(jnp.float32)
        high = terms.astype(jnp.bfloat16)
        low = (terms - high.astype(jnp.float32)).astype(jnp.bfloat16)
        dsend[dest, :, :tokens] = dot_f32(picks, high, NT) + dot_f32(picks, low, NT)
    for step in range(1, n_seq):
        d_copy(step).start()
    dgot[seq] = dsend[seq]
    for tile in range(tiles):
        gbuf[tile, pl.ds(mine, tokens), :] = inc[:, tile_cols(seq, tile)]
    kv_local.wait()
    for copy in q_local:
        copy.wait()
    for step in range(1, n_seq):
        d_copy(step).wait_recv()
    delta = None
    for source in range(n_seq):
        part = jnp.concatenate([dgot[source], jnp.zeros((heads, rows - LANES), jnp.float32)], axis=1)
        if source:
            part = pltpu.roll(part, source * tokens, 1)
        delta = part if delta is None else delta + part
    norm_local.wait()
    aux[0] = norm_ref[...]
    aux[1] = delta
    x_copy.start()

    inv_root = HD ** (-0.5)
    key_lane = lax.broadcasted_iota(jnp.int32, (1, 2 * HD), 1) < HD
    lane_scale = jnp.where(key_lane, inv_root, 1.0)
    lane_scale_half = lane_scale.astype(jnp.bfloat16)

    def block_terms(cache_rows, both_rows, bias, norm_row, delta_row):
        count, width_here = cache_rows.shape[0] // BLK, delta_row.shape[1]
        scaled = cache_rows * lane_scale_half
        products = dot_f32(scaled, both_rows, NT)
        scores = products[:, :width_here].reshape(count, BLK, width_here)
        shift = bias[:count] - norm_row
        weights = jnp.exp(scores + shift[:, None, :]).reshape(count * BLK, width_here)
        grad_scores = (weights * (products[:, width_here:] - delta_row)).astype(jnp.bfloat16)
        joined = jnp.concatenate([grad_scores, weights.astype(jnp.bfloat16)], axis=1)
        cache_part = dot_f32(joined, both_rows) * lane_scale
        query_part = dot_f32(scaled[:, :HD], grad_scores, TN)
        return query_part, cache_part

    def one_tile(tile, carry):
        for step in range(1, n_seq):
            q_copy(tile, step).wait_recv()
            g_copy(tile, step).wait_recv()

        @pl.when(tile < handed)
        def _():
            a_copy(tile, 0).start()
            a_copy(tile, 1).start()

        blank = jnp.zeros((rows, HD), jnp.bfloat16)
        for inner in range(PER_TILE):
            lanes = slice(inner * HD, (inner + 1) * HD)
            joint[inner, 0] = jnp.concatenate([qbuf[tile, :, lanes], blank], axis=1)
            joint[inner, 1] = jnp.concatenate([blank, gbuf[tile, :, lanes]], axis=1)
        @pl.when(tile < handed)
        def _():
            pair = pl.ds(tile * PER_TILE, PER_TILE)
            acc[pair] = jnp.zeros((PER_TILE, HD, rows), jnp.float32)

        @pl.when(tile >= handed)
        def _():
            h_copy(tile).wait_recv()
            for inner in range(PER_TILE):
                head = tile * PER_TILE + inner
                query_part, cache_part = block_terms(
                    halo[head],
                    joint[inner, :, pl.ds(window, span), :].reshape(2 * span, LANES),
                    bias_halo[:, pl.ds(window, span)],
                    aux[0, pl.ds(head, 1), pl.ds(window, span)],
                    aux[1, pl.ds(head, 1), pl.ds(window, span)],
                )
                back_out[head] = cache_part.astype(jnp.bfloat16)
                acc[head, :, pl.ds(window, span)] = query_part
                acc[head, :, pl.ds(pl.multiple_of(tp * span, LANES), rows - span)] = jnp.zeros(
                    (HD, rows - span), jnp.float32
                )
            b_copy(tile).start()

        for inner in range(PER_TILE):
            head = tile * PER_TILE + inner
            query_part, cache_part = block_terms(
                kv[head],
                joint[inner].reshape(2 * rows, LANES),
                bias_own[...],
                aux[0, pl.ds(head, 1), :],
                aux[1, pl.ds(head, 1), :],
            )
            acc[head] += query_part
            acc_kv[head] = cache_part

        @pl.when(tile == 1)
        def _():
            x_copy.wait_recv()

        @pl.when((tile >= 1) & (tile <= handed))
        def _():
            before = tile - 1
            a_copy(before, 0).wait_recv()
            a_copy(before, 1).wait_recv()
            empty = jnp.zeros((span, HD), jnp.bfloat16)
            for inner in range(PER_TILE):
                lanes = slice(inner * HD, (inner + 1) * HD)
                joint_cross[inner, 0] = jnp.concatenate([ahead_q[before, :, lanes], empty], axis=1)
                joint_cross[inner, 1] = jnp.concatenate([empty, ahead_g[before, :, lanes]], axis=1)
            for inner in range(PER_TILE):
                head = before * PER_TILE + inner
                query_part, cache_part = block_terms(
                    kv[head, pl.ds(window, span), :],
                    joint_cross[inner].reshape(2 * span, LANES),
                    bias_cross[:, pl.ds(mate_window, span)],
                    aux_got[0, pl.ds(head, 1), pl.ds(mate_window, span)],
                    aux_got[1, pl.ds(head, 1), pl.ds(mate_window, span)],
                )
                turned_out[head] = query_part.astype(jnp.bfloat16)
                acc_kv[head, pl.ds(window, span), :] += cache_part
            t_copy(before).start()

        return carry

    lax.fori_loop(0, tiles, one_tile, 0)

    def finish(tile, carry):
        @pl.when(tile < handed)
        def _():
            t_copy(tile).wait_recv()
            for inner in range(PER_TILE):
                head = tile * PER_TILE + inner
                acc[head, :, pl.ds(window, span)] += turned_in[head].astype(jnp.float32)

        @pl.when(tile >= handed)
        def _():
            b_copy(tile).wait_recv()
            for inner in range(PER_TILE):
                head = tile * PER_TILE + inner
                acc_kv[head, pl.ds(window, span), :] += back_in[head].astype(jnp.float32)

        for inner in range(PER_TILE):
            head = tile * PER_TILE + inner
            dq_ref[head] = acc[head].astype(jnp.bfloat16)
            dkv_ref[head] = acc_kv[head].astype(jnp.bfloat16)
        return carry

    lax.fori_loop(0, tiles, finish, 0)

    for tile in range(tiles):
        for dest in range(n_seq):
            up_copy(tile, dest).wait_send()
        for step in range(1, n_seq):
            q_copy(tile, step).wait_send()
            g_copy(tile, step).wait_send()
        if tile < handed:
            a_copy(tile, 0).wait_send()
            a_copy(tile, 1).wait_send()
            t_copy(tile).wait_send()
        else:
            h_copy(tile).wait_send()
            b_copy(tile).wait_send()
    x_copy.wait_send()
    for step in range(1, n_seq):
        d_copy(step).wait_send()


def fused_body(upstream, queries, attention_out, keys_values, log_totals, neighbours):
    tokens, width = queries.shape[2:]
    heads, rows = keys_values.shape[2:4]
    tiles = heads // PER_TILE
    n_seq = lax.axis_size("seq")
    span = REACH * BLK
    handed = tiles // 2
    blocks_pad = 8 * -(-(rows // BLK) // 8)
    bf16, f32 = jnp.bfloat16, jnp.float32
    vmem = pl.BlockSpec(memory_space=pltpu.VMEM)
    pinned = pl.BlockSpec(memory_space=pltpu.HBM)
    dma = pltpu.SemaphoreType.DMA
    query_turned, cache_grad = pl.pallas_call(
        fused_kernel,
        out_shape=(
            jax.ShapeDtypeStruct((heads, HD, rows), bf16),
            jax.ShapeDtypeStruct((heads, rows, 2 * HD), bf16),
        ),
        in_specs=[pinned] * 6,
        out_specs=(vmem, vmem),
        scratch_shapes=[
            pltpu.SMEM((NBR, neighbours.shape[0]), jnp.int32),
            pltpu.VMEM((heads, rows), f32),
            pltpu.VMEM((tokens, width), bf16),
            pltpu.VMEM((tokens, width), bf16),
            pltpu.VMEM((heads, rows, 2 * HD), bf16),
            pltpu.VMEM((heads, span, 2 * HD), bf16),
            pltpu.VMEM((tiles, rows, LANES), bf16),
            pltpu.VMEM((tiles, rows, LANES), bf16),
            pltpu.VMEM((n_seq, heads, LANES), f32),
            pltpu.VMEM((n_seq, heads, LANES), f32),
            pltpu.VMEM((heads, HD, rows), f32),
            pltpu.VMEM((heads, rows, 2 * HD), f32),
            pltpu.VMEM((heads, span, 2 * HD), bf16),
            pltpu.VMEM((heads, span, 2 * HD), bf16),
            pltpu.VMEM((blocks_pad, rows), f32),
            pltpu.VMEM((8, rows), f32),
            pltpu.VMEM((8, rows), f32),
            pltpu.VMEM((2, heads, rows), f32),
            pltpu.VMEM((2, heads, rows), f32),
            pltpu.VMEM((PER_TILE, 2, rows, LANES), bf16),
            pltpu.VMEM((PER_TILE, 2, span, LANES), bf16),
            pltpu.VMEM((handed, span, LANES), bf16),
            pltpu.VMEM((handed, span, LANES), bf16),
            pltpu.VMEM((handed * PER_TILE, HD, span), bf16),
            pltpu.VMEM((handed * PER_TILE, HD, span), bf16),
            dma((tiles, n_seq)),
            dma((tiles, n_seq)),
            dma((tiles, n_seq - 1)),
            dma((tiles, n_seq - 1)),
            dma((tiles, n_seq - 1)),
            dma((tiles, n_seq - 1)),
            dma((n_seq - 1,)),
            dma((n_seq - 1,)),
            dma((tiles,)),
            dma((tiles,)),
            dma((tiles,)),
            dma((tiles,)),
            dma((handed, 2)),
            dma((handed, 2)),
            dma((handed,)),
            dma((handed,)),
            dma((1,)),
            dma((1,)),
            dma((4 + tiles,)),
        ],
        compiler_params=pltpu.CompilerParams(
            collective_id=0, has_side_effects=True, vmem_limit_bytes=48 * 1024 * 1024
        ),
    )(
        *[
            pltpu.with_memory_space_constraint(operand, pltpu.HBM)
            for operand in (
                jnp.transpose(neighbours),
                log_totals.reshape(heads, rows),
                upstream.reshape(tokens, width),
                queries.reshape(tokens, width),
                attention_out.reshape(tokens, width),
                keys_values.reshape(heads, rows, 2 * HD),
            )
        ]
    )
    query_grad = jnp.transpose(query_turned, (0, 2, 1)).reshape(1, 1, heads, rows, HD)
    return query_grad, cache_grad.reshape(1, 1, heads, rows, 2 * HD)


def body(upstream, queries, attention_out, keys_values, log_totals, neighbours):
    tokens = queries.shape[2]
    heads, rows = keys_values.shape[2:4]
    fits = (
        lax.axis_size("tp") == 2
        and lax.axis_size("pipe") > 1
        and lax.axis_size("seq") > 1
        and heads == 8
        and tokens % 16 == 0
        and tokens <= LANES
        and rows % LANES == 0
        and REACH * BLK < rows <= 512
    )
    chosen = fused_body if fits else general_body
    return chosen(upstream, queries, attention_out, keys_values, log_totals, neighbours)


def solution(mesh):
    placed = (
        P("pipe", "tp", "seq", None),
        P("pipe", "tp", "seq", None),
        P("pipe", "tp", "seq", None),
        P("pipe", "tp", "seq", None, None),
        P("pipe", "tp", "seq", None),
        P(),
    )
    return jax.shard_map(
        body,
        mesh=mesh,
        in_specs=placed,
        out_specs=(P("pipe", "tp", "seq", None, None), P("pipe", "tp", "seq", None, None)),
        check_vma=False,
    )
```

```python
import jax
import jax.numpy as jnp
from jax import lax
from jax.experimental import pallas as pl
from jax.experimental.pallas import tpu as pltpu
from jax.sharding import PartitionSpec as P

H = 32
HD = 64
BLK = 64
REACH = 4
NBR = 7


pair_group = 32


def passed_along(value, axis, steps):
    count = lax.axis_size(axis)
    pairs = [(source, (source + steps) % count) for source in range(count)]
    return lax.ppermute(value, axis, pairs)


def padded_2(cells, sides, width):
    for axis, dim in sides:
        count = lax.axis_size(axis)
        ends = count - 1
        head = lax.slice_in_dim(cells, 0, width, axis=dim)
        tail = lax.slice_in_dim(cells, cells.shape[dim] - width, cells.shape[dim], axis=dim)
        cells = jnp.concatenate(
            [
                lax.ppermute(tail, axis, [(i, (i + 1) % count) for i in range(ends)]),
                cells,
                lax.ppermute(head, axis, [((i + 1) % count, i) for i in range(ends)]),
            ],
            axis=dim,
        )
    return cells


def block_layout(values, blocks_here):
    heads_here = values.shape[1]
    turned = jnp.transpose(values, (1, 0, 2))
    return turned.reshape(heads_here, blocks_here, BLK, values.shape[2])


def general_body(upstream, queries, attention_out, keys_values, log_totals, neighbours):
    tokens_here = queries.shape[2]
    inv_root = HD ** (-0.5)
    incoming = passed_along(upstream, "pipe", -1)
    query_tok = queries.reshape(tokens_here, H, HD)
    grad_tok = incoming.reshape(tokens_here, H, HD)
    out_tok = attention_out.reshape(tokens_here, H, HD)
    packed = jnp.concatenate([query_tok, grad_tok, out_tok], axis=2)
    regrouped = lax.all_to_all(packed, "seq", split_axis=1, concat_axis=0, tiled=True)
    query_heads = regrouped[:, :, :HD]
    grad_heads = regrouped[:, :, HD : 2 * HD]
    out_heads = regrouped[:, :, 2 * HD :]
    row_delta = jnp.sum(grad_heads.astype(jnp.float32) * out_heads.astype(jnp.float32), axis=2)
    rows_here = query_heads.shape[0]
    heads_here = query_heads.shape[1]
    blocks_here = rows_here // BLK
    query_blocks = block_layout(query_heads, blocks_here)
    grad_blocks = block_layout(grad_heads, blocks_here)
    delta_blocks = jnp.transpose(row_delta).reshape(heads_here, blocks_here, BLK)
    norm_blocks = log_totals.reshape(heads_here, blocks_here, BLK)
    cache_blocks = keys_values.reshape(heads_here, blocks_here, BLK, 2 * HD)
    padded = padded_2(cache_blocks, (("tp", 1),), REACH)
    first_block = lax.axis_index("tp") * blocks_here
    listed = lax.dynamic_slice_in_dim(neighbours, first_block, blocks_here, 0)
    present = (listed >= 0).reshape(-1)
    slot_count = blocks_here * NBR
    group_total = (slot_count + pair_group - 1) // pair_group
    capacity = group_total * pair_group
    running = jnp.cumsum(present.astype(jnp.int32)) - 1
    pair_count = jnp.sum(present.astype(jnp.int32))
    target = jnp.where(present, running, capacity)
    query_source = jnp.repeat(jnp.arange(blocks_here, dtype=jnp.int32), NBR)
    key_source = (listed - first_block + REACH).reshape(-1)
    pair_query = jnp.zeros((capacity,), jnp.int32).at[target].set(query_source, mode="drop")
    pair_key = jnp.zeros((capacity,), jnp.int32).at[target].set(key_source, mode="drop")

    def one_group(group_step, totals):
        query_acc, cache_acc = totals
        first_pair = group_step * pair_group
        query_pick = lax.dynamic_slice_in_dim(pair_query, first_pair, pair_group)
        key_pick = lax.dynamic_slice_in_dim(pair_key, first_pair, pair_group)
        live_mask = (first_pair + jnp.arange(pair_group) < pair_count).astype(jnp.float32)
        query_rows = query_blocks[:, query_pick]
        grad_rows = grad_blocks[:, query_pick]
        norm_rows = norm_blocks[:, query_pick]
        delta_rows = delta_blocks[:, query_pick]
        cache_rows = padded[:, key_pick]
        key_rows = cache_rows[..., :HD]
        value_rows = cache_rows[..., HD:]
        scores = (
            jnp.einsum("hgqd,hgkd->hgqk", query_rows, key_rows, preferred_element_type=jnp.float32)
            * inv_root
        )
        weights = jnp.exp(scores - norm_rows[..., None]) * live_mask[None, :, None, None]
        weights_half = weights.astype(jnp.bfloat16)
        grad_weights = jnp.einsum(
            "hgqd,hgkd->hgqk", grad_rows, value_rows, preferred_element_type=jnp.float32
        )
        grad_scores = (weights * (grad_weights - delta_rows[..., None])).astype(jnp.bfloat16)
        query_part = (
            jnp.einsum("hgqk,hgkd->hgqd", grad_scores, key_rows, preferred_element_type=jnp.float32)
            * inv_root
        )
        key_part = (
            jnp.einsum(
                "hgqk,hgqd->hgkd", grad_scores, query_rows, preferred_element_type=jnp.float32
            )
            * inv_root
        )
        value_part = jnp.einsum(
            "hgqk,hgqd->hgkd", weights_half, grad_rows, preferred_element_type=jnp.float32
        )
        query_acc = query_acc.at[:, query_pick].add(query_part)
        cache_acc = cache_acc.at[:, key_pick].add(jnp.concatenate([key_part, value_part], axis=-1))
        return (query_acc, cache_acc)

    group_live = (pair_count + pair_group - 1) // pair_group
    query_start = jnp.zeros((heads_here, blocks_here, BLK, HD), jnp.float32)
    cache_start = jnp.zeros((heads_here, blocks_here + 2 * REACH, BLK, 2 * HD), jnp.float32)
    query_acc, cache_acc = lax.fori_loop(0, group_live, one_group, (query_start, cache_start))
    rim_terms = jnp.concatenate([cache_acc[:, :REACH], cache_acc[:, REACH + blocks_here :]], axis=1)
    arrived = padded_2(rim_terms.astype(jnp.bfloat16), (("tp", 1),), REACH).astype(rim_terms.dtype)
    own_part = cache_acc[:, REACH : REACH + blocks_here]
    own_part = own_part.at[:, :REACH].add(arrived[:, :REACH])
    own_part = own_part.at[:, blocks_here - REACH :].add(arrived[:, 3 * REACH :])
    query_grad = query_acc.reshape(1, 1, heads_here, rows_here, HD).astype(jnp.bfloat16)
    cache_grad = own_part.reshape(1, 1, heads_here, rows_here, 2 * HD).astype(jnp.bfloat16)
    return (query_grad, cache_grad)


MESH = pl.DeviceIdType.MESH
LANES = 128
PER_TILE = LANES // HD
ABSENT = -1e30
NT = (((1,), (1,)), ((), ()))
TN = (((0,), (0,)), ((), ()))


def dot_f32(left, right, dims=(((1,), (0,)), ((), ()))):
    return lax.dot_general(left, right, dims, preferred_element_type=jnp.float32)


def listed_bias(neigh_ref, first_row, first_key, key_rows, blocks_here):
    lane = lax.broadcasted_iota(jnp.int32, (key_rows, LANES), 1)
    key = lax.broadcasted_iota(jnp.int32, (key_rows, LANES), 0) + first_key
    tiles = []
    for pair in range(blocks_here // 2):
        found = None
        for slot in range(NBR):
            here = jnp.where(
                lane < BLK,
                neigh_ref[slot, first_row + 2 * pair],
                neigh_ref[slot, first_row + 2 * pair + 1],
            )
            hit = (key == here).astype(jnp.float32)
            found = hit if found is None else jnp.maximum(found, hit)
        tiles.append((found - 1.0) * -ABSENT)
    return jnp.concatenate(tiles, axis=1)


def fused_kernel(
    neigh_hbm, norm_hbm, up_ref, query_ref, out_ref, cache_ref, dq_ref, dkv_ref,
    neigh_ref, norm_ref, inc, outs, kv, halo, qbuf, gbuf, dsend, dgot, acc, acc_kv, back_out, back_in, bias_own, bias_halo, rows_aux, joint,
    up_send, up_recv, q_send, q_recv, g_send, g_recv, d_send, d_recv, h_send, h_recv, b_send, b_recv, local_sem,
):
    n_pipe, n_seq = lax.axis_size("pipe"), lax.axis_size("seq")
    pipe, seq, tp = lax.axis_index("pipe"), lax.axis_index("seq"), lax.axis_index("tp")
    tokens, width = inc.shape
    heads, rows, _ = kv.shape
    tiles = heads // PER_TILE
    span = REACH * BLK
    blocks_here = rows // BLK
    share = heads * HD
    below, above = lax.rem(pipe + n_pipe - 1, n_pipe), lax.rem(pipe + 1, n_pipe)
    mate = 1 - tp
    window = pl.multiple_of(mate * (rows - span), LANES)
    mine = pl.multiple_of(seq * tokens, 16)

    def peer(step):
        return lax.rem(seq + step, n_seq)

    def tile_cols(dest, tile):
        return pl.ds(pl.multiple_of(dest * share + tile * LANES, LANES), LANES)

    def up_copy(tile, dest):
        cols = pl.ds(dest * share + tile * LANES, LANES)
        return pltpu.make_async_remote_copy(
            src_ref=up_ref.at[:, cols], dst_ref=inc.at[:, cols],
            send_sem=up_send.at[tile, dest], recv_sem=up_recv.at[tile, dest],
            device_id={"pipe": below}, device_id_type=MESH,
        )

    def q_copy(tile, step):
        return pltpu.make_async_remote_copy(
            src_ref=query_ref.at[:, tile_cols(peer(step), tile)],
            dst_ref=qbuf.at[tile, pl.ds(mine, tokens), :],
            send_sem=q_send.at[tile, step - 1], recv_sem=q_recv.at[tile, step - 1],
            device_id={"seq": peer(step)}, device_id_type=MESH,
        )

    def g_copy(tile, step):
        return pltpu.make_async_remote_copy(
            src_ref=inc.at[:, tile_cols(peer(step), tile)],
            dst_ref=gbuf.at[tile, pl.ds(mine, tokens), :],
            send_sem=g_send.at[tile, step - 1], recv_sem=g_recv.at[tile, step - 1],
            device_id={"seq": peer(step)}, device_id_type=MESH,
        )

    def d_copy(step):
        return pltpu.make_async_remote_copy(
            src_ref=dsend.at[peer(step)], dst_ref=dgot.at[seq],
            send_sem=d_send.at[step - 1], recv_sem=d_recv.at[step - 1],
            device_id={"seq": peer(step)}, device_id_type=MESH,
        )

    def h_copy(tile):
        pair = pl.ds(tile * PER_TILE, PER_TILE)
        return pltpu.make_async_remote_copy(
            src_ref=cache_ref.at[pair, pl.ds(window, span), :], dst_ref=halo.at[pair],
            send_sem=h_send.at[tile], recv_sem=h_recv.at[tile],
            device_id={"tp": mate}, device_id_type=MESH,
        )

    def b_copy(tile):
        pair = pl.ds(tile * PER_TILE, PER_TILE)
        return pltpu.make_async_remote_copy(
            src_ref=back_out.at[pair], dst_ref=back_in.at[pair],
            send_sem=b_send.at[tile], recv_sem=b_recv.at[tile],
            device_id={"tp": mate}, device_id_type=MESH,
        )

    out_local = pltpu.make_async_copy(out_ref, outs, local_sem.at[0])
    kv_local = pltpu.make_async_copy(cache_ref, kv, local_sem.at[1])
    q_local = [
        pltpu.make_async_copy(
            query_ref.at[:, tile_cols(seq, tile)], qbuf.at[tile, pl.ds(mine, tokens), :], local_sem.at[2 + tile]
        )
        for tile in range(tiles)
    ]
    neigh_local = pltpu.make_async_copy(neigh_hbm, neigh_ref, local_sem.at[2 + tiles])
    norm_local = pltpu.make_async_copy(norm_hbm, norm_ref, local_sem.at[3 + tiles])
    neigh_local.start()
    norm_local.start()
    out_local.start()
    kv_local.start()
    for copy in q_local:
        copy.start()

    barrier = pltpu.get_barrier_semaphore()
    pl.semaphore_signal(barrier, inc=1, device_id={"pipe": above}, device_id_type=MESH)
    pl.semaphore_signal(barrier, inc=1, device_id={"tp": mate}, device_id_type=MESH)
    for step in range(1, n_seq):
        pl.semaphore_signal(barrier, inc=1, device_id={"seq": peer(step)}, device_id_type=MESH)
    pl.semaphore_wait(barrier, n_seq + 1)

    def send_up(tile):
        for dest in range(n_seq):
            up_copy(tile, dest).start()

    def send_q(tile):
        for step in range(1, n_seq):
            q_copy(tile, step).start()

    def send_g(tile):
        for step in range(1, n_seq):
            g_copy(tile, step).start()

    send_up(0)
    send_q(0)
    h_copy(0).start()
    send_up(1)

    neigh_local.wait()
    first_row = tp * blocks_here
    halo_key = mate * blocks_here + tp * (blocks_here - REACH)
    bias_own[...] = listed_bias(neigh_ref, first_row, first_row, bias_own.shape[0], blocks_here)
    bias_halo[...] = listed_bias(neigh_ref, first_row, halo_key, bias_halo.shape[0], blocks_here)

    for tile in range(tiles):
        for dest in range(n_seq):
            up_copy(tile, dest).wait_recv()
        if tile + 2 < tiles:
            send_up(tile + 2)
        if tile < 2:
            send_g(tile)
        if tile == 0:
            send_q(1)
            h_copy(1).start()

    out_local.wait()
    picks = (
        lax.broadcasted_iota(jnp.int32, (heads, share), 1) // HD
        == lax.broadcasted_iota(jnp.int32, (heads, share), 0)
    ).astype(jnp.bfloat16)
    dsend[...] = jnp.zeros_like(dsend)
    for dest in range(n_seq):
        cols = pl.ds(dest * share, share)
        terms = inc[:, cols].astype(jnp.float32) * outs[:, cols].astype(jnp.float32)
        high = terms.astype(jnp.bfloat16)
        low = (terms - high.astype(jnp.float32)).astype(jnp.bfloat16)
        dsend[dest, :, :tokens] = dot_f32(picks, high, NT) + dot_f32(picks, low, NT)
    for step in range(1, n_seq):
        d_copy(step).start()
    dgot[seq] = dsend[seq]
    for tile in range(tiles):
        gbuf[tile, pl.ds(mine, tokens), :] = inc[:, tile_cols(seq, tile)]
    kv_local.wait()
    for copy in q_local:
        copy.wait()
    for step in range(1, n_seq):
        d_copy(step).wait_recv()
    delta = None
    for source in range(n_seq):
        part = jnp.concatenate([dgot[source], jnp.zeros((heads, rows - LANES), jnp.float32)], axis=1)
        if source:
            part = pltpu.roll(part, source * tokens, 1)
        delta = part if delta is None else delta + part
    norm_local.wait()
    norm = norm_ref[...]
    for head in range(heads):
        rows_aux[head, 0:1, :] = norm[head : head + 1]
        rows_aux[head, 1:2, :] = delta[head : head + 1]

    inv_root = HD ** (-0.5)
    key_lane = lax.broadcasted_iota(jnp.int32, (1, 2 * HD), 1) < HD
    lane_scale = jnp.where(key_lane, inv_root, 1.0)
    lane_scale_half = lane_scale.astype(jnp.bfloat16)

    def block_terms(cache_rows, both_rows, bias, norm_row, delta_row):
        count, width_here = cache_rows.shape[0] // BLK, delta_row.shape[1]
        scaled = cache_rows * lane_scale_half
        products = dot_f32(scaled, both_rows, NT)
        scores = products[:, :width_here].reshape(count, BLK, width_here)
        shift = bias[:count] - norm_row
        weights = jnp.exp(scores + shift[:, None, :]).reshape(count * BLK, width_here)
        grad_scores = (weights * (products[:, width_here:] - delta_row)).astype(jnp.bfloat16)
        joined = jnp.concatenate([grad_scores, weights.astype(jnp.bfloat16)], axis=1)
        cache_part = dot_f32(joined, both_rows) * lane_scale
        query_part = dot_f32(scaled[:, :HD], grad_scores, TN)
        return query_part, cache_part

    def finish(tile):
        b_copy(tile).wait_recv()
        for inner in range(PER_TILE):
            head = tile * PER_TILE + inner
            acc_kv[head, pl.ds(window, span), :] += back_in[head].astype(jnp.float32)
            dkv_ref[head] = acc_kv[head].astype(jnp.bfloat16)

    def one_tile(tile, carry):
        for step in range(1, n_seq):
            q_copy(tile, step).wait_recv()
            g_copy(tile, step).wait_recv()

        @pl.when(tile + 2 < tiles)
        def _():
            send_q(tile + 2)
            send_g(tile + 2)
            h_copy(tile + 2).start()

        blank = jnp.zeros((rows, HD), jnp.bfloat16)
        for inner in range(PER_TILE):
            lanes = slice(inner * HD, (inner + 1) * HD)
            joint[inner, 0] = jnp.concatenate([qbuf[tile, :, lanes], blank], axis=1)
            joint[inner, 1] = jnp.concatenate([blank, gbuf[tile, :, lanes]], axis=1)
        h_copy(tile).wait_recv()
        for inner in range(PER_TILE):
            head = tile * PER_TILE + inner
            query_part, cache_part = block_terms(
                halo[head],
                joint[inner, :, pl.ds(window, span), :].reshape(2 * span, LANES),
                bias_halo[:, pl.ds(window, span)],
                rows_aux[head, 0:1, pl.ds(window, span)],
                rows_aux[head, 1:2, pl.ds(window, span)],
            )
            back_out[head] = cache_part.astype(jnp.bfloat16)
            acc[head, :, pl.ds(window, span)] = query_part
            acc[head, :, pl.ds(pl.multiple_of(tp * span, LANES), rows - span)] = jnp.zeros(
                (HD, rows - span), jnp.float32
            )
        b_copy(tile).start()
        for inner in range(PER_TILE):
            head = tile * PER_TILE + inner
            query_part, cache_part = block_terms(
                kv[head],
                joint[inner].reshape(2 * rows, LANES),
                bias_own[...],
                rows_aux[head, 0:1, :],
                rows_aux[head, 1:2, :],
            )
            dq_ref[head] = (acc[head] + query_part).astype(jnp.bfloat16)
            acc_kv[head] = cache_part
        @pl.when(tile >= 2)
        def _():
            finish(tile - 2)

        return carry

    lax.fori_loop(0, tiles, one_tile, 0)
    finish(tiles - 2)
    finish(tiles - 1)

    for tile in range(tiles):
        for dest in range(n_seq):
            up_copy(tile, dest).wait_send()
        for step in range(1, n_seq):
            q_copy(tile, step).wait_send()
            g_copy(tile, step).wait_send()
        h_copy(tile).wait_send()
        b_copy(tile).wait_send()
    for step in range(1, n_seq):
        d_copy(step).wait_send()


def fused_body(upstream, queries, attention_out, keys_values, log_totals, neighbours):
    tokens, width = queries.shape[2:]
    heads, rows = keys_values.shape[2:4]
    tiles = heads // PER_TILE
    n_seq = lax.axis_size("seq")
    span = REACH * BLK
    blocks_pad = 8 * -(-(rows // BLK) // 8)
    bf16, f32 = jnp.bfloat16, jnp.float32
    vmem = pl.BlockSpec(memory_space=pltpu.VMEM)
    pinned = pl.BlockSpec(memory_space=pltpu.HBM)
    dma = pltpu.SemaphoreType.DMA
    query_turned, cache_grad = pl.pallas_call(
        fused_kernel,
        out_shape=(
            jax.ShapeDtypeStruct((heads, HD, rows), bf16),
            jax.ShapeDtypeStruct((heads, rows, 2 * HD), bf16),
        ),
        in_specs=[pinned] * 6,
        out_specs=(vmem, vmem),
        scratch_shapes=[
            pltpu.SMEM((NBR, neighbours.shape[0]), jnp.int32),
            pltpu.VMEM((heads, rows), f32),
            pltpu.VMEM((tokens, width), bf16),
            pltpu.VMEM((tokens, width), bf16),
            pltpu.VMEM((heads, rows, 2 * HD), bf16),
            pltpu.VMEM((heads, span, 2 * HD), bf16),
            pltpu.VMEM((tiles, rows, LANES), bf16),
            pltpu.VMEM((tiles, rows, LANES), bf16),
            pltpu.VMEM((n_seq, heads, LANES), f32),
            pltpu.VMEM((n_seq, heads, LANES), f32),
            pltpu.VMEM((heads, HD, rows), f32),
            pltpu.VMEM((heads, rows, 2 * HD), f32),
            pltpu.VMEM((heads, span, 2 * HD), bf16),
            pltpu.VMEM((heads, span, 2 * HD), bf16),
            pltpu.VMEM((blocks_pad, rows), f32),
            pltpu.VMEM((8, rows), f32),
            pltpu.VMEM((heads, 8, rows), f32),
            pltpu.VMEM((PER_TILE, 2, rows, LANES), bf16),
            dma((tiles, n_seq)),
            dma((tiles, n_seq)),
            dma((tiles, n_seq - 1)),
            dma((tiles, n_seq - 1)),
            dma((tiles, n_seq - 1)),
            dma((tiles, n_seq - 1)),
            dma((n_seq - 1,)),
            dma((n_seq - 1,)),
            dma((tiles,)),
            dma((tiles,)),
            dma((tiles,)),
            dma((tiles,)),
            dma((4 + tiles,)),
        ],
        compiler_params=pltpu.CompilerParams(
            collective_id=0, has_side_effects=True, vmem_limit_bytes=48 * 1024 * 1024
        ),
    )(
        *[
            pltpu.with_memory_space_constraint(operand, pltpu.HBM)
            for operand in (
                jnp.transpose(neighbours),
                log_totals.reshape(heads, rows),
                upstream.reshape(tokens, width),
                queries.reshape(tokens, width),
                attention_out.reshape(tokens, width),
                keys_values.reshape(heads, rows, 2 * HD),
            )
        ]
    )
    query_grad = jnp.transpose(query_turned, (0, 2, 1)).reshape(1, 1, heads, rows, HD)
    return query_grad, cache_grad.reshape(1, 1, heads, rows, 2 * HD)


def body(upstream, queries, attention_out, keys_values, log_totals, neighbours):
    tokens = queries.shape[2]
    heads, rows = keys_values.shape[2:4]
    fits = (
        lax.axis_size("tp") == 2
        and lax.axis_size("pipe") > 1
        and lax.axis_size("seq") > 1
        and heads == 8
        and tokens % 16 == 0
        and tokens <= LANES
        and rows % LANES == 0
        and REACH * BLK < rows <= 512
    )
    chosen = fused_body if fits else general_body
    return chosen(upstream, queries, attention_out, keys_values, log_totals, neighbours)


def solution(mesh):
    placed = (
        P("pipe", "tp", "seq", None),
        P("pipe", "tp", "seq", None),
        P("pipe", "tp", "seq", None),
        P("pipe", "tp", "seq", None, None),
        P("pipe", "tp", "seq", None),
        P(),
    )
    return jax.shard_map(
        body,
        mesh=mesh,
        in_specs=placed,
        out_specs=(P("pipe", "tp", "seq", None, None), P("pipe", "tp", "seq", None, None)),
        check_vma=False,
    )
```

```python
import jax
import jax.numpy as jnp
from jax import lax
from jax.experimental import pallas as pl
from jax.experimental.pallas import tpu as pltpu
from jax.sharding import PartitionSpec as P

H = 32
HD = 64
BLK = 64
REACH = 4
NBR = 7


pair_group = 32


def passed_along(value, axis, steps):
    count = lax.axis_size(axis)
    pairs = [(source, (source + steps) % count) for source in range(count)]
    return lax.ppermute(value, axis, pairs)


def padded_2(cells, sides, width):
    for axis, dim in sides:
        count = lax.axis_size(axis)
        ends = count - 1
        head = lax.slice_in_dim(cells, 0, width, axis=dim)
        tail = lax.slice_in_dim(cells, cells.shape[dim] - width, cells.shape[dim], axis=dim)
        cells = jnp.concatenate(
            [
                lax.ppermute(tail, axis, [(i, (i + 1) % count) for i in range(ends)]),
                cells,
                lax.ppermute(head, axis, [((i + 1) % count, i) for i in range(ends)]),
            ],
            axis=dim,
        )
    return cells


def block_layout(values, blocks_here):
    heads_here = values.shape[1]
    turned = jnp.transpose(values, (1, 0, 2))
    return turned.reshape(heads_here, blocks_here, BLK, values.shape[2])


def general_body(upstream, queries, attention_out, keys_values, log_totals, neighbours):
    tokens_here = queries.shape[2]
    inv_root = HD ** (-0.5)
    incoming = passed_along(upstream, "pipe", -1)
    query_tok = queries.reshape(tokens_here, H, HD)
    grad_tok = incoming.reshape(tokens_here, H, HD)
    out_tok = attention_out.reshape(tokens_here, H, HD)
    packed = jnp.concatenate([query_tok, grad_tok, out_tok], axis=2)
    regrouped = lax.all_to_all(packed, "seq", split_axis=1, concat_axis=0, tiled=True)
    query_heads = regrouped[:, :, :HD]
    grad_heads = regrouped[:, :, HD : 2 * HD]
    out_heads = regrouped[:, :, 2 * HD :]
    row_delta = jnp.sum(grad_heads.astype(jnp.float32) * out_heads.astype(jnp.float32), axis=2)
    rows_here = query_heads.shape[0]
    heads_here = query_heads.shape[1]
    blocks_here = rows_here // BLK
    query_blocks = block_layout(query_heads, blocks_here)
    grad_blocks = block_layout(grad_heads, blocks_here)
    delta_blocks = jnp.transpose(row_delta).reshape(heads_here, blocks_here, BLK)
    norm_blocks = log_totals.reshape(heads_here, blocks_here, BLK)
    cache_blocks = keys_values.reshape(heads_here, blocks_here, BLK, 2 * HD)
    padded = padded_2(cache_blocks, (("tp", 1),), REACH)
    first_block = lax.axis_index("tp") * blocks_here
    listed = lax.dynamic_slice_in_dim(neighbours, first_block, blocks_here, 0)
    present = (listed >= 0).reshape(-1)
    slot_count = blocks_here * NBR
    group_total = (slot_count + pair_group - 1) // pair_group
    capacity = group_total * pair_group
    running = jnp.cumsum(present.astype(jnp.int32)) - 1
    pair_count = jnp.sum(present.astype(jnp.int32))
    target = jnp.where(present, running, capacity)
    query_source = jnp.repeat(jnp.arange(blocks_here, dtype=jnp.int32), NBR)
    key_source = (listed - first_block + REACH).reshape(-1)
    pair_query = jnp.zeros((capacity,), jnp.int32).at[target].set(query_source, mode="drop")
    pair_key = jnp.zeros((capacity,), jnp.int32).at[target].set(key_source, mode="drop")

    def one_group(group_step, totals):
        query_acc, cache_acc = totals
        first_pair = group_step * pair_group
        query_pick = lax.dynamic_slice_in_dim(pair_query, first_pair, pair_group)
        key_pick = lax.dynamic_slice_in_dim(pair_key, first_pair, pair_group)
        live_mask = (first_pair + jnp.arange(pair_group) < pair_count).astype(jnp.float32)
        query_rows = query_blocks[:, query_pick]
        grad_rows = grad_blocks[:, query_pick]
        norm_rows = norm_blocks[:, query_pick]
        delta_rows = delta_blocks[:, query_pick]
        cache_rows = padded[:, key_pick]
        key_rows = cache_rows[..., :HD]
        value_rows = cache_rows[..., HD:]
        scores = (
            jnp.einsum("hgqd,hgkd->hgqk", query_rows, key_rows, preferred_element_type=jnp.float32)
            * inv_root
        )
        weights = jnp.exp(scores - norm_rows[..., None]) * live_mask[None, :, None, None]
        weights_half = weights.astype(jnp.bfloat16)
        grad_weights = jnp.einsum(
            "hgqd,hgkd->hgqk", grad_rows, value_rows, preferred_element_type=jnp.float32
        )
        grad_scores = (weights * (grad_weights - delta_rows[..., None])).astype(jnp.bfloat16)
        query_part = (
            jnp.einsum("hgqk,hgkd->hgqd", grad_scores, key_rows, preferred_element_type=jnp.float32)
            * inv_root
        )
        key_part = (
            jnp.einsum(
                "hgqk,hgqd->hgkd", grad_scores, query_rows, preferred_element_type=jnp.float32
            )
            * inv_root
        )
        value_part = jnp.einsum(
            "hgqk,hgqd->hgkd", weights_half, grad_rows, preferred_element_type=jnp.float32
        )
        query_acc = query_acc.at[:, query_pick].add(query_part)
        cache_acc = cache_acc.at[:, key_pick].add(jnp.concatenate([key_part, value_part], axis=-1))
        return (query_acc, cache_acc)

    group_live = (pair_count + pair_group - 1) // pair_group
    query_start = jnp.zeros((heads_here, blocks_here, BLK, HD), jnp.float32)
    cache_start = jnp.zeros((heads_here, blocks_here + 2 * REACH, BLK, 2 * HD), jnp.float32)
    query_acc, cache_acc = lax.fori_loop(0, group_live, one_group, (query_start, cache_start))
    rim_terms = jnp.concatenate([cache_acc[:, :REACH], cache_acc[:, REACH + blocks_here :]], axis=1)
    arrived = padded_2(rim_terms.astype(jnp.bfloat16), (("tp", 1),), REACH).astype(rim_terms.dtype)
    own_part = cache_acc[:, REACH : REACH + blocks_here]
    own_part = own_part.at[:, :REACH].add(arrived[:, :REACH])
    own_part = own_part.at[:, blocks_here - REACH :].add(arrived[:, 3 * REACH :])
    query_grad = query_acc.reshape(1, 1, heads_here, rows_here, HD).astype(jnp.bfloat16)
    cache_grad = own_part.reshape(1, 1, heads_here, rows_here, 2 * HD).astype(jnp.bfloat16)
    return (query_grad, cache_grad)


MESH = pl.DeviceIdType.MESH
LANES = 128
PER_TILE = LANES // HD
ABSENT = -1e30
NT = (((1,), (1,)), ((), ()))


def dot_f32(left, right, dims=(((1,), (0,)), ((), ()))):
    return lax.dot_general(left, right, dims, preferred_element_type=jnp.float32)


def listed_bias(neigh_ref, first_row, first_key, key_rows, blocks_here):
    lane = lax.broadcasted_iota(jnp.int32, (key_rows, LANES), 1)
    key = lax.broadcasted_iota(jnp.int32, (key_rows, LANES), 0) + first_key
    tiles = []
    for pair in range(blocks_here // 2):
        found = None
        for slot in range(NBR):
            here = jnp.where(
                lane < BLK,
                neigh_ref[slot, first_row + 2 * pair],
                neigh_ref[slot, first_row + 2 * pair + 1],
            )
            hit = (key == here).astype(jnp.float32)
            found = hit if found is None else jnp.maximum(found, hit)
        tiles.append((found - 1.0) * -ABSENT)
    return jnp.concatenate(tiles, axis=1)


def fused_kernel(
    neigh_hbm, norm_hbm, up_ref, query_ref, out_ref, cache_ref, dq_ref, dkv_ref,
    neigh_ref, norm_ref, inc, outs, kv, halo, qbuf, gbuf, dsend, dgot, acc, acc_kv, back_out, back_in, bias_own, bias_halo, rows_aux, joint, turned, key_turned,
    up_send, up_recv, q_send, q_recv, g_send, g_recv, d_send, d_recv, h_send, h_recv, b_send, b_recv, local_sem,
):
    n_pipe, n_seq = lax.axis_size("pipe"), lax.axis_size("seq")
    pipe, seq, tp = lax.axis_index("pipe"), lax.axis_index("seq"), lax.axis_index("tp")
    tokens, width = inc.shape
    heads, rows, _ = kv.shape
    tiles = heads // PER_TILE
    span = REACH * BLK
    blocks_here = rows // BLK
    share = heads * HD
    below, above = lax.rem(pipe + n_pipe - 1, n_pipe), lax.rem(pipe + 1, n_pipe)
    mate = 1 - tp
    window = pl.multiple_of(mate * (rows - span), LANES)
    far_window = pl.multiple_of(rows + mate * (rows - span), LANES)
    mine = pl.multiple_of(seq * tokens, 16)

    def peer(step):
        return lax.rem(seq + step, n_seq)

    def tile_cols(dest, tile):
        return pl.ds(pl.multiple_of(dest * share + tile * LANES, LANES), LANES)

    def up_copy(tile, dest):
        cols = pl.ds(dest * share + tile * LANES, LANES)
        return pltpu.make_async_remote_copy(
            src_ref=up_ref.at[:, cols], dst_ref=inc.at[:, cols],
            send_sem=up_send.at[tile, dest], recv_sem=up_recv.at[tile, dest],
            device_id={"pipe": below}, device_id_type=MESH,
        )

    def q_copy(tile, step):
        return pltpu.make_async_remote_copy(
            src_ref=query_ref.at[:, tile_cols(peer(step), tile)],
            dst_ref=qbuf.at[tile, pl.ds(mine, tokens), :],
            send_sem=q_send.at[tile, step - 1], recv_sem=q_recv.at[tile, step - 1],
            device_id={"seq": peer(step)}, device_id_type=MESH,
        )

    def g_copy(tile, step):
        return pltpu.make_async_remote_copy(
            src_ref=inc.at[:, tile_cols(peer(step), tile)],
            dst_ref=gbuf.at[tile, pl.ds(mine, tokens), :],
            send_sem=g_send.at[tile, step - 1], recv_sem=g_recv.at[tile, step - 1],
            device_id={"seq": peer(step)}, device_id_type=MESH,
        )

    def d_copy(step):
        return pltpu.make_async_remote_copy(
            src_ref=dsend.at[peer(step)], dst_ref=dgot.at[seq],
            send_sem=d_send.at[step - 1], recv_sem=d_recv.at[step - 1],
            device_id={"seq": peer(step)}, device_id_type=MESH,
        )

    def h_copy(tile):
        pair = pl.ds(tile * PER_TILE, PER_TILE)
        return pltpu.make_async_remote_copy(
            src_ref=cache_ref.at[pair, pl.ds(window, span), :], dst_ref=halo.at[pair],
            send_sem=h_send.at[tile], recv_sem=h_recv.at[tile],
            device_id={"tp": mate}, device_id_type=MESH,
        )

    def b_copy(tile):
        pair = pl.ds(tile * PER_TILE, PER_TILE)
        return pltpu.make_async_remote_copy(
            src_ref=back_out.at[pair], dst_ref=back_in.at[pair],
            send_sem=b_send.at[tile], recv_sem=b_recv.at[tile],
            device_id={"tp": mate}, device_id_type=MESH,
        )

    out_local = pltpu.make_async_copy(out_ref, outs, local_sem.at[0])
    kv_local = pltpu.make_async_copy(cache_ref, kv, local_sem.at[1])
    q_local = [
        pltpu.make_async_copy(
            query_ref.at[:, tile_cols(seq, tile)], qbuf.at[tile, pl.ds(mine, tokens), :], local_sem.at[2 + tile]
        )
        for tile in range(tiles)
    ]
    neigh_local = pltpu.make_async_copy(neigh_hbm, neigh_ref, local_sem.at[2 + tiles])
    norm_local = pltpu.make_async_copy(norm_hbm, norm_ref, local_sem.at[3 + tiles])
    neigh_local.start()
    norm_local.start()
    out_local.start()
    kv_local.start()
    for copy in q_local:
        copy.start()

    barrier = pltpu.get_barrier_semaphore()
    pl.semaphore_signal(barrier, inc=1, device_id={"pipe": above}, device_id_type=MESH)
    pl.semaphore_signal(barrier, inc=1, device_id={"tp": mate}, device_id_type=MESH)
    for step in range(1, n_seq):
        pl.semaphore_signal(barrier, inc=1, device_id={"seq": peer(step)}, device_id_type=MESH)
    pl.semaphore_wait(barrier, n_seq + 1)

    def send_up(tile):
        for dest in range(n_seq):
            up_copy(tile, dest).start()

    def send_q(tile):
        for step in range(1, n_seq):
            q_copy(tile, step).start()

    def send_g(tile):
        for step in range(1, n_seq):
            g_copy(tile, step).start()

    send_up(0)
    send_q(0)
    h_copy(0).start()
    send_up(1)

    neigh_local.wait()
    first_row = tp * blocks_here
    halo_key = mate * blocks_here + tp * (blocks_here - REACH)
    bias_own[...] = listed_bias(neigh_ref, first_row, first_row, bias_own.shape[0], blocks_here)
    bias_halo[...] = listed_bias(neigh_ref, first_row, halo_key, bias_halo.shape[0], blocks_here)

    inv_root = HD ** (-0.5)
    key_lane = lax.broadcasted_iota(jnp.int32, (1, 2 * HD), 1) < HD
    lane_scale = jnp.where(key_lane, inv_root, 1.0)
    lane_scale_half = lane_scale.astype(jnp.bfloat16)

    def prepare(head, carry):
        scaled = kv[head] * lane_scale_half
        kv[head] = scaled
        key_turned[head] = jnp.transpose(scaled)[:HD]
        return carry

    for tile in range(tiles):
        for dest in range(n_seq):
            up_copy(tile, dest).wait_recv()
        if tile + 2 < tiles:
            send_up(tile + 2)
        if tile < 2:
            send_g(tile)
        if tile == 0:
            send_q(1)
            h_copy(1).start()
        if tile == 1:
            turned[...] = jnp.zeros_like(turned)
            kv_local.wait()
            lax.fori_loop(0, heads, prepare, 0)

    out_local.wait()
    picks = (
        lax.broadcasted_iota(jnp.int32, (heads, share), 1) // HD
        == lax.broadcasted_iota(jnp.int32, (heads, share), 0)
    ).astype(jnp.bfloat16)
    dsend[...] = jnp.zeros_like(dsend)
    for dest in range(n_seq):
        cols = pl.ds(dest * share, share)
        terms = inc[:, cols].astype(jnp.float32) * outs[:, cols].astype(jnp.float32)
        high = terms.astype(jnp.bfloat16)
        low = (terms - high.astype(jnp.float32)).astype(jnp.bfloat16)
        dsend[dest, :, :tokens] = dot_f32(picks, high, NT) + dot_f32(picks, low, NT)
    for step in range(1, n_seq):
        d_copy(step).start()
    dgot[seq] = dsend[seq]
    for tile in range(tiles):
        gbuf[tile, pl.ds(mine, tokens), :] = inc[:, tile_cols(seq, tile)]
    for copy in q_local:
        copy.wait()
    for step in range(1, n_seq):
        d_copy(step).wait_recv()
    delta = None
    for source in range(n_seq):
        part = jnp.concatenate([dgot[source], jnp.zeros((heads, rows - LANES), jnp.float32)], axis=1)
        if source:
            part = pltpu.roll(part, source * tokens, 1)
        delta = part if delta is None else delta + part
    norm_local.wait()
    norm = norm_ref[...]
    for head in range(heads):
        rows_aux[head, 0:1, :] = norm[head : head + 1]
        rows_aux[head, 1:2, :] = delta[head : head + 1]

    def block_terms(scaled, keys_turned, both_rows, both_turned, bias, norm_row, delta_row):
        count, width_here = scaled.shape[0] // BLK, delta_row.shape[1]
        products = dot_f32(scaled, both_turned)
        scores = products[:, :width_here].reshape(count, BLK, width_here)
        shift = bias[:count] - norm_row
        weights = jnp.exp(scores + shift[:, None, :]).reshape(count * BLK, width_here)
        grad_scores = (weights * (products[:, width_here:] - delta_row)).astype(jnp.bfloat16)
        joined = jnp.concatenate([grad_scores, weights.astype(jnp.bfloat16)], axis=1)
        cache_part = dot_f32(joined, both_rows) * lane_scale
        query_part = dot_f32(keys_turned, grad_scores)
        return query_part, cache_part

    def finish(tile):
        b_copy(tile).wait_recv()
        for inner in range(PER_TILE):
            head = tile * PER_TILE + inner
            acc_kv[head, pl.ds(window, span), :] += back_in[head].astype(jnp.float32)
            dkv_ref[head] = acc_kv[head].astype(jnp.bfloat16)

    def one_tile(tile, carry):
        for step in range(1, n_seq):
            q_copy(tile, step).wait_recv()
            g_copy(tile, step).wait_recv()

        @pl.when(tile + 2 < tiles)
        def _():
            send_q(tile + 2)
            send_g(tile + 2)
            h_copy(tile + 2).start()

        blank = jnp.zeros((rows, HD), jnp.bfloat16)
        q_turned = jnp.transpose(qbuf[tile])
        g_turned = jnp.transpose(gbuf[tile])
        for inner in range(PER_TILE):
            lanes = slice(inner * HD, (inner + 1) * HD)
            joint[inner, 0] = jnp.concatenate([qbuf[tile, :, lanes], blank], axis=1)
            joint[inner, 1] = jnp.concatenate([blank, gbuf[tile, :, lanes]], axis=1)
            turned[inner, :HD, :rows] = q_turned[lanes]
            turned[inner, HD:, rows:] = g_turned[lanes]
        h_copy(tile).wait_recv()
        for inner in range(PER_TILE):
            head = tile * PER_TILE + inner
            scaled = halo[head] * lane_scale_half
            query_part, cache_part = block_terms(
                scaled,
                jnp.transpose(scaled)[:HD],
                joint[inner, :, pl.ds(window, span), :].reshape(2 * span, LANES),
                jnp.concatenate(
                    [turned[inner, :, pl.ds(window, span)], turned[inner, :, pl.ds(far_window, span)]], axis=1
                ),
                bias_halo[:, pl.ds(window, span)],
                rows_aux[head, 0:1, pl.ds(window, span)],
                rows_aux[head, 1:2, pl.ds(window, span)],
            )
            back_out[head] = cache_part.astype(jnp.bfloat16)
            acc[head, :, pl.ds(window, span)] = query_part
            acc[head, :, pl.ds(pl.multiple_of(tp * span, LANES), rows - span)] = jnp.zeros(
                (HD, rows - span), jnp.float32
            )
        b_copy(tile).start()
        for inner in range(PER_TILE):
            head = tile * PER_TILE + inner
            query_part, cache_part = block_terms(
                kv[head],
                key_turned[head],
                joint[inner].reshape(2 * rows, LANES),
                turned[inner],
                bias_own[...],
                rows_aux[head, 0:1, :],
                rows_aux[head, 1:2, :],
            )
            dq_ref[head] = (acc[head] + query_part).astype(jnp.bfloat16)
            acc_kv[head] = cache_part
        @pl.when(tile >= 2)
        def _():
            finish(tile - 2)

        return carry

    lax.fori_loop(0, tiles, one_tile, 0)
    finish(tiles - 2)
    finish(tiles - 1)

    for tile in range(tiles):
        for dest in range(n_seq):
            up_copy(tile, dest).wait_send()
        for step in range(1, n_seq):
            q_copy(tile, step).wait_send()
            g_copy(tile, step).wait_send()
        h_copy(tile).wait_send()
        b_copy(tile).wait_send()
    for step in range(1, n_seq):
        d_copy(step).wait_send()


def fused_body(upstream, queries, attention_out, keys_values, log_totals, neighbours):
    tokens, width = queries.shape[2:]
    heads, rows = keys_values.shape[2:4]
    tiles = heads // PER_TILE
    n_seq = lax.axis_size("seq")
    span = REACH * BLK
    blocks_pad = 8 * -(-(rows // BLK) // 8)
    bf16, f32 = jnp.bfloat16, jnp.float32
    vmem = pl.BlockSpec(memory_space=pltpu.VMEM)
    pinned = pl.BlockSpec(memory_space=pltpu.HBM)
    dma = pltpu.SemaphoreType.DMA
    query_turned, cache_grad = pl.pallas_call(
        fused_kernel,
        out_shape=(
            jax.ShapeDtypeStruct((heads, HD, rows), bf16),
            jax.ShapeDtypeStruct((heads, rows, 2 * HD), bf16),
        ),
        in_specs=[pinned] * 6,
        out_specs=(vmem, vmem),
        scratch_shapes=[
            pltpu.SMEM((NBR, neighbours.shape[0]), jnp.int32),
            pltpu.VMEM((heads, rows), f32),
            pltpu.VMEM((tokens, width), bf16),
            pltpu.VMEM((tokens, width), bf16),
            pltpu.VMEM((heads, rows, 2 * HD), bf16),
            pltpu.VMEM((heads, span, 2 * HD), bf16),
            pltpu.VMEM((tiles, rows, LANES), bf16),
            pltpu.VMEM((tiles, rows, LANES), bf16),
            pltpu.VMEM((n_seq, heads, LANES), f32),
            pltpu.VMEM((n_seq, heads, LANES), f32),
            pltpu.VMEM((heads, HD, rows), f32),
            pltpu.VMEM((heads, rows, 2 * HD), f32),
            pltpu.VMEM((heads, span, 2 * HD), bf16),
            pltpu.VMEM((heads, span, 2 * HD), bf16),
            pltpu.VMEM((blocks_pad, rows), f32),
            pltpu.VMEM((8, rows), f32),
            pltpu.VMEM((heads, 8, rows), f32),
            pltpu.VMEM((PER_TILE, 2, rows, LANES), bf16),
            pltpu.VMEM((PER_TILE, 2 * HD, 2 * rows), bf16),
            pltpu.VMEM((heads, HD, rows), bf16),
            dma((tiles, n_seq)),
            dma((tiles, n_seq)),
            dma((tiles, n_seq - 1)),
            dma((tiles, n_seq - 1)),
            dma((tiles, n_seq - 1)),
            dma((tiles, n_seq - 1)),
            dma((n_seq - 1,)),
            dma((n_seq - 1,)),
            dma((tiles,)),
            dma((tiles,)),
            dma((tiles,)),
            dma((tiles,)),
            dma((4 + tiles,)),
        ],
        compiler_params=pltpu.CompilerParams(
            collective_id=0, has_side_effects=True, vmem_limit_bytes=48 * 1024 * 1024
        ),
    )(
        *[
            pltpu.with_memory_space_constraint(operand, pltpu.HBM)
            for operand in (
                jnp.transpose(neighbours),
                log_totals.reshape(heads, rows),
                upstream.reshape(tokens, width),
                queries.reshape(tokens, width),
                attention_out.reshape(tokens, width),
                keys_values.reshape(heads, rows, 2 * HD),
            )
        ]
    )
    query_grad = jnp.transpose(query_turned, (0, 2, 1)).reshape(1, 1, heads, rows, HD)
    return query_grad, cache_grad.reshape(1, 1, heads, rows, 2 * HD)


def body(upstream, queries, attention_out, keys_values, log_totals, neighbours):
    tokens = queries.shape[2]
    heads, rows = keys_values.shape[2:4]
    fits = (
        lax.axis_size("tp") == 2
        and lax.axis_size("pipe") > 1
        and lax.axis_size("seq") > 1
        and heads == 8
        and tokens % 16 == 0
        and tokens <= LANES
        and rows % LANES == 0
        and REACH * BLK < rows <= 512
    )
    chosen = fused_body if fits else general_body
    return chosen(upstream, queries, attention_out, keys_values, log_totals, neighbours)


def solution(mesh):
    placed = (
        P("pipe", "tp", "seq", None),
        P("pipe", "tp", "seq", None),
        P("pipe", "tp", "seq", None),
        P("pipe", "tp", "seq", None, None),
        P("pipe", "tp", "seq", None),
        P(),
    )
    return jax.shard_map(
        body,
        mesh=mesh,
        in_specs=placed,
        out_specs=(P("pipe", "tp", "seq", None, None), P("pipe", "tp", "seq", None, None)),
        check_vma=False,
    )
```

```python
import jax
import jax.numpy as jnp
from jax import lax
from jax.experimental import pallas as pl
from jax.experimental.pallas import tpu as pltpu
from jax.sharding import PartitionSpec as P

H = 32
HD = 64
BLK = 64
REACH = 4
NBR = 7


pair_group = 32


def passed_along(value, axis, steps):
    count = lax.axis_size(axis)
    pairs = [(source, (source + steps) % count) for source in range(count)]
    return lax.ppermute(value, axis, pairs)


def padded_2(cells, sides, width):
    for axis, dim in sides:
        count = lax.axis_size(axis)
        ends = count - 1
        head = lax.slice_in_dim(cells, 0, width, axis=dim)
        tail = lax.slice_in_dim(cells, cells.shape[dim] - width, cells.shape[dim], axis=dim)
        cells = jnp.concatenate(
            [
                lax.ppermute(tail, axis, [(i, (i + 1) % count) for i in range(ends)]),
                cells,
                lax.ppermute(head, axis, [((i + 1) % count, i) for i in range(ends)]),
            ],
            axis=dim,
        )
    return cells


def block_layout(values, blocks_here):
    heads_here = values.shape[1]
    turned = jnp.transpose(values, (1, 0, 2))
    return turned.reshape(heads_here, blocks_here, BLK, values.shape[2])


def general_body(upstream, queries, attention_out, keys_values, log_totals, neighbours):
    tokens_here = queries.shape[2]
    inv_root = HD ** (-0.5)
    incoming = passed_along(upstream, "pipe", -1)
    query_tok = queries.reshape(tokens_here, H, HD)
    grad_tok = incoming.reshape(tokens_here, H, HD)
    out_tok = attention_out.reshape(tokens_here, H, HD)
    packed = jnp.concatenate([query_tok, grad_tok, out_tok], axis=2)
    regrouped = lax.all_to_all(packed, "seq", split_axis=1, concat_axis=0, tiled=True)
    query_heads = regrouped[:, :, :HD]
    grad_heads = regrouped[:, :, HD : 2 * HD]
    out_heads = regrouped[:, :, 2 * HD :]
    row_delta = jnp.sum(grad_heads.astype(jnp.float32) * out_heads.astype(jnp.float32), axis=2)
    rows_here = query_heads.shape[0]
    heads_here = query_heads.shape[1]
    blocks_here = rows_here // BLK
    query_blocks = block_layout(query_heads, blocks_here)
    grad_blocks = block_layout(grad_heads, blocks_here)
    delta_blocks = jnp.transpose(row_delta).reshape(heads_here, blocks_here, BLK)
    norm_blocks = log_totals.reshape(heads_here, blocks_here, BLK)
    cache_blocks = keys_values.reshape(heads_here, blocks_here, BLK, 2 * HD)
    padded = padded_2(cache_blocks, (("tp", 1),), REACH)
    first_block = lax.axis_index("tp") * blocks_here
    listed = lax.dynamic_slice_in_dim(neighbours, first_block, blocks_here, 0)
    present = (listed >= 0).reshape(-1)
    slot_count = blocks_here * NBR
    group_total = (slot_count + pair_group - 1) // pair_group
    capacity = group_total * pair_group
    running = jnp.cumsum(present.astype(jnp.int32)) - 1
    pair_count = jnp.sum(present.astype(jnp.int32))
    target = jnp.where(present, running, capacity)
    query_source = jnp.repeat(jnp.arange(blocks_here, dtype=jnp.int32), NBR)
    key_source = (listed - first_block + REACH).reshape(-1)
    pair_query = jnp.zeros((capacity,), jnp.int32).at[target].set(query_source, mode="drop")
    pair_key = jnp.zeros((capacity,), jnp.int32).at[target].set(key_source, mode="drop")

    def one_group(group_step, totals):
        query_acc, cache_acc = totals
        first_pair = group_step * pair_group
        query_pick = lax.dynamic_slice_in_dim(pair_query, first_pair, pair_group)
        key_pick = lax.dynamic_slice_in_dim(pair_key, first_pair, pair_group)
        live_mask = (first_pair + jnp.arange(pair_group) < pair_count).astype(jnp.float32)
        query_rows = query_blocks[:, query_pick]
        grad_rows = grad_blocks[:, query_pick]
        norm_rows = norm_blocks[:, query_pick]
        delta_rows = delta_blocks[:, query_pick]
        cache_rows = padded[:, key_pick]
        key_rows = cache_rows[..., :HD]
        value_rows = cache_rows[..., HD:]
        scores = (
            jnp.einsum("hgqd,hgkd->hgqk", query_rows, key_rows, preferred_element_type=jnp.float32)
            * inv_root
        )
        weights = jnp.exp(scores - norm_rows[..., None]) * live_mask[None, :, None, None]
        weights_half = weights.astype(jnp.bfloat16)
        grad_weights = jnp.einsum(
            "hgqd,hgkd->hgqk", grad_rows, value_rows, preferred_element_type=jnp.float32
        )
        grad_scores = (weights * (grad_weights - delta_rows[..., None])).astype(jnp.bfloat16)
        query_part = (
            jnp.einsum("hgqk,hgkd->hgqd", grad_scores, key_rows, preferred_element_type=jnp.float32)
            * inv_root
        )
        key_part = (
            jnp.einsum(
                "hgqk,hgqd->hgkd", grad_scores, query_rows, preferred_element_type=jnp.float32
            )
            * inv_root
        )
        value_part = jnp.einsum(
            "hgqk,hgqd->hgkd", weights_half, grad_rows, preferred_element_type=jnp.float32
        )
        query_acc = query_acc.at[:, query_pick].add(query_part)
        cache_acc = cache_acc.at[:, key_pick].add(jnp.concatenate([key_part, value_part], axis=-1))
        return (query_acc, cache_acc)

    group_live = (pair_count + pair_group - 1) // pair_group
    query_start = jnp.zeros((heads_here, blocks_here, BLK, HD), jnp.float32)
    cache_start = jnp.zeros((heads_here, blocks_here + 2 * REACH, BLK, 2 * HD), jnp.float32)
    query_acc, cache_acc = lax.fori_loop(0, group_live, one_group, (query_start, cache_start))
    rim_terms = jnp.concatenate([cache_acc[:, :REACH], cache_acc[:, REACH + blocks_here :]], axis=1)
    arrived = padded_2(rim_terms.astype(jnp.bfloat16), (("tp", 1),), REACH).astype(rim_terms.dtype)
    own_part = cache_acc[:, REACH : REACH + blocks_here]
    own_part = own_part.at[:, :REACH].add(arrived[:, :REACH])
    own_part = own_part.at[:, blocks_here - REACH :].add(arrived[:, 3 * REACH :])
    query_grad = query_acc.reshape(1, 1, heads_here, rows_here, HD).astype(jnp.bfloat16)
    cache_grad = own_part.reshape(1, 1, heads_here, rows_here, 2 * HD).astype(jnp.bfloat16)
    return (query_grad, cache_grad)


MESH = pl.DeviceIdType.MESH
LANES = 128
PER_TILE = LANES // HD
ABSENT = -1e30
NT = (((1,), (1,)), ((), ()))


def dot_f32(left, right, dims=(((1,), (0,)), ((), ()))):
    return lax.dot_general(left, right, dims, preferred_element_type=jnp.float32)


def listed_bias(neigh_ref, first_row, first_key, key_rows, blocks_here):
    lane = lax.broadcasted_iota(jnp.int32, (key_rows, LANES), 1)
    key = lax.broadcasted_iota(jnp.int32, (key_rows, LANES), 0) + first_key
    tiles = []
    for pair in range(blocks_here // 2):
        found = None
        for slot in range(NBR):
            here = jnp.where(
                lane < BLK,
                neigh_ref[slot, first_row + 2 * pair],
                neigh_ref[slot, first_row + 2 * pair + 1],
            )
            hit = (key == here).astype(jnp.float32)
            found = hit if found is None else jnp.maximum(found, hit)
        tiles.append((found - 1.0) * -ABSENT)
    return jnp.concatenate(tiles, axis=1)


def fused_kernel(
    neigh_hbm, norm_hbm, up_ref, query_ref, out_ref, cache_ref, dq_ref, dkv_ref,
    neigh_ref, norm_ref, inc, outs, kv, halo, qbuf, gbuf, dsend, dgot, acc, acc_kv, back_out, back_in, bias_own, bias_halo, rows_aux, joint, turned, key_turned,
    up_send, up_recv, q_send, q_recv, g_send, g_recv, d_send, d_recv, h_send, h_recv, b_send, b_recv, local_sem,
):
    n_pipe, n_seq = lax.axis_size("pipe"), lax.axis_size("seq")
    pipe, seq, tp = lax.axis_index("pipe"), lax.axis_index("seq"), lax.axis_index("tp")
    tokens, width = inc.shape
    heads, rows, _ = kv.shape
    tiles = heads // PER_TILE
    span = REACH * BLK
    blocks_here = rows // BLK
    share = heads * HD
    below, above = lax.rem(pipe + n_pipe - 1, n_pipe), lax.rem(pipe + 1, n_pipe)
    mate = 1 - tp
    window = pl.multiple_of(mate * (rows - span), LANES)
    far_window = pl.multiple_of(rows + mate * (rows - span), LANES)
    mine = pl.multiple_of(seq * tokens, 16)

    def peer(step):
        if n_seq == 4:
            return (lax.rem(seq + 2, 4), 3 - seq, seq + 1 - 2 * lax.rem(seq, 2))[step - 1]
        return lax.rem(seq + step, n_seq)

    def tile_cols(dest, tile):
        return pl.ds(pl.multiple_of(dest * share + tile * LANES, LANES), LANES)

    def up_copy(tile, dest):
        cols = pl.ds(dest * share + tile * LANES, LANES)
        return pltpu.make_async_remote_copy(
            src_ref=up_ref.at[:, cols], dst_ref=inc.at[:, cols],
            send_sem=up_send.at[tile, dest], recv_sem=up_recv.at[tile, dest],
            device_id={"pipe": below}, device_id_type=MESH,
        )

    def q_copy(tile, step):
        return pltpu.make_async_remote_copy(
            src_ref=query_ref.at[:, tile_cols(peer(step), tile)],
            dst_ref=qbuf.at[tile, pl.ds(mine, tokens), :],
            send_sem=q_send.at[tile, step - 1], recv_sem=q_recv.at[tile, step - 1],
            device_id={"seq": peer(step)}, device_id_type=MESH,
        )

    def g_copy(tile, step):
        return pltpu.make_async_remote_copy(
            src_ref=inc.at[:, tile_cols(peer(step), tile)],
            dst_ref=gbuf.at[tile, pl.ds(mine, tokens), :],
            send_sem=g_send.at[tile, step - 1], recv_sem=g_recv.at[tile, step - 1],
            device_id={"seq": peer(step)}, device_id_type=MESH,
        )

    def d_copy(step):
        return pltpu.make_async_remote_copy(
            src_ref=dsend.at[peer(step)], dst_ref=dgot.at[seq],
            send_sem=d_send.at[step - 1], recv_sem=d_recv.at[step - 1],
            device_id={"seq": peer(step)}, device_id_type=MESH,
        )

    def h_copy(tile):
        pair = pl.ds(tile * PER_TILE, PER_TILE)
        return pltpu.make_async_remote_copy(
            src_ref=cache_ref.at[pair, pl.ds(window, span), :], dst_ref=halo.at[pair],
            send_sem=h_send.at[tile], recv_sem=h_recv.at[tile],
            device_id={"tp": mate}, device_id_type=MESH,
        )

    def b_copy(head):
        return pltpu.make_async_remote_copy(
            src_ref=back_out.at[head], dst_ref=back_in.at[head],
            send_sem=b_send.at[head], recv_sem=b_recv.at[head],
            device_id={"tp": mate}, device_id_type=MESH,
        )

    out_local = pltpu.make_async_copy(out_ref, outs, local_sem.at[0])
    kv_local = pltpu.make_async_copy(cache_ref, kv, local_sem.at[1])
    q_local = [
        pltpu.make_async_copy(
            query_ref.at[:, tile_cols(seq, tile)], qbuf.at[tile, pl.ds(mine, tokens), :], local_sem.at[2 + tile]
        )
        for tile in range(tiles)
    ]
    neigh_local = pltpu.make_async_copy(neigh_hbm, neigh_ref, local_sem.at[2 + tiles])
    norm_local = pltpu.make_async_copy(norm_hbm, norm_ref, local_sem.at[3 + tiles])
    neigh_local.start()
    norm_local.start()
    out_local.start()
    kv_local.start()
    for copy in q_local:
        copy.start()

    barrier = pltpu.get_barrier_semaphore()
    pl.semaphore_signal(barrier, inc=1, device_id={"pipe": above}, device_id_type=MESH)
    pl.semaphore_signal(barrier, inc=1, device_id={"tp": mate}, device_id_type=MESH)
    for step in range(1, n_seq):
        pl.semaphore_signal(barrier, inc=1, device_id={"seq": peer(step)}, device_id_type=MESH)
    pl.semaphore_wait(barrier, n_seq + 1)

    def send_up(tile):
        for dest in range(n_seq):
            up_copy(tile, dest).start()

    def send_q(tile):
        for step in range(1, n_seq):
            q_copy(tile, step).start()

    def send_g(tile):
        for step in range(1, n_seq):
            g_copy(tile, step).start()

    send_up(0)
    send_q(0)
    h_copy(0).start()
    send_up(1)

    neigh_local.wait()
    first_row = tp * blocks_here
    halo_key = mate * blocks_here + tp * (blocks_here - REACH)
    bias_own[...] = listed_bias(neigh_ref, first_row, first_row, bias_own.shape[0], blocks_here)
    bias_halo[...] = listed_bias(neigh_ref, first_row, halo_key, bias_halo.shape[0], blocks_here)

    inv_root = HD ** (-0.5)
    key_lane = lax.broadcasted_iota(jnp.int32, (1, 2 * HD), 1) < HD
    lane_scale = jnp.where(key_lane, inv_root, 1.0)
    lane_scale_half = lane_scale.astype(jnp.bfloat16)

    def prepare(head, carry):
        scaled = kv[head] * lane_scale_half
        kv[head] = scaled
        key_turned[head] = jnp.transpose(scaled)[:HD]
        return carry

    for tile in range(tiles):
        for dest in range(n_seq):
            up_copy(tile, dest).wait_recv()
        if tile + 2 < tiles:
            send_up(tile + 2)
        if tile < 2:
            send_g(tile)
            send_q(tile + 1)
        if tile + 1 < tiles:
            h_copy(tile + 1).start()
        if tile == 1:
            turned[...] = jnp.zeros_like(turned)
            kv_local.wait()
            lax.fori_loop(0, heads, prepare, 0)

    out_local.wait()
    picks = (
        lax.broadcasted_iota(jnp.int32, (heads, share), 1) // HD
        == lax.broadcasted_iota(jnp.int32, (heads, share), 0)
    ).astype(jnp.bfloat16)
    dsend[...] = jnp.zeros_like(dsend)
    for dest in range(n_seq):
        cols = pl.ds(dest * share, share)
        terms = inc[:, cols].astype(jnp.float32) * outs[:, cols].astype(jnp.float32)
        high = terms.astype(jnp.bfloat16)
        low = (terms - high.astype(jnp.float32)).astype(jnp.bfloat16)
        dsend[dest, :, :tokens] = dot_f32(picks, high, NT) + dot_f32(picks, low, NT)
    for step in range(1, n_seq):
        d_copy(step).start()
    dgot[seq] = dsend[seq]
    for tile in range(tiles):
        gbuf[tile, pl.ds(mine, tokens), :] = inc[:, tile_cols(seq, tile)]
    for copy in q_local:
        copy.wait()
    for step in range(1, n_seq):
        d_copy(step).wait_recv()
    delta = None
    for source in range(n_seq):
        part = jnp.concatenate([dgot[source], jnp.zeros((heads, rows - LANES), jnp.float32)], axis=1)
        if source:
            part = pltpu.roll(part, source * tokens, 1)
        delta = part if delta is None else delta + part
    norm_local.wait()
    norm = norm_ref[...]
    for head in range(heads):
        rows_aux[head, 0:1, :] = norm[head : head + 1]
        rows_aux[head, 1:2, :] = delta[head : head + 1]

    def block_terms(scaled, keys_turned, both_rows, both_turned, bias, norm_row, delta_row):
        count, width_here = scaled.shape[0] // BLK, delta_row.shape[1]
        products = dot_f32(scaled, both_turned)
        scores = products[:, :width_here].reshape(count, BLK, width_here)
        shift = bias[:count] - norm_row
        weights = jnp.exp(scores + shift[:, None, :]).reshape(count * BLK, width_here)
        grad_scores = (weights * (products[:, width_here:] - delta_row)).astype(jnp.bfloat16)
        joined = jnp.concatenate([grad_scores, weights.astype(jnp.bfloat16)], axis=1)
        cache_part = dot_f32(joined, both_rows) * lane_scale
        query_part = dot_f32(keys_turned, grad_scores)
        return query_part, cache_part

    def finish(tile):
        for inner in range(PER_TILE):
            head = tile * PER_TILE + inner
            b_copy(head).wait_recv()
            acc_kv[head, pl.ds(window, span), :] += back_in[head].astype(jnp.float32)
            dkv_ref[head] = acc_kv[head].astype(jnp.bfloat16)

    def one_tile(tile, carry):
        for step in range(1, n_seq):
            q_copy(tile, step).wait_recv()
            g_copy(tile, step).wait_recv()

        @pl.when(tile + 2 < tiles)
        def _():
            send_g(tile + 2)

        @pl.when(tile + 3 < tiles)
        def _():
            send_q(tile + 3)

        blank = jnp.zeros((rows, HD), jnp.bfloat16)
        q_turned = jnp.transpose(qbuf[tile])
        g_turned = jnp.transpose(gbuf[tile])
        for inner in range(PER_TILE):
            lanes = slice(inner * HD, (inner + 1) * HD)
            joint[inner, 0] = jnp.concatenate([qbuf[tile, :, lanes], blank], axis=1)
            joint[inner, 1] = jnp.concatenate([blank, gbuf[tile, :, lanes]], axis=1)
            turned[inner, :HD, :rows] = q_turned[lanes]
            turned[inner, HD:, rows:] = g_turned[lanes]
        h_copy(tile).wait_recv()
        for inner in range(PER_TILE):
            head = tile * PER_TILE + inner
            scaled = halo[head] * lane_scale_half
            query_part, cache_part = block_terms(
                scaled,
                jnp.transpose(scaled)[:HD],
                joint[inner, :, pl.ds(window, span), :].reshape(2 * span, LANES),
                jnp.concatenate(
                    [turned[inner, :, pl.ds(window, span)], turned[inner, :, pl.ds(far_window, span)]], axis=1
                ),
                bias_halo[:, pl.ds(window, span)],
                rows_aux[head, 0:1, pl.ds(window, span)],
                rows_aux[head, 1:2, pl.ds(window, span)],
            )
            back_out[head] = cache_part.astype(jnp.bfloat16)
            b_copy(head).start()
            acc[head, :, pl.ds(window, span)] = query_part
            acc[head, :, pl.ds(pl.multiple_of(tp * span, LANES), rows - span)] = jnp.zeros(
                (HD, rows - span), jnp.float32
            )
        for inner in range(PER_TILE):
            head = tile * PER_TILE + inner
            query_part, cache_part = block_terms(
                kv[head],
                key_turned[head],
                joint[inner].reshape(2 * rows, LANES),
                turned[inner],
                bias_own[...],
                rows_aux[head, 0:1, :],
                rows_aux[head, 1:2, :],
            )
            dq_ref[head] = (acc[head] + query_part).astype(jnp.bfloat16)
            acc_kv[head] = cache_part
        @pl.when(tile >= 2)
        def _():
            finish(tile - 2)

        return carry

    lax.fori_loop(0, tiles, one_tile, 0)
    finish(tiles - 2)
    finish(tiles - 1)

    for tile in range(tiles):
        for dest in range(n_seq):
            up_copy(tile, dest).wait_send()
        for step in range(1, n_seq):
            q_copy(tile, step).wait_send()
            g_copy(tile, step).wait_send()
        h_copy(tile).wait_send()
        for inner in range(PER_TILE):
            b_copy(tile * PER_TILE + inner).wait_send()
    for step in range(1, n_seq):
        d_copy(step).wait_send()


def fused_body(upstream, queries, attention_out, keys_values, log_totals, neighbours):
    tokens, width = queries.shape[2:]
    heads, rows = keys_values.shape[2:4]
    tiles = heads // PER_TILE
    n_seq = lax.axis_size("seq")
    span = REACH * BLK
    blocks_pad = 8 * -(-(rows // BLK) // 8)
    bf16, f32 = jnp.bfloat16, jnp.float32
    vmem = pl.BlockSpec(memory_space=pltpu.VMEM)
    pinned = pl.BlockSpec(memory_space=pltpu.HBM)
    dma = pltpu.SemaphoreType.DMA
    query_turned, cache_grad = pl.pallas_call(
        fused_kernel,
        out_shape=(
            jax.ShapeDtypeStruct((heads, HD, rows), bf16),
            jax.ShapeDtypeStruct((heads, rows, 2 * HD), bf16),
        ),
        in_specs=[pinned] * 6,
        out_specs=(vmem, vmem),
        scratch_shapes=[
            pltpu.SMEM((NBR, neighbours.shape[0]), jnp.int32),
            pltpu.VMEM((heads, rows), f32),
            pltpu.VMEM((tokens, width), bf16),
            pltpu.VMEM((tokens, width), bf16),
            pltpu.VMEM((heads, rows, 2 * HD), bf16),
            pltpu.VMEM((heads, span, 2 * HD), bf16),
            pltpu.VMEM((tiles, rows, LANES), bf16),
            pltpu.VMEM((tiles, rows, LANES), bf16),
            pltpu.VMEM((n_seq, heads, LANES), f32),
            pltpu.VMEM((n_seq, heads, LANES), f32),
            pltpu.VMEM((heads, HD, rows), f32),
            pltpu.VMEM((heads, rows, 2 * HD), f32),
            pltpu.VMEM((heads, span, 2 * HD), bf16),
            pltpu.VMEM((heads, span, 2 * HD), bf16),
            pltpu.VMEM((blocks_pad, rows), f32),
            pltpu.VMEM((8, rows), f32),
            pltpu.VMEM((heads, 8, rows), f32),
            pltpu.VMEM((PER_TILE, 2, rows, LANES), bf16),
            pltpu.VMEM((PER_TILE, 2 * HD, 2 * rows), bf16),
            pltpu.VMEM((heads, HD, rows), bf16),
            dma((tiles, n_seq)),
            dma((tiles, n_seq)),
            dma((tiles, n_seq - 1)),
            dma((tiles, n_seq - 1)),
            dma((tiles, n_seq - 1)),
            dma((tiles, n_seq - 1)),
            dma((n_seq - 1,)),
            dma((n_seq - 1,)),
            dma((tiles,)),
            dma((tiles,)),
            dma((heads,)),
            dma((heads,)),
            dma((4 + tiles,)),
        ],
        compiler_params=pltpu.CompilerParams(
            collective_id=0, has_side_effects=True, vmem_limit_bytes=48 * 1024 * 1024
        ),
    )(
        *[
            pltpu.with_memory_space_constraint(operand, pltpu.HBM)
            for operand in (
                jnp.transpose(neighbours),
                log_totals.reshape(heads, rows),
                upstream.reshape(tokens, width),
                queries.reshape(tokens, width),
                attention_out.reshape(tokens, width),
                keys_values.reshape(heads, rows, 2 * HD),
            )
        ]
    )
    query_grad = jnp.transpose(query_turned, (0, 2, 1)).reshape(1, 1, heads, rows, HD)
    return query_grad, cache_grad.reshape(1, 1, heads, rows, 2 * HD)


def body(upstream, queries, attention_out, keys_values, log_totals, neighbours):
    tokens = queries.shape[2]
    heads, rows = keys_values.shape[2:4]
    fits = (
        lax.axis_size("tp") == 2
        and lax.axis_size("pipe") > 1
        and lax.axis_size("seq") > 1
        and heads == 8
        and tokens % 16 == 0
        and tokens <= LANES
        and rows % LANES == 0
        and REACH * BLK < rows <= 512
    )
    chosen = fused_body if fits else general_body
    return chosen(upstream, queries, attention_out, keys_values, log_totals, neighbours)


def solution(mesh):
    placed = (
        P("pipe", "tp", "seq", None),
        P("pipe", "tp", "seq", None),
        P("pipe", "tp", "seq", None),
        P("pipe", "tp", "seq", None, None),
        P("pipe", "tp", "seq", None),
        P(),
    )
    return jax.shard_map(
        body,
        mesh=mesh,
        in_specs=placed,
        out_specs=(P("pipe", "tp", "seq", None, None), P("pipe", "tp", "seq", None, None)),
        check_vma=False,
    )
```

```python
import jax
import jax.numpy as jnp
from jax import lax
from jax.experimental import pallas as pl
from jax.experimental.pallas import tpu as pltpu
from jax.sharding import PartitionSpec as P

H = 32
HD = 64
BLK = 64
REACH = 4
NBR = 7


pair_group = 32


def passed_along(value, axis, steps):
    count = lax.axis_size(axis)
    pairs = [(source, (source + steps) % count) for source in range(count)]
    return lax.ppermute(value, axis, pairs)


def padded_2(cells, sides, width):
    for axis, dim in sides:
        count = lax.axis_size(axis)
        ends = count - 1
        head = lax.slice_in_dim(cells, 0, width, axis=dim)
        tail = lax.slice_in_dim(cells, cells.shape[dim] - width, cells.shape[dim], axis=dim)
        cells = jnp.concatenate(
            [
                lax.ppermute(tail, axis, [(i, (i + 1) % count) for i in range(ends)]),
                cells,
                lax.ppermute(head, axis, [((i + 1) % count, i) for i in range(ends)]),
            ],
            axis=dim,
        )
    return cells


def block_layout(values, blocks_here):
    heads_here = values.shape[1]
    turned = jnp.transpose(values, (1, 0, 2))
    return turned.reshape(heads_here, blocks_here, BLK, values.shape[2])


def general_body(upstream, queries, attention_out, keys_values, log_totals, neighbours):
    tokens_here = queries.shape[2]
    inv_root = HD ** (-0.5)
    incoming = passed_along(upstream, "pipe", -1)
    query_tok = queries.reshape(tokens_here, H, HD)
    grad_tok = incoming.reshape(tokens_here, H, HD)
    out_tok = attention_out.reshape(tokens_here, H, HD)
    packed = jnp.concatenate([query_tok, grad_tok, out_tok], axis=2)
    regrouped = lax.all_to_all(packed, "seq", split_axis=1, concat_axis=0, tiled=True)
    query_heads = regrouped[:, :, :HD]
    grad_heads = regrouped[:, :, HD : 2 * HD]
    out_heads = regrouped[:, :, 2 * HD :]
    row_delta = jnp.sum(grad_heads.astype(jnp.float32) * out_heads.astype(jnp.float32), axis=2)
    rows_here = query_heads.shape[0]
    heads_here = query_heads.shape[1]
    blocks_here = rows_here // BLK
    query_blocks = block_layout(query_heads, blocks_here)
    grad_blocks = block_layout(grad_heads, blocks_here)
    delta_blocks = jnp.transpose(row_delta).reshape(heads_here, blocks_here, BLK)
    norm_blocks = log_totals.reshape(heads_here, blocks_here, BLK)
    cache_blocks = keys_values.reshape(heads_here, blocks_here, BLK, 2 * HD)
    padded = padded_2(cache_blocks, (("tp", 1),), REACH)
    first_block = lax.axis_index("tp") * blocks_here
    listed = lax.dynamic_slice_in_dim(neighbours, first_block, blocks_here, 0)
    present = (listed >= 0).reshape(-1)
    slot_count = blocks_here * NBR
    group_total = (slot_count + pair_group - 1) // pair_group
    capacity = group_total * pair_group
    running = jnp.cumsum(present.astype(jnp.int32)) - 1
    pair_count = jnp.sum(present.astype(jnp.int32))
    target = jnp.where(present, running, capacity)
    query_source = jnp.repeat(jnp.arange(blocks_here, dtype=jnp.int32), NBR)
    key_source = (listed - first_block + REACH).reshape(-1)
    pair_query = jnp.zeros((capacity,), jnp.int32).at[target].set(query_source, mode="drop")
    pair_key = jnp.zeros((capacity,), jnp.int32).at[target].set(key_source, mode="drop")

    def one_group(group_step, totals):
        query_acc, cache_acc = totals
        first_pair = group_step * pair_group
        query_pick = lax.dynamic_slice_in_dim(pair_query, first_pair, pair_group)
        key_pick = lax.dynamic_slice_in_dim(pair_key, first_pair, pair_group)
        live_mask = (first_pair + jnp.arange(pair_group) < pair_count).astype(jnp.float32)
        query_rows = query_blocks[:, query_pick]
        grad_rows = grad_blocks[:, query_pick]
        norm_rows = norm_blocks[:, query_pick]
        delta_rows = delta_blocks[:, query_pick]
        cache_rows = padded[:, key_pick]
        key_rows = cache_rows[..., :HD]
        value_rows = cache_rows[..., HD:]
        scores = (
            jnp.einsum("hgqd,hgkd->hgqk", query_rows, key_rows, preferred_element_type=jnp.float32)
            * inv_root
        )
        weights = jnp.exp(scores - norm_rows[..., None]) * live_mask[None, :, None, None]
        weights_half = weights.astype(jnp.bfloat16)
        grad_weights = jnp.einsum(
            "hgqd,hgkd->hgqk", grad_rows, value_rows, preferred_element_type=jnp.float32
        )
        grad_scores = (weights * (grad_weights - delta_rows[..., None])).astype(jnp.bfloat16)
        query_part = (
            jnp.einsum("hgqk,hgkd->hgqd", grad_scores, key_rows, preferred_element_type=jnp.float32)
            * inv_root
        )
        key_part = (
            jnp.einsum(
                "hgqk,hgqd->hgkd", grad_scores, query_rows, preferred_element_type=jnp.float32
            )
            * inv_root
        )
        value_part = jnp.einsum(
            "hgqk,hgqd->hgkd", weights_half, grad_rows, preferred_element_type=jnp.float32
        )
        query_acc = query_acc.at[:, query_pick].add(query_part)
        cache_acc = cache_acc.at[:, key_pick].add(jnp.concatenate([key_part, value_part], axis=-1))
        return (query_acc, cache_acc)

    group_live = (pair_count + pair_group - 1) // pair_group
    query_start = jnp.zeros((heads_here, blocks_here, BLK, HD), jnp.float32)
    cache_start = jnp.zeros((heads_here, blocks_here + 2 * REACH, BLK, 2 * HD), jnp.float32)
    query_acc, cache_acc = lax.fori_loop(0, group_live, one_group, (query_start, cache_start))
    rim_terms = jnp.concatenate([cache_acc[:, :REACH], cache_acc[:, REACH + blocks_here :]], axis=1)
    arrived = padded_2(rim_terms.astype(jnp.bfloat16), (("tp", 1),), REACH).astype(rim_terms.dtype)
    own_part = cache_acc[:, REACH : REACH + blocks_here]
    own_part = own_part.at[:, :REACH].add(arrived[:, :REACH])
    own_part = own_part.at[:, blocks_here - REACH :].add(arrived[:, 3 * REACH :])
    query_grad = query_acc.reshape(1, 1, heads_here, rows_here, HD).astype(jnp.bfloat16)
    cache_grad = own_part.reshape(1, 1, heads_here, rows_here, 2 * HD).astype(jnp.bfloat16)
    return (query_grad, cache_grad)


MESH = pl.DeviceIdType.MESH
LANES = 128
PER_TILE = LANES // HD
ABSENT = -1e30
NT = (((1,), (1,)), ((), ()))


def dot_f32(left, right, dims=(((1,), (0,)), ((), ()))):
    return lax.dot_general(left, right, dims, preferred_element_type=jnp.float32)


def listed_bias(neigh_ref, first_row, first_key, key_rows, blocks_here):
    lane = lax.broadcasted_iota(jnp.int32, (key_rows, LANES), 1)
    key = lax.broadcasted_iota(jnp.int32, (key_rows, LANES), 0) + first_key
    tiles = []
    for pair in range(blocks_here // 2):
        found = None
        for slot in range(NBR):
            here = jnp.where(
                lane < BLK,
                neigh_ref[slot, first_row + 2 * pair],
                neigh_ref[slot, first_row + 2 * pair + 1],
            )
            hit = (key == here).astype(jnp.float32)
            found = hit if found is None else jnp.maximum(found, hit)
        tiles.append((found - 1.0) * -ABSENT)
    return jnp.concatenate(tiles, axis=1)


def fused_kernel(
    neigh_hbm, norm_hbm, up_ref, query_ref, out_ref, cache_ref, dq_ref, dkv_ref,
    neigh_ref, norm_ref, inc, outs, kv, halo, qbuf, gbuf, dsend, dgot, acc, acc_kv, back_out, back_in, bias_own, bias_halo, rows_aux, joint, turned, key_turned,
    up_send, up_recv, q_send, q_recv, g_send, g_recv, d_send, d_recv, h_send, h_recv, b_send, b_recv, local_sem,
):
    n_pipe, n_seq = lax.axis_size("pipe"), lax.axis_size("seq")
    pipe, seq, tp = lax.axis_index("pipe"), lax.axis_index("seq"), lax.axis_index("tp")
    tokens, width = inc.shape
    heads, rows, _ = kv.shape
    tiles = heads // PER_TILE
    span = REACH * BLK
    blocks_here = rows // BLK
    share = heads * HD
    below, above = lax.rem(pipe + n_pipe - 1, n_pipe), lax.rem(pipe + 1, n_pipe)
    mate = 1 - tp
    window = pl.multiple_of(mate * (rows - span), LANES)
    far_window = pl.multiple_of(rows + mate * (rows - span), LANES)
    mine = pl.multiple_of(seq * tokens, 16)

    def peer(step):
        if n_seq == 4:
            return (lax.rem(seq + 2, 4), 3 - seq, seq + 1 - 2 * lax.rem(seq, 2))[step - 1]
        return lax.rem(seq + step, n_seq)

    def tile_cols(dest, tile):
        return pl.ds(pl.multiple_of(dest * share + tile * LANES, LANES), LANES)

    def up_copy(tile, dest):
        cols = pl.ds(dest * share + tile * LANES, LANES)
        return pltpu.make_async_remote_copy(
            src_ref=up_ref.at[:, cols], dst_ref=inc.at[:, cols],
            send_sem=up_send.at[tile, dest], recv_sem=up_recv.at[tile, dest],
            device_id={"pipe": below}, device_id_type=MESH,
        )

    def q_copy(tile, step):
        return pltpu.make_async_remote_copy(
            src_ref=query_ref.at[:, tile_cols(peer(step), tile)],
            dst_ref=qbuf.at[tile, pl.ds(mine, tokens), :],
            send_sem=q_send.at[tile, step - 1], recv_sem=q_recv.at[tile, step - 1],
            device_id={"seq": peer(step)}, device_id_type=MESH,
        )

    def g_copy(tile, step):
        return pltpu.make_async_remote_copy(
            src_ref=inc.at[:, tile_cols(peer(step), tile)],
            dst_ref=gbuf.at[tile, pl.ds(mine, tokens), :],
            send_sem=g_send.at[tile, step - 1], recv_sem=g_recv.at[tile, step - 1],
            device_id={"seq": peer(step)}, device_id_type=MESH,
        )

    def d_copy(step):
        return pltpu.make_async_remote_copy(
            src_ref=dsend.at[peer(step)], dst_ref=dgot.at[seq],
            send_sem=d_send.at[step - 1], recv_sem=d_recv.at[step - 1],
            device_id={"seq": peer(step)}, device_id_type=MESH,
        )

    def h_copy(tile):
        pair = pl.ds(tile * PER_TILE, PER_TILE)
        return pltpu.make_async_remote_copy(
            src_ref=cache_ref.at[pair, pl.ds(window, span), :], dst_ref=halo.at[pair],
            send_sem=h_send.at[tile], recv_sem=h_recv.at[tile],
            device_id={"tp": mate}, device_id_type=MESH,
        )

    def b_copy(head):
        return pltpu.make_async_remote_copy(
            src_ref=back_out.at[head], dst_ref=back_in.at[head],
            send_sem=b_send.at[head], recv_sem=b_recv.at[head],
            device_id={"tp": mate}, device_id_type=MESH,
        )

    out_local = pltpu.make_async_copy(out_ref, outs, local_sem.at[0])
    kv_local = pltpu.make_async_copy(cache_ref, kv, local_sem.at[1])
    q_local = [
        pltpu.make_async_copy(
            query_ref.at[:, tile_cols(seq, tile)], qbuf.at[tile, pl.ds(mine, tokens), :], local_sem.at[2 + tile]
        )
        for tile in range(tiles)
    ]
    neigh_local = pltpu.make_async_copy(neigh_hbm, neigh_ref, local_sem.at[2 + tiles])
    norm_local = pltpu.make_async_copy(norm_hbm, norm_ref, local_sem.at[3 + tiles])
    neigh_local.start()
    norm_local.start()
    out_local.start()
    kv_local.start()
    for copy in q_local:
        copy.start()

    barrier = pltpu.get_barrier_semaphore()
    pl.semaphore_signal(barrier, inc=1, device_id={"pipe": above}, device_id_type=MESH)
    pl.semaphore_signal(barrier, inc=1, device_id={"tp": mate}, device_id_type=MESH)
    for step in range(1, n_seq):
        pl.semaphore_signal(barrier, inc=1, device_id={"seq": peer(step)}, device_id_type=MESH)
    pl.semaphore_wait(barrier, n_seq + 1)

    def send_up(tile):
        for dest in range(n_seq):
            up_copy(tile, dest).start()

    def send_q(tile):
        for step in range(1, n_seq):
            q_copy(tile, step).start()

    def send_g(tile):
        for step in range(1, n_seq):
            g_copy(tile, step).start()

    send_q(0)
    send_up(0)
    send_q(1)
    h_copy(0).start()
    send_up(1)

    neigh_local.wait()
    first_row = tp * blocks_here
    halo_key = mate * blocks_here + tp * (blocks_here - REACH)
    bias_own[...] = listed_bias(neigh_ref, first_row, first_row, bias_own.shape[0], blocks_here)
    bias_halo[...] = listed_bias(neigh_ref, first_row, halo_key, bias_halo.shape[0], blocks_here)

    inv_root = HD ** (-0.5)
    key_lane = lax.broadcasted_iota(jnp.int32, (1, 2 * HD), 1) < HD
    lane_scale = jnp.where(key_lane, inv_root, 1.0)
    lane_scale_half = lane_scale.astype(jnp.bfloat16)

    def prepare(head, carry):
        scaled = kv[head] * lane_scale_half
        kv[head] = scaled
        key_turned[head] = jnp.transpose(scaled)[:HD]
        return carry

    for tile in range(tiles):
        for dest in range(n_seq):
            up_copy(tile, dest).wait_recv()
        if tile + 2 < tiles:
            send_up(tile + 2)
        if tile < 2:
            send_g(tile)
        if tile == 1:
            send_q(tile + 1)
        if tile + 1 < tiles:
            h_copy(tile + 1).start()
        if tile == 1:
            turned[...] = jnp.zeros_like(turned)
            kv_local.wait()
            lax.fori_loop(0, heads, prepare, 0)

    out_local.wait()
    picks = (
        lax.broadcasted_iota(jnp.int32, (heads, share), 1) // HD
        == lax.broadcasted_iota(jnp.int32, (heads, share), 0)
    ).astype(jnp.bfloat16)
    dsend[...] = jnp.zeros_like(dsend)
    for dest in range(n_seq):
        cols = pl.ds(dest * share, share)
        terms = inc[:, cols].astype(jnp.float32) * outs[:, cols].astype(jnp.float32)
        high = terms.astype(jnp.bfloat16)
        low = (terms - high.astype(jnp.float32)).astype(jnp.bfloat16)
        dsend[dest, :, :tokens] = dot_f32(picks, high, NT) + dot_f32(picks, low, NT)
    for step in range(1, n_seq):
        d_copy(step).start()
    dgot[seq] = dsend[seq]
    for tile in range(tiles):
        gbuf[tile, pl.ds(mine, tokens), :] = inc[:, tile_cols(seq, tile)]
    for copy in q_local:
        copy.wait()
    for step in range(1, n_seq):
        d_copy(step).wait_recv()
    delta = None
    for source in range(n_seq):
        part = jnp.concatenate([dgot[source], jnp.zeros((heads, rows - LANES), jnp.float32)], axis=1)
        if source:
            part = pltpu.roll(part, source * tokens, 1)
        delta = part if delta is None else delta + part
    norm_local.wait()
    norm = norm_ref[...]
    for head in range(heads):
        rows_aux[head, 0:1, :] = norm[head : head + 1]
        rows_aux[head, 1:2, :] = delta[head : head + 1]

    def block_terms(scaled, keys_turned, both_rows, both_turned, bias, norm_row, delta_row):
        count, width_here = scaled.shape[0] // BLK, delta_row.shape[1]
        products = dot_f32(scaled, both_turned)
        scores = products[:, :width_here].reshape(count, BLK, width_here)
        shift = bias[:count] - norm_row
        weights = jnp.exp(scores + shift[:, None, :]).reshape(count * BLK, width_here)
        grad_scores = (weights * (products[:, width_here:] - delta_row)).astype(jnp.bfloat16)
        joined = jnp.concatenate([grad_scores, weights.astype(jnp.bfloat16)], axis=1)
        cache_part = dot_f32(joined, both_rows) * lane_scale
        query_part = dot_f32(keys_turned, grad_scores)
        return query_part, cache_part

    def finish(tile):
        for inner in range(PER_TILE):
            head = tile * PER_TILE + inner
            b_copy(head).wait_recv()
            acc_kv[head, pl.ds(window, span), :] += back_in[head].astype(jnp.float32)
            dkv_ref[head] = acc_kv[head].astype(jnp.bfloat16)

    def one_tile(tile, carry):
        for step in range(1, n_seq):
            q_copy(tile, step).wait_recv()
            g_copy(tile, step).wait_recv()

        @pl.when(tile + 2 < tiles)
        def _():
            send_g(tile + 2)

        @pl.when(tile + 3 < tiles)
        def _():
            send_q(tile + 3)

        blank = jnp.zeros((rows, HD), jnp.bfloat16)
        q_turned = jnp.transpose(qbuf[tile])
        g_turned = jnp.transpose(gbuf[tile])
        for inner in range(PER_TILE):
            lanes = slice(inner * HD, (inner + 1) * HD)
            joint[inner, 0] = jnp.concatenate([qbuf[tile, :, lanes], blank], axis=1)
            joint[inner, 1] = jnp.concatenate([blank, gbuf[tile, :, lanes]], axis=1)
            turned[inner, :HD, :rows] = q_turned[lanes]
            turned[inner, HD:, rows:] = g_turned[lanes]
        h_copy(tile).wait_recv()
        for inner in range(PER_TILE):
            head = tile * PER_TILE + inner
            scaled = halo[head] * lane_scale_half
            query_part, cache_part = block_terms(
                scaled,
                jnp.transpose(scaled)[:HD],
                joint[inner, :, pl.ds(window, span), :].reshape(2 * span, LANES),
                jnp.concatenate(
                    [turned[inner, :, pl.ds(window, span)], turned[inner, :, pl.ds(far_window, span)]], axis=1
                ),
                bias_halo[:, pl.ds(window, span)],
                rows_aux[head, 0:1, pl.ds(window, span)],
                rows_aux[head, 1:2, pl.ds(window, span)],
            )
            back_out[head] = cache_part.astype(jnp.bfloat16)
            b_copy(head).start()
            acc[head, :, pl.ds(window, span)] = query_part
            acc[head, :, pl.ds(pl.multiple_of(tp * span, LANES), rows - span)] = jnp.zeros(
                (HD, rows - span), jnp.float32
            )
        for inner in range(PER_TILE):
            head = tile * PER_TILE + inner
            query_part, cache_part = block_terms(
                kv[head],
                key_turned[head],
                joint[inner].reshape(2 * rows, LANES),
                turned[inner],
                bias_own[...],
                rows_aux[head, 0:1, :],
                rows_aux[head, 1:2, :],
            )
            dq_ref[head] = (acc[head] + query_part).astype(jnp.bfloat16)
            acc_kv[head] = cache_part
        @pl.when(tile >= 2)
        def _():
            finish(tile - 2)

        return carry

    lax.fori_loop(0, tiles, one_tile, 0)
    finish(tiles - 2)
    finish(tiles - 1)

    for tile in range(tiles):
        for dest in range(n_seq):
            up_copy(tile, dest).wait_send()
        for step in range(1, n_seq):
            q_copy(tile, step).wait_send()
            g_copy(tile, step).wait_send()
        h_copy(tile).wait_send()
        for inner in range(PER_TILE):
            b_copy(tile * PER_TILE + inner).wait_send()
    for step in range(1, n_seq):
        d_copy(step).wait_send()


def fused_body(upstream, queries, attention_out, keys_values, log_totals, neighbours):
    tokens, width = queries.shape[2:]
    heads, rows = keys_values.shape[2:4]
    tiles = heads // PER_TILE
    n_seq = lax.axis_size("seq")
    span = REACH * BLK
    blocks_pad = 8 * -(-(rows // BLK) // 8)
    bf16, f32 = jnp.bfloat16, jnp.float32
    vmem = pl.BlockSpec(memory_space=pltpu.VMEM)
    pinned = pl.BlockSpec(memory_space=pltpu.HBM)
    dma = pltpu.SemaphoreType.DMA
    query_turned, cache_grad = pl.pallas_call(
        fused_kernel,
        out_shape=(
            jax.ShapeDtypeStruct((heads, HD, rows), bf16),
            jax.ShapeDtypeStruct((heads, rows, 2 * HD), bf16),
        ),
        in_specs=[pinned] * 6,
        out_specs=(vmem, vmem),
        scratch_shapes=[
            pltpu.SMEM((NBR, neighbours.shape[0]), jnp.int32),
            pltpu.VMEM((heads, rows), f32),
            pltpu.VMEM((tokens, width), bf16),
            pltpu.VMEM((tokens, width), bf16),
            pltpu.VMEM((heads, rows, 2 * HD), bf16),
            pltpu.VMEM((heads, span, 2 * HD), bf16),
            pltpu.VMEM((tiles, rows, LANES), bf16),
            pltpu.VMEM((tiles, rows, LANES), bf16),
            pltpu.VMEM((n_seq, heads, LANES), f32),
            pltpu.VMEM((n_seq, heads, LANES), f32),
            pltpu.VMEM((heads, HD, rows), f32),
            pltpu.VMEM((heads, rows, 2 * HD), f32),
            pltpu.VMEM((heads, span, 2 * HD), bf16),
            pltpu.VMEM((heads, span, 2 * HD), bf16),
            pltpu.VMEM((blocks_pad, rows), f32),
            pltpu.VMEM((8, rows), f32),
            pltpu.VMEM((heads, 8, rows), f32),
            pltpu.VMEM((PER_TILE, 2, rows, LANES), bf16),
            pltpu.VMEM((PER_TILE, 2 * HD, 2 * rows), bf16),
            pltpu.VMEM((heads, HD, rows), bf16),
            dma((tiles, n_seq)),
            dma((tiles, n_seq)),
            dma((tiles, n_seq - 1)),
            dma((tiles, n_seq - 1)),
            dma((tiles, n_seq - 1)),
            dma((tiles, n_seq - 1)),
            dma((n_seq - 1,)),
            dma((n_seq - 1,)),
            dma((tiles,)),
            dma((tiles,)),
            dma((heads,)),
            dma((heads,)),
            dma((4 + tiles,)),
        ],
        compiler_params=pltpu.CompilerParams(
            collective_id=0, has_side_effects=True, vmem_limit_bytes=48 * 1024 * 1024
        ),
    )(
        *[
            pltpu.with_memory_space_constraint(operand, pltpu.HBM)
            for operand in (
                jnp.transpose(neighbours),
                log_totals.reshape(heads, rows),
                upstream.reshape(tokens, width),
                queries.reshape(tokens, width),
                attention_out.reshape(tokens, width),
                keys_values.reshape(heads, rows, 2 * HD),
            )
        ]
    )
    query_grad = jnp.transpose(query_turned, (0, 2, 1)).reshape(1, 1, heads, rows, HD)
    return query_grad, cache_grad.reshape(1, 1, heads, rows, 2 * HD)


def body(upstream, queries, attention_out, keys_values, log_totals, neighbours):
    tokens = queries.shape[2]
    heads, rows = keys_values.shape[2:4]
    fits = (
        lax.axis_size("tp") == 2
        and lax.axis_size("pipe") > 1
        and lax.axis_size("seq") > 1
        and heads == 8
        and tokens % 16 == 0
        and tokens <= LANES
        and rows % LANES == 0
        and REACH * BLK < rows <= 512
    )
    chosen = fused_body if fits else general_body
    return chosen(upstream, queries, attention_out, keys_values, log_totals, neighbours)


def solution(mesh):
    placed = (
        P("pipe", "tp", "seq", None),
        P("pipe", "tp", "seq", None),
        P("pipe", "tp", "seq", None),
        P("pipe", "tp", "seq", None, None),
        P("pipe", "tp", "seq", None),
        P(),
    )
    return jax.shard_map(
        body,
        mesh=mesh,
        in_specs=placed,
        out_specs=(P("pipe", "tp", "seq", None, None), P("pipe", "tp", "seq", None, None)),
        check_vma=False,
    )
```

```python
import jax
import jax.numpy as jnp
from jax import lax
from jax.experimental import pallas as pl
from jax.experimental.pallas import tpu as pltpu
from jax.sharding import PartitionSpec as P

H = 32
HD = 64
BLK = 64
REACH = 4
NBR = 7


pair_group = 32


def passed_along(value, axis, steps):
    count = lax.axis_size(axis)
    pairs = [(source, (source + steps) % count) for source in range(count)]
    return lax.ppermute(value, axis, pairs)


def padded_2(cells, sides, width):
    for axis, dim in sides:
        count = lax.axis_size(axis)
        ends = count - 1
        head = lax.slice_in_dim(cells, 0, width, axis=dim)
        tail = lax.slice_in_dim(cells, cells.shape[dim] - width, cells.shape[dim], axis=dim)
        cells = jnp.concatenate(
            [
                lax.ppermute(tail, axis, [(i, (i + 1) % count) for i in range(ends)]),
                cells,
                lax.ppermute(head, axis, [((i + 1) % count, i) for i in range(ends)]),
            ],
            axis=dim,
        )
    return cells


def block_layout(values, blocks_here):
    heads_here = values.shape[1]
    turned = jnp.transpose(values, (1, 0, 2))
    return turned.reshape(heads_here, blocks_here, BLK, values.shape[2])


def general_body(upstream, queries, attention_out, keys_values, log_totals, neighbours):
    tokens_here = queries.shape[2]
    inv_root = HD ** (-0.5)
    incoming = passed_along(upstream, "pipe", -1)
    query_tok = queries.reshape(tokens_here, H, HD)
    grad_tok = incoming.reshape(tokens_here, H, HD)
    out_tok = attention_out.reshape(tokens_here, H, HD)
    packed = jnp.concatenate([query_tok, grad_tok, out_tok], axis=2)
    regrouped = lax.all_to_all(packed, "seq", split_axis=1, concat_axis=0, tiled=True)
    query_heads = regrouped[:, :, :HD]
    grad_heads = regrouped[:, :, HD : 2 * HD]
    out_heads = regrouped[:, :, 2 * HD :]
    row_delta = jnp.sum(grad_heads.astype(jnp.float32) * out_heads.astype(jnp.float32), axis=2)
    rows_here = query_heads.shape[0]
    heads_here = query_heads.shape[1]
    blocks_here = rows_here // BLK
    query_blocks = block_layout(query_heads, blocks_here)
    grad_blocks = block_layout(grad_heads, blocks_here)
    delta_blocks = jnp.transpose(row_delta).reshape(heads_here, blocks_here, BLK)
    norm_blocks = log_totals.reshape(heads_here, blocks_here, BLK)
    cache_blocks = keys_values.reshape(heads_here, blocks_here, BLK, 2 * HD)
    padded = padded_2(cache_blocks, (("tp", 1),), REACH)
    first_block = lax.axis_index("tp") * blocks_here
    listed = lax.dynamic_slice_in_dim(neighbours, first_block, blocks_here, 0)
    present = (listed >= 0).reshape(-1)
    slot_count = blocks_here * NBR
    group_total = (slot_count + pair_group - 1) // pair_group
    capacity = group_total * pair_group
    running = jnp.cumsum(present.astype(jnp.int32)) - 1
    pair_count = jnp.sum(present.astype(jnp.int32))
    target = jnp.where(present, running, capacity)
    query_source = jnp.repeat(jnp.arange(blocks_here, dtype=jnp.int32), NBR)
    key_source = (listed - first_block + REACH).reshape(-1)
    pair_query = jnp.zeros((capacity,), jnp.int32).at[target].set(query_source, mode="drop")
    pair_key = jnp.zeros((capacity,), jnp.int32).at[target].set(key_source, mode="drop")

    def one_group(group_step, totals):
        query_acc, cache_acc = totals
        first_pair = group_step * pair_group
        query_pick = lax.dynamic_slice_in_dim(pair_query, first_pair, pair_group)
        key_pick = lax.dynamic_slice_in_dim(pair_key, first_pair, pair_group)
        live_mask = (first_pair + jnp.arange(pair_group) < pair_count).astype(jnp.float32)
        query_rows = query_blocks[:, query_pick]
        grad_rows = grad_blocks[:, query_pick]
        norm_rows = norm_blocks[:, query_pick]
        delta_rows = delta_blocks[:, query_pick]
        cache_rows = padded[:, key_pick]
        key_rows = cache_rows[..., :HD]
        value_rows = cache_rows[..., HD:]
        scores = (
            jnp.einsum("hgqd,hgkd->hgqk", query_rows, key_rows, preferred_element_type=jnp.float32)
            * inv_root
        )
        weights = jnp.exp(scores - norm_rows[..., None]) * live_mask[None, :, None, None]
        weights_half = weights.astype(jnp.bfloat16)
        grad_weights = jnp.einsum(
            "hgqd,hgkd->hgqk", grad_rows, value_rows, preferred_element_type=jnp.float32
        )
        grad_scores = (weights * (grad_weights - delta_rows[..., None])).astype(jnp.bfloat16)
        query_part = (
            jnp.einsum("hgqk,hgkd->hgqd", grad_scores, key_rows, preferred_element_type=jnp.float32)
            * inv_root
        )
        key_part = (
            jnp.einsum(
                "hgqk,hgqd->hgkd", grad_scores, query_rows, preferred_element_type=jnp.float32
            )
            * inv_root
        )
        value_part = jnp.einsum(
            "hgqk,hgqd->hgkd", weights_half, grad_rows, preferred_element_type=jnp.float32
        )
        query_acc = query_acc.at[:, query_pick].add(query_part)
        cache_acc = cache_acc.at[:, key_pick].add(jnp.concatenate([key_part, value_part], axis=-1))
        return (query_acc, cache_acc)

    group_live = (pair_count + pair_group - 1) // pair_group
    query_start = jnp.zeros((heads_here, blocks_here, BLK, HD), jnp.float32)
    cache_start = jnp.zeros((heads_here, blocks_here + 2 * REACH, BLK, 2 * HD), jnp.float32)
    query_acc, cache_acc = lax.fori_loop(0, group_live, one_group, (query_start, cache_start))
    rim_terms = jnp.concatenate([cache_acc[:, :REACH], cache_acc[:, REACH + blocks_here :]], axis=1)
    arrived = padded_2(rim_terms.astype(jnp.bfloat16), (("tp", 1),), REACH).astype(rim_terms.dtype)
    own_part = cache_acc[:, REACH : REACH + blocks_here]
    own_part = own_part.at[:, :REACH].add(arrived[:, :REACH])
    own_part = own_part.at[:, blocks_here - REACH :].add(arrived[:, 3 * REACH :])
    query_grad = query_acc.reshape(1, 1, heads_here, rows_here, HD).astype(jnp.bfloat16)
    cache_grad = own_part.reshape(1, 1, heads_here, rows_here, 2 * HD).astype(jnp.bfloat16)
    return (query_grad, cache_grad)


MESH = pl.DeviceIdType.MESH
LANES = 128
PER_TILE = LANES // HD
ABSENT = -1e30
NT = (((1,), (1,)), ((), ()))


def dot_f32(left, right, dims=(((1,), (0,)), ((), ()))):
    return lax.dot_general(left, right, dims, preferred_element_type=jnp.float32)


def listed_bias(neigh_ref, first_row, first_key, key_rows, blocks_here):
    lane = lax.broadcasted_iota(jnp.int32, (key_rows, LANES), 1)
    key = lax.broadcasted_iota(jnp.int32, (key_rows, LANES), 0) + first_key
    tiles = []
    for pair in range(blocks_here // 2):
        found = None
        for slot in range(NBR):
            here = jnp.where(
                lane < BLK,
                neigh_ref[slot, first_row + 2 * pair],
                neigh_ref[slot, first_row + 2 * pair + 1],
            )
            hit = (key == here).astype(jnp.float32)
            found = hit if found is None else jnp.maximum(found, hit)
        tiles.append((found - 1.0) * -ABSENT)
    return jnp.concatenate(tiles, axis=1)


def fused_kernel(
    neigh_hbm, norm_hbm, up_ref, query_ref, out_ref, cache_ref, dq_ref, dkv_ref,
    neigh_ref, norm_ref, inc, outs, kv, halo, qbuf, gbuf, dsend, dgot, acc, acc_kv, back_out, back_in, bias_own, bias_halo, rows_aux, joint, turned, key_turned,
    up_send, up_recv, q_send, q_recv, g_send, g_recv, d_send, d_recv, h_send, h_recv, b_send, b_recv, local_sem,
):
    n_pipe, n_seq = lax.axis_size("pipe"), lax.axis_size("seq")
    pipe, seq, tp = lax.axis_index("pipe"), lax.axis_index("seq"), lax.axis_index("tp")
    tokens, width = inc.shape
    heads, rows, _ = kv.shape
    tiles = heads // PER_TILE
    span = REACH * BLK
    blocks_here = rows // BLK
    share = heads * HD
    below, above = lax.rem(pipe + n_pipe - 1, n_pipe), lax.rem(pipe + 1, n_pipe)
    mate = 1 - tp
    window = pl.multiple_of(mate * (rows - span), LANES)
    far_window = pl.multiple_of(rows + mate * (rows - span), LANES)
    mine = pl.multiple_of(seq * tokens, 16)

    def peer(step):
        if n_seq == 4:
            return (lax.rem(seq + 2, 4), 3 - seq, seq + 1 - 2 * lax.rem(seq, 2))[step - 1]
        return lax.rem(seq + step, n_seq)

    def tile_cols(dest, tile):
        return pl.ds(pl.multiple_of(dest * share + tile * LANES, LANES), LANES)

    def up_copy(tile, dest):
        cols = pl.ds(dest * share + tile * LANES, LANES)
        return pltpu.make_async_remote_copy(
            src_ref=up_ref.at[:, cols], dst_ref=inc.at[:, cols],
            send_sem=up_send.at[tile, dest], recv_sem=up_recv.at[tile, dest],
            device_id={"pipe": below}, device_id_type=MESH,
        )

    def q_copy(tile, step):
        return pltpu.make_async_remote_copy(
            src_ref=query_ref.at[:, tile_cols(peer(step), tile)],
            dst_ref=qbuf.at[tile, pl.ds(mine, tokens), :],
            send_sem=q_send.at[tile, step - 1], recv_sem=q_recv.at[tile, step - 1],
            device_id={"seq": peer(step)}, device_id_type=MESH,
        )

    def g_copy(tile, step):
        return pltpu.make_async_remote_copy(
            src_ref=inc.at[:, tile_cols(peer(step), tile)],
            dst_ref=gbuf.at[tile, pl.ds(mine, tokens), :],
            send_sem=g_send.at[tile, step - 1], recv_sem=g_recv.at[tile, step - 1],
            device_id={"seq": peer(step)}, device_id_type=MESH,
        )

    def d_copy(step):
        return pltpu.make_async_remote_copy(
            src_ref=dsend.at[peer(step)], dst_ref=dgot.at[seq],
            send_sem=d_send.at[step - 1], recv_sem=d_recv.at[step - 1],
            device_id={"seq": peer(step)}, device_id_type=MESH,
        )

    def h_copy(tile):
        pair = pl.ds(tile * PER_TILE, PER_TILE)
        return pltpu.make_async_remote_copy(
            src_ref=cache_ref.at[pair, pl.ds(window, span), :], dst_ref=halo.at[pair],
            send_sem=h_send.at[tile], recv_sem=h_recv.at[tile],
            device_id={"tp": mate}, device_id_type=MESH,
        )

    def b_copy(head):
        return pltpu.make_async_remote_copy(
            src_ref=back_out.at[head], dst_ref=back_in.at[head],
            send_sem=b_send.at[head], recv_sem=b_recv.at[head],
            device_id={"tp": mate}, device_id_type=MESH,
        )

    out_local = pltpu.make_async_copy(out_ref, outs, local_sem.at[0])
    kv_local = pltpu.make_async_copy(cache_ref, kv, local_sem.at[1])
    q_local = [
        pltpu.make_async_copy(
            query_ref.at[:, tile_cols(seq, tile)], qbuf.at[tile, pl.ds(mine, tokens), :], local_sem.at[2 + tile]
        )
        for tile in range(tiles)
    ]
    neigh_local = pltpu.make_async_copy(neigh_hbm, neigh_ref, local_sem.at[2 + tiles])
    norm_local = pltpu.make_async_copy(norm_hbm, norm_ref, local_sem.at[3 + tiles])
    neigh_local.start()
    norm_local.start()
    out_local.start()
    kv_local.start()
    for copy in q_local:
        copy.start()

    barrier = pltpu.get_barrier_semaphore()
    pl.semaphore_signal(barrier, inc=1, device_id={"pipe": above}, device_id_type=MESH)
    pl.semaphore_signal(barrier, inc=1, device_id={"tp": mate}, device_id_type=MESH)
    for step in range(1, n_seq):
        pl.semaphore_signal(barrier, inc=1, device_id={"seq": peer(step)}, device_id_type=MESH)
    pl.semaphore_wait(barrier, n_seq + 1)

    def send_up(tile):
        for dest in range(n_seq):
            up_copy(tile, dest).start()

    def send_q(tile):
        for step in range(1, n_seq):
            q_copy(tile, step).start()

    def send_g(tile):
        for step in range(1, n_seq):
            g_copy(tile, step).start()

    send_q(0)
    send_up(0)
    send_q(1)
    h_copy(0).start()
    send_up(1)

    neigh_local.wait()
    first_row = tp * blocks_here
    halo_key = mate * blocks_here + tp * (blocks_here - REACH)
    bias_own[...] = listed_bias(neigh_ref, first_row, first_row, bias_own.shape[0], blocks_here)
    bias_halo[...] = listed_bias(neigh_ref, first_row, halo_key, bias_halo.shape[0], blocks_here)

    inv_root = HD ** (-0.5)
    key_lane = lax.broadcasted_iota(jnp.int32, (1, 2 * HD), 1) < HD
    lane_scale = jnp.where(key_lane, inv_root, 1.0)
    lane_scale_half = lane_scale.astype(jnp.bfloat16)

    def prepare(head, carry):
        scaled = kv[head] * lane_scale_half
        kv[head] = scaled
        key_turned[head] = jnp.transpose(scaled)[:HD]
        return carry

    for tile in range(tiles):
        for dest in range(n_seq):
            up_copy(tile, dest).wait_recv()
        if tile + 2 < tiles:
            send_up(tile + 2)
        if tile < 3:
            send_g(tile)
        if tile == 1:
            send_q(tile + 1)
        if tile + 1 < tiles:
            h_copy(tile + 1).start()
        if tile == 1:
            turned[...] = jnp.zeros_like(turned)
            kv_local.wait()
            lax.fori_loop(0, heads, prepare, 0)

    out_local.wait()
    picks = (
        lax.broadcasted_iota(jnp.int32, (heads, share), 1) // HD
        == lax.broadcasted_iota(jnp.int32, (heads, share), 0)
    ).astype(jnp.bfloat16)
    dsend[...] = jnp.zeros_like(dsend)
    for dest in range(n_seq):
        cols = pl.ds(dest * share, share)
        terms = inc[:, cols].astype(jnp.float32) * outs[:, cols].astype(jnp.float32)
        high = terms.astype(jnp.bfloat16)
        low = (terms - high.astype(jnp.float32)).astype(jnp.bfloat16)
        dsend[dest, :, :tokens] = dot_f32(picks, high, NT) + dot_f32(picks, low, NT)
    for step in range(1, n_seq):
        d_copy(step).start()
    dgot[seq] = dsend[seq]
    for tile in range(tiles):
        gbuf[tile, pl.ds(mine, tokens), :] = inc[:, tile_cols(seq, tile)]
    for copy in q_local:
        copy.wait()
    for step in range(1, n_seq):
        d_copy(step).wait_recv()
    delta = None
    for source in range(n_seq):
        part = jnp.concatenate([dgot[source], jnp.zeros((heads, rows - LANES), jnp.float32)], axis=1)
        if source:
            part = pltpu.roll(part, source * tokens, 1)
        delta = part if delta is None else delta + part
    norm_local.wait()
    norm = norm_ref[...]
    for head in range(heads):
        rows_aux[head, 0:1, :] = norm[head : head + 1]
        rows_aux[head, 1:2, :] = delta[head : head + 1]

    def block_terms(scaled, keys_turned, both_rows, both_turned, bias, norm_row, delta_row):
        count, width_here = scaled.shape[0] // BLK, delta_row.shape[1]
        products = dot_f32(scaled, both_turned)
        scores = products[:, :width_here].reshape(count, BLK, width_here)
        shift = bias[:count] - norm_row
        weights = jnp.exp(scores + shift[:, None, :]).reshape(count * BLK, width_here)
        grad_scores = (weights * (products[:, width_here:] - delta_row)).astype(jnp.bfloat16)
        joined = jnp.concatenate([grad_scores, weights.astype(jnp.bfloat16)], axis=1)
        cache_part = dot_f32(joined, both_rows) * lane_scale
        query_part = dot_f32(keys_turned, grad_scores)
        return query_part, cache_part

    def finish(tile):
        for inner in range(PER_TILE):
            head = tile * PER_TILE + inner
            b_copy(head).wait_recv()
            acc_kv[head, pl.ds(window, span), :] += back_in[head].astype(jnp.float32)
            dkv_ref[head] = acc_kv[head].astype(jnp.bfloat16)

    def one_tile(tile, carry):
        for step in range(1, n_seq):
            q_copy(tile, step).wait_recv()
            g_copy(tile, step).wait_recv()

        @pl.when(tile + 3 < tiles)
        def _():
            send_q(tile + 3)
            send_g(tile + 3)

        blank = jnp.zeros((rows, HD), jnp.bfloat16)
        q_turned = jnp.transpose(qbuf[tile])
        g_turned = jnp.transpose(gbuf[tile])
        for inner in range(PER_TILE):
            lanes = slice(inner * HD, (inner + 1) * HD)
            joint[inner, 0] = jnp.concatenate([qbuf[tile, :, lanes], blank], axis=1)
            joint[inner, 1] = jnp.concatenate([blank, gbuf[tile, :, lanes]], axis=1)
            turned[inner, :HD, :rows] = q_turned[lanes]
            turned[inner, HD:, rows:] = g_turned[lanes]
        h_copy(tile).wait_recv()
        for inner in range(PER_TILE):
            head = tile * PER_TILE + inner
            scaled = halo[head] * lane_scale_half
            query_part, cache_part = block_terms(
                scaled,
                jnp.transpose(scaled)[:HD],
                joint[inner, :, pl.ds(window, span), :].reshape(2 * span, LANES),
                jnp.concatenate(
                    [turned[inner, :, pl.ds(window, span)], turned[inner, :, pl.ds(far_window, span)]], axis=1
                ),
                bias_halo[:, pl.ds(window, span)],
                rows_aux[head, 0:1, pl.ds(window, span)],
                rows_aux[head, 1:2, pl.ds(window, span)],
            )
            back_out[head] = cache_part.astype(jnp.bfloat16)
            b_copy(head).start()
            acc[head, :, pl.ds(window, span)] = query_part
            acc[head, :, pl.ds(pl.multiple_of(tp * span, LANES), rows - span)] = jnp.zeros(
                (HD, rows - span), jnp.float32
            )
        for inner in range(PER_TILE):
            head = tile * PER_TILE + inner
            query_part, cache_part = block_terms(
                kv[head],
                key_turned[head],
                joint[inner].reshape(2 * rows, LANES),
                turned[inner],
                bias_own[...],
                rows_aux[head, 0:1, :],
                rows_aux[head, 1:2, :],
            )
            dq_ref[head] = (acc[head] + query_part).astype(jnp.bfloat16)
            acc_kv[head] = cache_part
        @pl.when(tile >= 2)
        def _():
            finish(tile - 2)

        return carry

    lax.fori_loop(0, tiles, one_tile, 0)
    finish(tiles - 2)
    finish(tiles - 1)

    for tile in range(tiles):
        for dest in range(n_seq):
            up_copy(tile, dest).wait_send()
        for step in range(1, n_seq):
            q_copy(tile, step).wait_send()
            g_copy(tile, step).wait_send()
        h_copy(tile).wait_send()
        for inner in range(PER_TILE):
            b_copy(tile * PER_TILE + inner).wait_send()
    for step in range(1, n_seq):
        d_copy(step).wait_send()


def fused_body(upstream, queries, attention_out, keys_values, log_totals, neighbours):
    tokens, width = queries.shape[2:]
    heads, rows = keys_values.shape[2:4]
    tiles = heads // PER_TILE
    n_seq = lax.axis_size("seq")
    span = REACH * BLK
    blocks_pad = 8 * -(-(rows // BLK) // 8)
    bf16, f32 = jnp.bfloat16, jnp.float32
    vmem = pl.BlockSpec(memory_space=pltpu.VMEM)
    pinned = pl.BlockSpec(memory_space=pltpu.HBM)
    dma = pltpu.SemaphoreType.DMA
    query_turned, cache_grad = pl.pallas_call(
        fused_kernel,
        out_shape=(
            jax.ShapeDtypeStruct((heads, HD, rows), bf16),
            jax.ShapeDtypeStruct((heads, rows, 2 * HD), bf16),
        ),
        in_specs=[pinned] * 6,
        out_specs=(vmem, vmem),
        scratch_shapes=[
            pltpu.SMEM((NBR, neighbours.shape[0]), jnp.int32),
            pltpu.VMEM((heads, rows), f32),
            pltpu.VMEM((tokens, width), bf16),
            pltpu.VMEM((tokens, width), bf16),
            pltpu.VMEM((heads, rows, 2 * HD), bf16),
            pltpu.VMEM((heads, span, 2 * HD), bf16),
            pltpu.VMEM((tiles, rows, LANES), bf16),
            pltpu.VMEM((tiles, rows, LANES), bf16),
            pltpu.VMEM((n_seq, heads, LANES), f32),
            pltpu.VMEM((n_seq, heads, LANES), f32),
            pltpu.VMEM((heads, HD, rows), f32),
            pltpu.VMEM((heads, rows, 2 * HD), f32),
            pltpu.VMEM((heads, span, 2 * HD), bf16),
            pltpu.VMEM((heads, span, 2 * HD), bf16),
            pltpu.VMEM((blocks_pad, rows), f32),
            pltpu.VMEM((8, rows), f32),
            pltpu.VMEM((heads, 8, rows), f32),
            pltpu.VMEM((PER_TILE, 2, rows, LANES), bf16),
            pltpu.VMEM((PER_TILE, 2 * HD, 2 * rows), bf16),
            pltpu.VMEM((heads, HD, rows), bf16),
            dma((tiles, n_seq)),
            dma((tiles, n_seq)),
            dma((tiles, n_seq - 1)),
            dma((tiles, n_seq - 1)),
            dma((tiles, n_seq - 1)),
            dma((tiles, n_seq - 1)),
            dma((n_seq - 1,)),
            dma((n_seq - 1,)),
            dma((tiles,)),
            dma((tiles,)),
            dma((heads,)),
            dma((heads,)),
            dma((4 + tiles,)),
        ],
        compiler_params=pltpu.CompilerParams(
            collective_id=0, has_side_effects=True, vmem_limit_bytes=48 * 1024 * 1024
        ),
    )(
        *[
            pltpu.with_memory_space_constraint(operand, pltpu.HBM)
            for operand in (
                jnp.transpose(neighbours),
                log_totals.reshape(heads, rows),
                upstream.reshape(tokens, width),
                queries.reshape(tokens, width),
                attention_out.reshape(tokens, width),
                keys_values.reshape(heads, rows, 2 * HD),
            )
        ]
    )
    query_grad = jnp.transpose(query_turned, (0, 2, 1)).reshape(1, 1, heads, rows, HD)
    return query_grad, cache_grad.reshape(1, 1, heads, rows, 2 * HD)


def body(upstream, queries, attention_out, keys_values, log_totals, neighbours):
    tokens = queries.shape[2]
    heads, rows = keys_values.shape[2:4]
    fits = (
        lax.axis_size("tp") == 2
        and lax.axis_size("pipe") > 1
        and lax.axis_size("seq") > 1
        and heads == 8
        and tokens % 16 == 0
        and tokens <= LANES
        and rows % LANES == 0
        and REACH * BLK < rows <= 512
    )
    chosen = fused_body if fits else general_body
    return chosen(upstream, queries, attention_out, keys_values, log_totals, neighbours)


def solution(mesh):
    placed = (
        P("pipe", "tp", "seq", None),
        P("pipe", "tp", "seq", None),
        P("pipe", "tp", "seq", None),
        P("pipe", "tp", "seq", None, None),
        P("pipe", "tp", "seq", None),
        P(),
    )
    return jax.shard_map(
        body,
        mesh=mesh,
        in_specs=placed,
        out_specs=(P("pipe", "tp", "seq", None, None), P("pipe", "tp", "seq", None, None)),
        check_vma=False,
    )
```
